32 devices in a mesh: grp: 2 (over y), row: 8 (over z, x), col: 2 (over core).
Axes of the slice: x: 2, y: 2, z: 4, core: 2. Of those that a mesh axis runs over, the one named last changes fastest.
Arguments:
- tokens: bfloat16 [128, 256, 180], P(('grp', 'row'), 'col'), parts along dimension 0, may hold values from -6 to 6
- grad_out: bfloat16 [128, 256, 180], P(('grp', 'row'), 'col'), parts along dimension 0, may hold values from -8 to 8
- regions: int32 [128, 256], P(('grp', 'row'), 'col'), parts along dimension 0, may hold values from 0 to 15, as said below
- ln_gain: float32 [180], replicated, may hold values from 0.1 to 1.9
- ln_offset: float32 [180], replicated, may hold values from -1.5 to 1.5
- qkv_weight: bfloat16 [180, 540], replicated, may hold values from -0.4375 to 0.4375
- qkv_bias: float32 [540], replicated, may hold values from -1.5 to 1.5
- proj_weight: bfloat16 [180, 180], replicated, may hold values from -0.4375 to 0.4375
- bias_table: float32 [225, 6], replicated, may hold values from -4 to 320
Outputs:
- d_tokens: bfloat16 [128, 256, 180], P(('grp', 'row'), 'col'), parts along dimension 0
- d_qkv_weight: float32 [360, 540], P('grp'), parts along dimension 0
- d_qkv_bias: float32 [1080], P('grp'), parts along dimension 0
- d_proj_weight: float32 [360, 180], P('grp'), parts along dimension 0
- d_bias_table: float32 [450, 6], P('grp'), parts along dimension 0
- d_ln_gain: float32 [360], P('grp'), parts along dimension 0
- d_ln_offset: float32 [360], P('grp'), parts along dimension 0
The draws below stay inside these ranges and needn't reach their ends.
There are 2 independent parts, one for each index of `grp`. The reference program is written for one: setup_inputs(seed, part) draws one part's arguments, and reference() takes and returns one part's arrays. A program takes and returns all parts, laid end to end along the dimension named above; an argument that names none is the same for every part. Nothing has to cross between parts.
Inputs may be any that keep to these rules, and one draw needn't show every extreme that they name: `regions`: A token attends only to tokens of its window with the same id. The map is a grid: the id is 4 a + b, where a, from 0 to 3, depends only on the token's row and b, from 0 to 3, only on its column.
All inputs are finite; a program needn't handle non-finite values.
Results may differ from the reference program's by a relative error of at most 0.0085.
Values may be sent and summed in bfloat16 or wider, within the bound.
No kernel may reach another device: no remote copies, remote signals or barrier semaphores. Data moves between devices by JAX's collectives and lax.ppermute only.
A program may use at most 64 MiB of HBM per device.

```python
import jax
import jax.numpy as jnp
from jax import lax

C = 180
HEADS = 6
WIN = 8
SHIFT = 4
TABLE = 225
H = 64
W = 256


def draw_grad_out(key, part):
    key_one = jax.random.fold_in(key, 0)
    noise = jax.random.normal(key_one, (H, W, C), jnp.float32)
    values = noise
    return jnp.clip(values, -8.0, 8.0).astype(jnp.bfloat16)


def draw_regions(key, part):
    row_key, col_key = jax.random.split(key)
    row_flag = (jax.random.randint(row_key, (H,), 0, 16) == 0).astype(jnp.int32)
    row_flag = row_flag.at[0].set(0).at[1:4].set(1)
    col_flag = (jax.random.randint(col_key, (W,), 0, 16) == 0).astype(jnp.int32)
    col_flag = col_flag.at[0].set(0).at[1:4].set(1)
    row_band = jnp.cumsum(row_flag) % 4
    col_band = jnp.cumsum(col_flag) % 4
    return (row_band[:, None] * 4 + col_band[None, :]).astype(jnp.int32)


def draw_bias_table(key, part):
    values = jnp.clip(jax.random.normal(key, (TABLE, HEADS), jnp.float32), -4.0, 4.0)
    return values


def level_of(rng, dims, shards, smallest, top_value):
    def one(dim, shards_of):
        steps = jax.random.uniform(jax.random.fold_in(jax.random.fold_in(rng, 6), dim), (shards_of,), jnp.float32, smallest / len(shards), top_value / len(shards))
        return jnp.repeat(jnp.exp(steps), dims[dim] // shards_of).reshape((-1,) + (1,) * (len(dims) - dim - 1))

    factor_of = one(*shards[0])
    for cut in shards[1:]:
        factor_of = factor_of * one(*cut)
    return factor_of


def normal_values(own_key, extent, scale, reach, shards=(), kind=jnp.bfloat16):
    gain = level_of(own_key, extent, shards, -0.22, 0.18) if shards else 1.0
    entries = jax.random.normal(own_key, extent, jnp.float32) * scale * gain
    return jnp.minimum(jnp.maximum(entries, -reach), reach).astype(kind)


def setup_inputs(seed: int = 0, part: int = 0) -> dict:
    arg_keys = jax.random.split(jax.random.key(seed), 10)
    own_keys = jax.random.split(jax.random.fold_in(arg_keys[9], part), 10)
    return {
        "tokens": normal_values(own_keys[0], (H, W, C), 1.0, 6.0, ((0, 8), (1, 2))),
        "grad_out": draw_grad_out(jax.random.fold_in(jax.random.fold_in(arg_keys[9], part), 71), part),
        "regions": draw_regions(jax.random.fold_in(jax.random.fold_in(arg_keys[9], part), 71), part),
        "ln_gain": jnp.clip(1.0 + 0.18 * jax.random.normal(arg_keys[3], (C,), jnp.float32), 0.1, 1.9),
        "ln_offset": normal_values(arg_keys[4], (C,), 0.3, 1.5, (), jnp.float32),
        "qkv_weight": normal_values(arg_keys[5], (C, 3 * C), C ** -0.5, 0.4375),
        "qkv_bias": normal_values(arg_keys[6], (3 * C,), 0.3, 1.5, (), jnp.float32),
        "proj_weight": normal_values(arg_keys[7], (C, C), C ** -0.5, 0.4375),
        "bias_table": draw_bias_table(jax.random.fold_in(arg_keys[9], 71), part),
    }


masked_score = -10000.0

def multiply(form, left, right):
    return jnp.einsum(form, left.astype(jnp.float32), right.astype(jnp.float32))

def relative_onehot(table_rows):
    span_size = WIN * WIN
    position = jnp.arange(span_size, dtype=jnp.int32)
    row_pos = position // WIN
    col_pos = position % WIN
    entry_index = (row_pos[:, None] - row_pos[None, :] + WIN - 1) * (2 * WIN - 1) + col_pos[:, None] - col_pos[None, :] + WIN - 1
    return (entry_index.reshape(-1)[:, None] == jnp.arange(table_rows, dtype=jnp.int32)[None, :]).astype(jnp.float32)

def normalize(values, gain_vec, offset_vec):
    as_float = values.astype(jnp.float32)
    center = lax.optimization_barrier(jnp.mean(as_float, -1, keepdims=True))
    variance = lax.optimization_barrier(jnp.mean(jnp.square(as_float - center), -1, keepdims=True))
    inv_std = lax.rsqrt(variance + 1e-05)
    unit_tokens = (as_float - center) * inv_std
    normed = (unit_tokens * gain_vec + offset_vec).astype(jnp.bfloat16)
    return (normed, unit_tokens, inv_std)

def project(normed, weights, offsets):
    channels = normed.shape[-1]
    summed = multiply('rcd,df->rcf', normed, weights) + offsets
    factor = jnp.where(jnp.arange(3 * channels) < channels, (channels // HEADS) ** (-0.5), 1.0)
    return (summed * factor).astype(jnp.bfloat16)

def window_band(qkv, grad_band, label_band, rel_bias, proj_weight):
    channels = grad_band.shape[-1]
    head_count = rel_bias.shape[0]
    head_size = channels // head_count
    tile_cols = grad_band.shape[1]
    win_count = tile_cols // WIN
    span_size = WIN * WIN

    def windows(array):
        array = array.reshape((WIN, win_count, WIN) + array.shape[2:])
        array = jnp.moveaxis(array, 1, 0)
        return array.reshape((win_count, span_size) + array.shape[3:])

    def unwindow(array):
        array = array.reshape((win_count, WIN, WIN) + array.shape[2:])
        array = jnp.moveaxis(array, 0, 1)
        return array.reshape((WIN, tile_cols) + array.shape[3:])
    parted = windows(qkv).reshape(win_count, span_size, 3, head_count, head_size)
    query_part = parted[:, :, 0]
    key_part = parted[:, :, 1]
    value_part = parted[:, :, 2]
    grad_win = windows(grad_band)
    label_win = windows(label_band)
    matched = label_win[:, :, None] == label_win[:, None, :]
    scores = multiply('nihd,njhd->nhij', query_part, key_part) + rel_bias[None]
    scores = jnp.where(matched[:, None], scores, masked_score)
    probability = jax.nn.softmax(scores, axis=-1)
    prob_low = probability.astype(jnp.bfloat16)
    attended = multiply('nhij,njhd->nihd', prob_low, value_part).astype(jnp.bfloat16).reshape(win_count * span_size, channels)
    flat_grad = grad_win.reshape(win_count * span_size, channels)
    d_proj = multiply('tc,td->cd', attended, flat_grad)
    d_attended = multiply('td,cd->tc', flat_grad, proj_weight).astype(jnp.bfloat16).reshape(win_count, span_size, head_count, head_size)
    d_prob = multiply('nihd,njhd->nhij', d_attended, value_part)
    d_scores = probability * (d_prob - lax.optimization_barrier(jnp.sum(probability * d_prob, -1, keepdims=True)))
    score_sum = lax.optimization_barrier(jnp.sum(d_scores, 0))
    d_score_low = d_scores.astype(jnp.bfloat16)
    d_query = multiply('nhij,njhd->nihd', d_score_low, key_part) * head_size ** (-0.5)
    d_key = multiply('nhij,nihd->njhd', d_score_low, query_part)
    d_value = multiply('nhij,nihd->njhd', prob_low, d_attended)
    d_qkv = jnp.stack([d_query, d_key, d_value], 2).astype(jnp.bfloat16).reshape(win_count, span_size, 3 * channels)
    return (unwindow(d_qkv), d_proj, score_sum)

def input_backward(d_qkv, normed, unit_tokens, inv_std, gain_vec, qkv_weight):
    d_weight = multiply('rcd,rcf->df', normed, d_qkv)
    d_offsets = lax.optimization_barrier(jnp.sum(d_qkv.astype(jnp.float32), (0, 1)))
    d_normed = multiply('rcf,df->rcd', d_qkv, qkv_weight)
    d_gain = lax.optimization_barrier(jnp.sum(d_normed * unit_tokens, (0, 1)))
    d_offset = lax.optimization_barrier(jnp.sum(d_normed, (0, 1)))
    scaled_grad = d_normed * gain_vec
    d_input = inv_std * (scaled_grad - lax.optimization_barrier(jnp.mean(scaled_grad, -1, keepdims=True)) - unit_tokens * lax.optimization_barrier(jnp.mean(scaled_grad * unit_tokens, -1, keepdims=True)))
    return (d_input, d_weight, d_offsets, d_gain, d_offset)

def reference(tokens, grad_out, regions, ln_gain, ln_offset, qkv_weight, qkv_bias, proj_weight, bias_table):
    shifted = jnp.roll(tokens, (-SHIFT, -SHIFT), (0, 1))
    grad_shifted = jnp.roll(grad_out, (-SHIFT, -SHIFT), (0, 1))
    labels = jnp.roll(regions, (-SHIFT, -SHIFT), (0, 1))
    entry_table = relative_onehot(bias_table.shape[0])
    rel_bias = jnp.dot(entry_table, bias_table, precision=lax.Precision.HIGHEST).reshape(WIN * WIN, WIN * WIN, HEADS).transpose(2, 0, 1)
    band_count = H // WIN

    def to_bands(array):
        return array.reshape((band_count, WIN) + array.shape[1:])

    def band_step(running, pieces):
        normed, unit_tokens, inv_std = normalize(pieces[0], ln_gain, ln_offset)
        qkv = project(normed, qkv_weight, qkv_bias)
        d_qkv, d_proj, score_sum = window_band(qkv, pieces[1], pieces[2], rel_bias, proj_weight)
        d_input, d_weight, d_offsets, d_gain, d_offset = input_backward(d_qkv, normed, unit_tokens, inv_std, ln_gain, qkv_weight)
        added = (d_proj, score_sum, d_weight, d_offsets, d_gain, d_offset)
        return (tuple((before + extra for before, extra in zip(running, added))), d_input)
    initial = (jnp.zeros((C, C), jnp.float32), jnp.zeros((HEADS, WIN * WIN, WIN * WIN), jnp.float32), jnp.zeros((C, 3 * C), jnp.float32), jnp.zeros((3 * C,), jnp.float32), jnp.zeros((C,), jnp.float32), jnp.zeros((C,), jnp.float32))
    totals, d_shifted = lax.scan(band_step, initial, (to_bands(shifted), to_bands(grad_shifted), to_bands(labels)))
    d_shifted = d_shifted.reshape(H, W, C)
    d_tokens = (grad_out.astype(jnp.float32) + jnp.roll(d_shifted, (SHIFT, SHIFT), (0, 1))).astype(jnp.bfloat16)
    out_scale = (H * W) ** (-0.5)
    d_table = jnp.dot(entry_table.T, jnp.transpose(totals[1], (1, 2, 0)).reshape(-1, HEADS), precision=lax.Precision.HIGHEST)
    return (d_tokens, totals[2] * out_scale, totals[3] * out_scale, totals[0] * out_scale, d_table * out_scale, totals[4] * out_scale, totals[5] * out_scale)
```

```python
import functools

import jax
import jax.numpy as jnp
from jax import lax
from jax.experimental import pallas as pl
from jax.experimental.pallas import tpu as pltpu
from jax.sharding import PartitionSpec as P

HEADS = 6
WIN = 8
SHIFT = 4
SPAN = WIN * WIN
MASKED = -10000.0
LANES = 128
SLOT = 32
ROWS = 184
TABLE_ROWS = 16
BUFFER_ROWS = 6 * ROWS + TABLE_ROWS

VMEM_LIMIT = 48 * 1024 * 1024


def nn(left, right):
    return lax.dot_general(left, right, (((1,), (0,)), ((), ())), preferred_element_type=jnp.float32)


def nt(left, right):
    return lax.dot_general(left, right, (((1,), (1,)), ((), ())), preferred_element_type=jnp.float32)


def iota(shape, dim):
    return lax.broadcasted_iota(jnp.int32, shape, dim)


def table_hits(cj, lanes_first):
    shape = (LANES, 2 * LANES) if lanes_first else (2 * LANES, LANES)
    lane = iota(shape, 0 if lanes_first else 1)
    entry = iota(shape, 1 if lanes_first else 0)
    wanted = (lane // WIN) * (2 * WIN - 1) + lane % WIN + (WIN - 1) - cj
    return jnp.where((entry == wanted) & (lane < WIN * (2 * WIN - 1)), 1.0, 0.0).astype(jnp.bfloat16)


def split_three(value):
    high = value.astype(jnp.bfloat16)
    rest = value - high.astype(jnp.float32)
    middle = rest.astype(jnp.bfloat16)
    low = (rest - middle.astype(jnp.float32)).astype(jnp.bfloat16)
    return high, middle, low


def slots(rows):
    size = rows.shape[0] // HEADS
    blank = jnp.zeros((SLOT - size, rows.shape[1]), rows.dtype)
    pieces = []
    for head in range(HEADS):
        pieces += [rows[head * size : (head + 1) * size], blank]
    return jnp.concatenate(pieces, 0)


def unslot(rows, size):
    return jnp.concatenate([rows[head * SLOT : head * SLOT + size] for head in range(HEADS)], 0)


def prepare_kernel(weight_ref, offsets_ref, proj_ref, table_ref, bias_ref, tok_ref, chan_ref, proj_slots_ref, parts_ref):
    channels = weight_ref.shape[0]
    for part in range(3):
        weight = weight_ref[:, part * channels : (part + 1) * channels].astype(jnp.float32)
        parts_ref[part] = weight.astype(jnp.bfloat16)
        high, middle, low = split_three(offsets_ref[:, part * channels : (part + 1) * channels])
        full = jnp.concatenate(
            [
                weight,
                high.astype(jnp.float32),
                middle.astype(jnp.float32),
                low.astype(jnp.float32),
                jnp.zeros((256 - channels - 3, channels), jnp.float32),
            ],
            0,
        )
        turned = slots(full.T)
        chan_ref[part] = turned.astype(jnp.bfloat16)
        if part == 0:
            tok_ref[part, :, 0:channels] = full.astype(jnp.bfloat16)
            tok_ref[part, :, channels:] = jnp.zeros((256, HEADS * SLOT - channels), jnp.bfloat16)
        else:
            tok_ref[part] = turned.T.astype(jnp.bfloat16)
    proj_slots_ref[...] = slots(proj_ref[...].astype(jnp.float32)).astype(jnp.bfloat16)
    pieces = split_three(table_ref[...])
    lane = iota((8, LANES), 1)
    for cj in range(WIN):
        hits = table_hits(cj, False)
        spread = nn(pieces[0], hits) + nn(pieces[1], hits) + nn(pieces[2], hits)
        for rj in range(WIN):
            by = WIN * (WIN - 1 - rj)
            moved = spread if by == 0 else pltpu.roll(spread, LANES - by, 1)
            both = jnp.where(lane < SPAN, moved, pltpu.roll(moved, SPAN, 1))
            for head in range(HEADS):
                bias_ref[head, rj * WIN + cj : rj * WIN + cj + 1, :] = both[head : head + 1, :]


def main_kernel(
    tokens_ref,
    grad_ref,
    region_ref,
    below_ref,
    right_ref,
    corner_ref,
    gain_ref,
    offset_ref,
    bias_ref,
    tok_ref,
    chan_ref,
    proj_ref,
    proj_slots_ref,
    parts_ref,
    own_ref,
    down_ref,
    over_ref,
    sums_ref,
    x_s,
    g_s,
    id_s,
    unit_s,
    inv_s,
    unit_low_s,
    normed_s,
    grad_s,
    q_tok_s,
    k_tok_s,
    v_tok_s,
    da_tok_s,
    q_chan_s,
    k_chan_s,
    v_chan_s,
    da_chan_s,
    attended_s,
    d_qkv_s,
    score_s,
    out_s,
    pack_s,
):
    rows, cols, channels = tokens_ref.shape
    head_size = channels // HEADS
    scale = head_size ** (-0.5)
    count = rows * cols
    wins = cols // WIN
    f32 = jnp.float32
    bf16 = jnp.bfloat16

    x_s[:, :, :, LANES:] = jnp.zeros(x_s.shape[:3] + (LANES,), f32)
    ids = region_ref[...].astype(f32).T
    for r in range(rows):
        if r < rows - SHIFT:
            x_body = tokens_ref[r + SHIFT].astype(f32)
            g_body = grad_ref[r + SHIFT].astype(f32)
            side = right_ref[r].astype(f32)
            id_body = ids[:, r + SHIFT : r + SHIFT + 1]
        else:
            payload = below_ref[r - (rows - SHIFT)].astype(f32)
            x_body = payload[:, 0:channels]
            g_body = payload[:, channels : 2 * channels]
            id_body = payload[:, 2 * channels : 2 * channels + 1]
            side = corner_ref[r - (rows - SHIFT)].astype(f32)
        x_row = jnp.concatenate([x_body[SHIFT:], side[:, 0:channels]], 0)
        g_row = jnp.concatenate([g_body[SHIFT:], side[:, channels : 2 * channels]], 0)
        id_row = jnp.concatenate([id_body[SHIFT:], side[:, 2 * channels : 2 * channels + 1]], 0)
        x_s[:, r, :, 0:channels] = x_row.reshape(wins, WIN, channels)
        g_s[:, r, :, :] = g_row.reshape(wins, WIN, channels)
        id_s[:, r, :, :] = id_row.reshape(wins, WIN, 1)

    x = x_s[...].reshape(count, 2 * LANES)
    lane = iota((1, 2 * LANES), 1)
    inside = lane < channels
    center = jnp.sum(x, -1, keepdims=True) * (1.0 / channels)
    away = jnp.where(inside, x - center, 0.0)
    variance = jnp.sum(away * away, -1, keepdims=True) * (1.0 / channels)
    inv_std = lax.rsqrt(variance + 1e-05)
    unit = away * inv_std
    unit_s[...] = unit
    inv_s[...] = inv_std
    unit_low_s[...] = jnp.where(lane == channels, 1.0, unit).astype(bf16)
    normed_s[...] = jnp.where(
        (lane >= channels) & (lane < channels + 3), 1.0, unit * gain_ref[...] + offset_ref[...]
    ).astype(bf16)
    grad_s[...] = g_s[...].reshape(count, channels).astype(bf16)

    normed = normed_s[...]
    q_tok_s[...] = (nn(normed, tok_ref[0, :, 0:channels]) * scale).astype(bf16)
    k_tok_s[...] = nn(normed, tok_ref[1]).astype(bf16)
    v_tok_s[...] = nn(normed, tok_ref[2]).astype(bf16)
    da_tok_s[...] = nt(grad_s[...], proj_ref[...]).astype(bf16)
    q_chan_s[...] = (nt(chan_ref[0], normed) * scale).astype(bf16)
    k_chan_s[...] = nt(chan_ref[1], normed).astype(bf16)
    v_chan_s[...] = nt(chan_ref[2], normed).astype(bf16)
    da_chan_s[...] = nt(proj_slots_ref[...], grad_s[...]).astype(bf16)

    score_s[...] = jnp.zeros(score_s.shape, f32)
    first = iota((1, LANES), 1) < SPAN
    first_low = jnp.where(first, 1.0, 0.0).astype(bf16)
    second_low = jnp.where(first, 0.0, 1.0).astype(bf16)
    head_of = iota((1, channels), 1) // head_size
    id_lane = iota((1, LANES), 1).astype(f32)

    def pack(square):
        return jnp.where(first, square[0:SPAN], square[SPAN:])

    def spread(packed):
        low = packed.astype(bf16)
        return jnp.concatenate([low * first_low, low * second_low], 0)

    def in_blocks(chan):
        blank = jnp.zeros((SLOT, LANES), bf16)
        lines = []
        for head in range(HEADS):
            line = [blank] * HEADS
            line[head] = chan[head * SLOT : (head + 1) * SLOT]
            lines.append(jnp.concatenate(line, 1))
        return jnp.concatenate(lines, 0)

    def by_head(tok):
        return jnp.concatenate(
            [jnp.where(head_of == head, tok, jnp.zeros_like(tok)) for head in range(HEADS)], 0
        )

    def pair_step(pair, carry):
        at = pl.ds(pl.multiple_of(pair * LANES, LANES), LANES)
        hot = jnp.where(id_s[pl.ds(pair * 2, 2)].reshape(LANES, 1) == id_lane, 1.0, 0.0).astype(bf16)
        match = pack(nt(hot, hot)) > 0.5
        k_chan = k_chan_s[:, at]
        v_chan = v_chan_s[:, at]
        scores = nn(k_tok_s[at, :], in_blocks(q_chan_s[:, at]))
        d_prob = nn(v_tok_s[at, :], in_blocks(da_chan_s[:, at]))
        attended = []
        d_query = []
        probs = []
        d_scores = []
        for head in range(HEADS):
            here = slice(head * LANES, (head + 1) * LANES)
            band = slice(head * SLOT, (head + 1) * SLOT)
            score = jnp.where(match, pack(scores[:, here]) + bias_ref[head], MASKED)
            power = jnp.exp(score - jnp.max(score, 0, keepdims=True))
            prob = power * (1.0 / jnp.sum(power, 0, keepdims=True))
            gradient = pack(d_prob[:, here])
            d_score = prob * (gradient - jnp.sum(prob * gradient, 0, keepdims=True))
            score_s[head] += d_score
            prob_low = spread(prob)
            d_low = spread(d_score)
            attended.append(nn(v_chan[band], prob_low))
            d_query.append(nn(k_chan[band], d_low) * scale)
            probs.append(prob_low)
            d_scores.append(d_low)
        attended_s[:, at] = jnp.concatenate(attended, 0).astype(bf16)
        d_query = jnp.concatenate([piece[0:head_size] for piece in d_query], 0)
        d_qkv_s[0, at, :] = d_query.T.astype(bf16)
        d_qkv_s[1, at, :] = nn(jnp.concatenate(d_scores, 1), by_head(q_tok_s[at, :])).astype(bf16)
        d_qkv_s[2, at, :] = nn(jnp.concatenate(probs, 1), by_head(da_tok_s[at, :])).astype(bf16)
        return carry

    lax.fori_loop(0, count // LANES, pair_step, 0)

    unit_turned = unit_low_s[...].T[0:ROWS]
    rest = channels - LANES
    pieces = [nn(unit_turned, d_qkv_s[part]) for part in range(3)]
    d_proj = nn(attended_s[...], grad_s[...])
    pieces.append(
        jnp.concatenate([unslot(d_proj, head_size), jnp.zeros((ROWS - channels, channels), f32)], 0)
    )
    pack_s[...] = jnp.zeros(pack_s.shape, f32)
    for at, piece in enumerate(pieces):
        pack_s[at * ROWS : (at + 1) * ROWS, :] = piece[:, 0:LANES]
        low = (4 + at // 2) * ROWS
        side = (at % 2) * SPAN
        pack_s[low : low + ROWS, side : side + rest] = piece[:, LANES:]
    lines = []
    for head in range(HEADS):
        both = score_s[head]
        both = jnp.where(first, both + pltpu.roll(both, SPAN, 1), 0.0)
        line = both[(WIN - 1) * WIN :]
        for rj in range(WIN - 1):
            line += pltpu.roll(both[rj * WIN : (rj + 1) * WIN], WIN * (WIN - 1 - rj), 1)
        lines.append(line)
    lines = jnp.concatenate(lines, 0)
    high = lines.astype(bf16)
    low = (lines - high.astype(f32)).astype(bf16)
    cj_of = iota((HEADS * WIN, 1), 0) % WIN
    table = jnp.zeros((HEADS * WIN, 2 * LANES), f32)
    for cj in range(WIN):
        hits = table_hits(cj, True)
        table += jnp.where(cj_of == cj, nn(high, hits) + nn(low, hits), 0.0)
    table = table.reshape(HEADS, WIN, 2 * LANES).sum(1)
    pack_s[6 * ROWS : 6 * ROWS + HEADS, :] = table[:, 0:LANES]
    pack_s[6 * ROWS + 8 : 6 * ROWS + 8 + HEADS, :] = table[:, LANES:]
    sums_ref[...] = pack_s[...].astype(bf16)

    d_normed = nt(d_qkv_s[0], parts_ref[0]) + nt(d_qkv_s[1], parts_ref[1]) + nt(d_qkv_s[2], parts_ref[2])
    scaled = d_normed * gain_ref[:, 0:channels]
    unit = unit_s[:, 0:channels]
    mean_one = jnp.sum(scaled, -1, keepdims=True) * (1.0 / channels)
    mean_two = jnp.sum(scaled * unit, -1, keepdims=True) * (1.0 / channels)
    d_input = inv_s[...] * (scaled - mean_one - unit * mean_two)
    out_s[...] = g_s[...] + d_input.reshape(wins, rows, WIN, channels)
    for r in range(rows):
        row = out_s[:, r].reshape(cols, channels)
        moved = jnp.concatenate([row[cols - SHIFT :], row[: cols - SHIFT]], 0).astype(bf16)
        target, place = (own_ref, r) if r < rows - SHIFT else (down_ref, r - (rows - SHIFT))
        target[place] = moved
        over_ref[r] = row[cols - SHIFT :].astype(bf16)


def finish_kernel(out_scale, mine_ref, other_ref, core_ref, weight_ref, gain_ref, offset_ref, d_weight_ref, d_bias_ref, d_proj_ref, d_table_ref, d_gain_ref, d_offset_ref):
    channels = weight_ref.shape[0]
    f32 = jnp.float32
    rest = channels - LANES
    mine = mine_ref[...].astype(f32)
    other = other_ref[...].astype(f32)
    here = core_ref[0] == 0
    low = jnp.where(here, mine, other)
    high = jnp.where(here, other, mine)
    both = jnp.concatenate([low, high], 0) * out_scale
    pieces = []
    for at in range(4):
        row = (4 + at // 2) * ROWS
        side = (at % 2) * SPAN
        pieces.append(
            jnp.concatenate(
                [both[at * ROWS : (at + 1) * ROWS, :], both[row : row + ROWS, side : side + rest]], 1
            )
        )
    gain = gain_ref[...].T
    offset = offset_ref[...].T
    d_gain = jnp.zeros((channels, 1), f32)
    d_offset = jnp.zeros((channels, 1), f32)
    for part in range(3):
        across = slice(part * channels, (part + 1) * channels)
        unit = pieces[part][0:channels]
        bias = pieces[part][channels : channels + 1]
        weight = weight_ref[:, across].astype(f32)
        d_weight_ref[:, across] = gain * unit + offset * bias
        d_bias_ref[:, across] = bias
        d_gain += jnp.sum(weight * unit, -1, keepdims=True)
        d_offset += jnp.sum(weight * bias, -1, keepdims=True)
    d_gain_ref[...] = d_gain.T
    d_offset_ref[...] = d_offset.T
    d_proj_ref[...] = pieces[3][0:channels]
    table = jnp.concatenate([both[6 * ROWS : 6 * ROWS + 8], both[6 * ROWS + 8 :]], 1).T
    d_table_ref[...] = table[0 : d_table_ref.shape[0], 0:HEADS]


def whole(memory_space=pltpu.VMEM):
    return pl.BlockSpec(memory_space=memory_space)


def from_behind(shard, axis, by):
    count = lax.axis_size(axis)
    return lax.ppermute(shard, axis, [(i, (i + by) % count) for i in range(count)])


def diagonal(shard, by):
    rows, cols = lax.axis_size("row"), lax.axis_size("col")
    pairs = [
        (r * cols + c, ((r + by) % rows) * cols + (c + by) % cols) for r in range(rows) for c in range(cols)
    ]
    return lax.ppermute(shard, ("row", "col"), pairs)


def sum_over_crop(buffer):
    rows, cols = lax.axis_size("row"), lax.axis_size("col")
    half = buffer.shape[0] // cols
    core = lax.axis_index("col")
    other = from_behind(buffer, "col", 1)
    start = core * half
    mine = lax.dynamic_slice_in_dim(buffer, start, half, 0).astype(jnp.float32) + lax.dynamic_slice_in_dim(
        other, start, half, 0
    ).astype(jnp.float32)
    mine = mine.astype(jnp.bfloat16)
    steps = [1 << bit for bit in range((rows - 1).bit_length())]
    for at in range(len(steps)):
        pairs = []
        for r in range(rows):
            for c in range(cols):
                step = steps[(at + c) % len(steps)]
                pairs.append((r * cols + c, (r ^ step) * cols + c))
        came = lax.ppermute(mine, ("row", "col"), pairs)
        mine = (mine.astype(jnp.float32) + came.astype(jnp.float32)).astype(jnp.bfloat16)
    return mine, from_behind(mine, "col", 1)


def on_device(
    tokens, grad_out, regions, ln_gain, ln_offset, qkv_weight, qkv_bias, proj_weight, bias_table
):
    rows, cols, channels = tokens.shape
    f32, bf16 = jnp.float32, jnp.bfloat16
    count = rows * cols
    params = pltpu.CompilerParams(vmem_limit_bytes=VMEM_LIMIT)

    def payload(row_slice, col_slice):
        return jnp.concatenate(
            [
                tokens[row_slice, col_slice],
                grad_out[row_slice, col_slice],
                regions[row_slice, col_slice, None].astype(bf16),
            ],
            -1,
        )

    below = from_behind(payload(slice(0, SHIFT), slice(None)), "row", -1)
    right = from_behind(payload(slice(SHIFT, None), slice(0, SHIFT)), "col", -1)
    corner = diagonal(payload(slice(0, SHIFT), slice(0, SHIFT)), -1)

    table = jnp.pad(bias_table.T, ((0, 8 - HEADS), (0, 2 * LANES - bias_table.shape[0])))
    wide = HEADS * SLOT
    bias, tok, chan, proj_slots, parts = pl.pallas_call(
        prepare_kernel,
        name="prepare",
        out_shape=(
            jax.ShapeDtypeStruct((HEADS, SPAN, LANES), f32),
            jax.ShapeDtypeStruct((3, 2 * LANES, wide), bf16),
            jax.ShapeDtypeStruct((3, wide, 2 * LANES), bf16),
            jax.ShapeDtypeStruct((wide, channels), bf16),
            jax.ShapeDtypeStruct((3, channels, channels), bf16),
        ),
        in_specs=[whole()] * 4,
        out_specs=(whole(),) * 5,
        compiler_params=params,
    )(qkv_weight, qkv_bias[None], proj_weight, table)

    gain = jnp.pad(ln_gain, (0, 2 * LANES - channels))[None]
    offset = jnp.pad(ln_offset, (0, 2 * LANES - channels))[None]
    wins = cols // WIN
    own, down, over, sums = pl.pallas_call(
        main_kernel,
        name="window_attention_backward",
        out_shape=(
            jax.ShapeDtypeStruct((SHIFT, cols, channels), bf16),
            jax.ShapeDtypeStruct((SHIFT, cols, channels), bf16),
            jax.ShapeDtypeStruct((rows, SHIFT, channels), bf16),
            jax.ShapeDtypeStruct((BUFFER_ROWS, LANES), bf16),
        ),
        in_specs=[whole()] * 14,
        out_specs=(whole(),) * 4,
        scratch_shapes=[
            pltpu.VMEM((wins, rows, WIN, 2 * LANES), f32),
            pltpu.VMEM((wins, rows, WIN, channels), f32),
            pltpu.VMEM((wins, rows, WIN, 1), f32),
            pltpu.VMEM((count, 2 * LANES), f32),
            pltpu.VMEM((count, 1), f32),
            pltpu.VMEM((count, 2 * LANES), bf16),
            pltpu.VMEM((count, 2 * LANES), bf16),
            pltpu.VMEM((count, channels), bf16),
            pltpu.VMEM((count, channels), bf16),
            pltpu.VMEM((count, wide), bf16),
            pltpu.VMEM((count, wide), bf16),
            pltpu.VMEM((count, channels), bf16),
            pltpu.VMEM((wide, count), bf16),
            pltpu.VMEM((wide, count), bf16),
            pltpu.VMEM((wide, count), bf16),
            pltpu.VMEM((wide, count), bf16),
            pltpu.VMEM((wide, count), bf16),
            pltpu.VMEM((3, count, channels), bf16),
            pltpu.VMEM((HEADS, SPAN, LANES), f32),
            pltpu.VMEM((wins, rows, WIN, channels), f32),
            pltpu.VMEM((BUFFER_ROWS, LANES), f32),
        ],
        compiler_params=params,
    )(
        tokens, grad_out, regions, below, right, corner, gain, offset, bias, tok, chan, proj_weight, proj_slots, parts
    )

    mine, other = sum_over_crop(sums)

    from_above = from_behind(down, "row", 1)
    from_left = from_behind(over[: rows - SHIFT], "col", 1)
    from_corner = diagonal(over[rows - SHIFT :], 1)
    d_tokens = jnp.concatenate(
        [
            jnp.concatenate([from_corner, from_above[:, SHIFT:]], 1),
            jnp.concatenate([from_left, own[:, SHIFT:]], 1),
        ],
        0,
    )

    total_tokens = count * lax.axis_size("row") * lax.axis_size("col")
    core = lax.axis_index("col").astype(jnp.int32).reshape(1)
    d_weight, d_bias, d_proj, d_table, d_gain, d_offset = pl.pallas_call(
        functools.partial(finish_kernel, total_tokens ** (-0.5)),
        name="finish",
        out_shape=(
            jax.ShapeDtypeStruct(qkv_weight.shape, f32),
            jax.ShapeDtypeStruct((1,) + qkv_bias.shape, f32),
            jax.ShapeDtypeStruct(proj_weight.shape, f32),
            jax.ShapeDtypeStruct(bias_table.shape, f32),
            jax.ShapeDtypeStruct((1,) + ln_gain.shape, f32),
            jax.ShapeDtypeStruct((1,) + ln_offset.shape, f32),
        ),
        in_specs=[whole(), whole(), whole(pltpu.SMEM), whole(), whole(), whole()],
        out_specs=(whole(),) * 6,
        compiler_params=params,
    )(mine, other, core, qkv_weight, ln_gain[None], ln_offset[None])
    return (d_tokens, d_weight, d_bias[0], d_proj, d_table, d_gain[0], d_offset[0])


def solution(mesh):
    placed = (
        P(("grp", "row"), "col", None),
        P(("grp", "row"), "col", None),
        P(("grp", "row"), "col"),
        P(),
        P(),
        P(),
        P(),
        P(),
        P(),
    )
    return jax.shard_map(
        on_device,
        mesh=mesh,
        in_specs=placed,
        out_specs=(
            P(("grp", "row"), "col", None),
            P("grp", None),
            P("grp"),
            P("grp", None),
            P("grp", None),
            P("grp"),
            P("grp"),
        ),
        check_vma=False,
    )
```

```python
import functools

import jax
import jax.numpy as jnp
from jax import lax
from jax.experimental import pallas as pl
from jax.experimental.pallas import tpu as pltpu
from jax.sharding import PartitionSpec as P

HEADS = 6
WIN = 8
SHIFT = 4
SPAN = WIN * WIN
MASKED = -10000.0
LANES = 128
SLOT = 32
ROWS = 184
DEEP = 184
TABLE_ROWS = 16
BUFFER_ROWS = 6 * ROWS + TABLE_ROWS

VMEM_LIMIT = 48 * 1024 * 1024


def nn(left, right):
    return lax.dot_general(left, right, (((1,), (0,)), ((), ())), preferred_element_type=jnp.float32)


def nt(left, right):
    return lax.dot_general(left, right, (((1,), (1,)), ((), ())), preferred_element_type=jnp.float32)


def iota(shape, dim):
    return lax.broadcasted_iota(jnp.int32, shape, dim)


def table_hits(cj, lanes_first):
    shape = (LANES, 2 * LANES) if lanes_first else (2 * LANES, LANES)
    lane = iota(shape, 0 if lanes_first else 1)
    entry = iota(shape, 1 if lanes_first else 0)
    wanted = (lane // WIN) * (2 * WIN - 1) + lane % WIN + (WIN - 1) - cj
    return jnp.where((entry == wanted) & (lane < WIN * (2 * WIN - 1)), 1.0, 0.0).astype(jnp.bfloat16)


def split_three(value):
    high = value.astype(jnp.bfloat16)
    rest = value - high.astype(jnp.float32)
    middle = rest.astype(jnp.bfloat16)
    low = (rest - middle.astype(jnp.float32)).astype(jnp.bfloat16)
    return high, middle, low


def slots(rows):
    size = rows.shape[0] // HEADS
    blank = jnp.zeros((SLOT - size, rows.shape[1]), rows.dtype)
    pieces = []
    for head in range(HEADS):
        pieces += [rows[head * size : (head + 1) * size], blank]
    return jnp.concatenate(pieces, 0)


def unslot(rows, size):
    return jnp.concatenate([rows[head * SLOT : head * SLOT + size] for head in range(HEADS)], 0)


def pack_kernel(tokens_ref, grad_ref, region_ref, first_ref, second_ref, edge_ref):
    channels = tokens_ref.shape[0]
    f32, bf16 = jnp.float32, jnp.bfloat16
    tokens = tokens_ref[...].astype(f32)
    grad = grad_ref[...].astype(f32)
    ids = region_ref[...].astype(f32)[None]
    left = iota((1, 1, LANES), 2) < SPAN
    first = jnp.where(left, tokens, pltpu.roll(grad, SPAN, 2)).astype(bf16)
    second = jnp.where(left, pltpu.roll(tokens, SPAN, 2), grad).astype(bf16)
    blank = jnp.zeros((DEEP - channels - 1,) + ids.shape[1:], bf16)
    id_first = ids.astype(bf16)
    id_second = pltpu.roll(ids, SPAN, 2).astype(bf16)
    first_ref[0:channels] = first[:, 0:SHIFT]
    first_ref[channels : channels + 1] = id_first[:, 0:SHIFT]
    first_ref[channels + 1 :] = blank[:, 0:SHIFT]
    second_ref[0:channels] = second[:, 0:SHIFT]
    second_ref[channels : channels + 1] = id_second[:, 0:SHIFT]
    second_ref[channels + 1 :] = blank[:, 0:SHIFT]
    edge_ref[0:channels] = first
    edge_ref[channels : channels + 1] = id_first
    edge_ref[channels + 1 :] = blank


def prepare_kernel(
    tokens_ref,
    grad_ref,
    region_ref,
    weight_ref,
    offsets_ref,
    proj_ref,
    table_ref,
    x_ref,
    g_ref,
    id_ref,
    bias_ref,
    tok_ref,
    chan_ref,
    proj_slots_ref,
    parts_ref,
    turn_s,
):
    channels = weight_ref.shape[0]
    wins = x_ref.shape[0]
    f32 = jnp.float32
    ids = region_ref[...].astype(f32).T
    for source, target in ((tokens_ref, x_ref), (grad_ref, g_ref)):
        turn_s[...] = source[...].astype(f32)
        for r in range(SHIFT):
            row = turn_s[:, SHIFT + r, :].T
            row = jnp.concatenate([row[SHIFT:], row[:SHIFT]], 0)
            target[:, r] = row.reshape(wins, WIN, channels)
    for r in range(SHIFT):
        row = ids[:, SHIFT + r : SHIFT + r + 1]
        row = jnp.concatenate([row[SHIFT:], row[:SHIFT]], 0)
        id_ref[:, r] = row.reshape(wins, WIN, 1)
    for part in range(3):
        weight = weight_ref[:, part * channels : (part + 1) * channels].astype(jnp.float32)
        parts_ref[part] = weight.astype(jnp.bfloat16)
        high, middle, low = split_three(offsets_ref[:, part * channels : (part + 1) * channels])
        full = jnp.concatenate(
            [
                weight,
                high.astype(jnp.float32),
                middle.astype(jnp.float32),
                low.astype(jnp.float32),
                jnp.zeros((256 - channels - 3, channels), jnp.float32),
            ],
            0,
        )
        turned = slots(full.T)
        chan_ref[part] = turned.astype(jnp.bfloat16)
        if part == 0:
            tok_ref[part, :, 0:channels] = full.astype(jnp.bfloat16)
            tok_ref[part, :, channels:] = jnp.zeros((256, HEADS * SLOT - channels), jnp.bfloat16)
        else:
            tok_ref[part] = turned.T.astype(jnp.bfloat16)
    proj_slots_ref[...] = slots(proj_ref[...].astype(jnp.float32)).astype(jnp.bfloat16)
    pieces = split_three(table_ref[...])
    lane = iota((8, LANES), 1)
    for cj in range(WIN):
        hits = table_hits(cj, False)
        spread = nn(pieces[0], hits) + nn(pieces[1], hits) + nn(pieces[2], hits)
        for rj in range(WIN):
            by = WIN * (WIN - 1 - rj)
            moved = spread if by == 0 else pltpu.roll(spread, LANES - by, 1)
            both = jnp.where(lane < SPAN, moved, pltpu.roll(moved, SPAN, 1))
            for head in range(HEADS):
                bias_ref[head, rj * WIN + cj : rj * WIN + cj + 1, :] = both[head : head + 1, :]


def unpack(payload_ref, turn_s, lo):
    turn_s[...] = payload_ref[...].astype(jnp.float32)
    rows = []
    for r in range(lo, lo + SHIFT):
        row = turn_s[:, r, :].T
        rows.append((row[0:SPAN], row[SPAN:]))
    return rows


def windows_kernel(
    last,
    first_win,
    *refs,
):
    if last:
        (payload_ref, payload_two_ref, edge_ref, corner_ref, sums_in_ref, score_in_ref) = refs[:6]
        refs = refs[6:]
    else:
        payload_ref = refs[0]
        refs = refs[1:]
    (
        own_x_ref,
        own_g_ref,
        own_id_ref,
        gain_ref,
        offset_ref,
        bias_ref,
        tok_ref,
        chan_ref,
        proj_ref,
        proj_slots_ref,
        d_qkv_s,
        unit_s,
        inv_s,
        g_s,
        sums_ref,
    ) = refs[:15]
    refs = refs[15:]
    if last:
        score_s = refs[-1]
        pack_s = refs[-2]
        refs = refs[:-2]
    else:
        score_s = refs[0]
        refs = refs[1:]
    (
        turn_s,
        turn_two_s,
        x_s,
        id_s,
        unit_low_s,
        normed_s,
        grad_s,
        q_tok_s,
        k_tok_s,
        v_tok_s,
        da_tok_s,
        q_chan_s,
        k_chan_s,
        v_chan_s,
        da_chan_s,
        attended_s,
    ) = refs
    wins, rows = x_s.shape[0:2]
    channels = g_s.shape[-1]
    head_size = channels // HEADS
    scale = head_size ** (-0.5)
    cols = wins * WIN
    count = rows * cols
    f32 = jnp.float32
    bf16 = jnp.bfloat16

    here = slice(first_win, first_win + wins)
    x_s[:, :, :, LANES:] = jnp.zeros(x_s.shape[:3] + (LANES,), f32)
    x_s[:, 0:SHIFT, :, 0:channels] = own_x_ref[here]
    g_s[:, 0:SHIFT] = own_g_ref[here]
    id_s[:, 0:SHIFT] = own_id_ref[here]
    start = SHIFT + first_win * WIN
    halves = [unpack(payload_ref, turn_s, 0)]
    if last:
        halves.append(unpack(payload_two_ref, turn_s, 0))
        corner = unpack(corner_ref, turn_s, 0)
        edge = unpack(edge_ref, turn_two_s, SHIFT)
    for r in range(SHIFT):
        if last:
            x_row = jnp.concatenate([halves[0][r][0][start:], halves[1][r][0], corner[r][0][:SHIFT]], 0)
            g_row = jnp.concatenate([halves[0][r][1][start:], halves[1][r][1], corner[r][1][:SHIFT]], 0)
        else:
            x_row = halves[0][r][0][start : start + cols]
            g_row = halves[0][r][1][start : start + cols]
        x_s[:, SHIFT + r, :, 0:channels] = x_row[:, 0:channels].reshape(wins, WIN, channels)
        g_s[:, SHIFT + r] = g_row[:, 0:channels].reshape(wins, WIN, channels)
        id_s[:, SHIFT + r] = x_row[:, channels : channels + 1].reshape(wins, WIN, 1)
        if last:
            x_s[wins - 1, r, SHIFT:, 0:channels] = edge[r][0][:SHIFT, 0:channels]
            g_s[wins - 1, r, SHIFT:, :] = edge[r][1][:SHIFT, 0:channels]
            id_s[wins - 1, r, SHIFT:, :] = edge[r][0][:SHIFT, channels : channels + 1]

    x = x_s[...].reshape(count, 2 * LANES)
    lane = iota((1, 2 * LANES), 1)
    inside = lane < channels
    center = jnp.sum(x, -1, keepdims=True) * (1.0 / channels)
    away = jnp.where(inside, x - center, 0.0)
    variance = jnp.sum(away * away, -1, keepdims=True) * (1.0 / channels)
    inv_std = lax.rsqrt(variance + 1e-05)
    unit = away * inv_std
    unit_s[...] = unit
    inv_s[...] = inv_std
    unit_low_s[...] = jnp.where(lane == channels, 1.0, unit).astype(bf16)
    normed_s[...] = jnp.where(
        (lane >= channels) & (lane < channels + 3), 1.0, unit * gain_ref[...] + offset_ref[...]
    ).astype(bf16)
    grad_s[...] = g_s[...].reshape(count, channels).astype(bf16)

    normed = normed_s[...]
    q_tok_s[...] = (nn(normed, tok_ref[0, :, 0:channels]) * scale).astype(bf16)
    k_tok_s[...] = nn(normed, tok_ref[1]).astype(bf16)
    v_tok_s[...] = nn(normed, tok_ref[2]).astype(bf16)
    da_tok_s[...] = nt(grad_s[...], proj_ref[...]).astype(bf16)
    q_chan_s[...] = (nt(chan_ref[0], normed) * scale).astype(bf16)
    k_chan_s[...] = nt(chan_ref[1], normed).astype(bf16)
    v_chan_s[...] = nt(chan_ref[2], normed).astype(bf16)
    da_chan_s[...] = nt(proj_slots_ref[...], grad_s[...]).astype(bf16)

    score_s[...] = score_in_ref[...] if last else jnp.zeros(score_s.shape, f32)
    first = iota((1, LANES), 1) < SPAN
    first_low = jnp.where(first, 1.0, 0.0).astype(bf16)
    second_low = jnp.where(first, 0.0, 1.0).astype(bf16)
    head_of = iota((1, channels), 1) // head_size
    id_lane = iota((1, LANES), 1).astype(f32)

    def pack(square):
        return jnp.where(first, square[0:SPAN], square[SPAN:])

    def spread(packed):
        low = packed.astype(bf16)
        return jnp.concatenate([low * first_low, low * second_low], 0)

    def in_blocks(chan):
        blank = jnp.zeros((SLOT, LANES), bf16)
        lines = []
        for head in range(HEADS):
            line = [blank] * HEADS
            line[head] = chan[head * SLOT : (head + 1) * SLOT]
            lines.append(jnp.concatenate(line, 1))
        return jnp.concatenate(lines, 0)

    def by_head(tok):
        return jnp.concatenate(
            [jnp.where(head_of == head, tok, jnp.zeros_like(tok)) for head in range(HEADS)], 0
        )

    def pair_step(pair, carry):
        at = pl.ds(pl.multiple_of(pair * LANES, LANES), LANES)
        hot = jnp.where(id_s[pl.ds(pair * 2, 2)].reshape(LANES, 1) == id_lane, 1.0, 0.0).astype(bf16)
        match = pack(nt(hot, hot)) > 0.5
        k_chan = k_chan_s[:, at]
        v_chan = v_chan_s[:, at]
        scores = nn(k_tok_s[at, :], in_blocks(q_chan_s[:, at]))
        d_prob = nn(v_tok_s[at, :], in_blocks(da_chan_s[:, at]))
        attended = []
        d_query = []
        probs = []
        d_scores = []
        for head in range(HEADS):
            here = slice(head * LANES, (head + 1) * LANES)
            band = slice(head * SLOT, (head + 1) * SLOT)
            score = jnp.where(match, pack(scores[:, here]) + bias_ref[head], MASKED)
            power = jnp.exp(score - jnp.max(score, 0, keepdims=True))
            prob = power * (1.0 / jnp.sum(power, 0, keepdims=True))
            gradient = pack(d_prob[:, here])
            d_score = prob * (gradient - jnp.sum(prob * gradient, 0, keepdims=True))
            score_s[head] += d_score
            prob_low = spread(prob)
            d_low = spread(d_score)
            attended.append(nn(v_chan[band], prob_low))
            d_query.append(nn(k_chan[band], d_low) * scale)
            probs.append(prob_low)
            d_scores.append(d_low)
        attended_s[:, at] = jnp.concatenate(attended, 0).astype(bf16)
        d_query = jnp.concatenate([piece[0:head_size] for piece in d_query], 0)
        d_qkv_s[0, at, :] = d_query.T.astype(bf16)
        d_qkv_s[1, at, :] = nn(jnp.concatenate(d_scores, 1), by_head(q_tok_s[at, :])).astype(bf16)
        d_qkv_s[2, at, :] = nn(jnp.concatenate(probs, 1), by_head(da_tok_s[at, :])).astype(bf16)
        return carry

    lax.fori_loop(0, count // LANES, pair_step, 0)

    unit_turned = unit_low_s[...].T[0:ROWS]
    rest = channels - LANES
    pieces = [nn(unit_turned, d_qkv_s[part]) for part in range(3)]
    d_proj = nn(attended_s[...], grad_s[...])
    pieces.append(
        jnp.concatenate([unslot(d_proj, head_size), jnp.zeros((ROWS - channels, channels), f32)], 0)
    )
    if not last:
        for at, piece in enumerate(pieces):
            sums_ref[at] = piece
        return
    pack_s[...] = jnp.zeros(pack_s.shape, f32)
    for at, piece in enumerate(pieces):
        piece = piece + sums_in_ref[at]
        pack_s[at * ROWS : (at + 1) * ROWS, :] = piece[:, 0:LANES]
        low = (4 + at // 2) * ROWS
        side = (at % 2) * SPAN
        pack_s[low : low + ROWS, side : side + rest] = piece[:, LANES:]
    lines = []
    for head in range(HEADS):
        both = score_s[head]
        both = jnp.where(first, both + pltpu.roll(both, SPAN, 1), 0.0)
        line = both[(WIN - 1) * WIN :]
        for rj in range(WIN - 1):
            line += pltpu.roll(both[rj * WIN : (rj + 1) * WIN], WIN * (WIN - 1 - rj), 1)
        lines.append(line)
    lines = jnp.concatenate(lines, 0)
    high = lines.astype(bf16)
    low = (lines - high.astype(f32)).astype(bf16)
    cj_of = iota((HEADS * WIN, 1), 0) % WIN
    table = jnp.zeros((HEADS * WIN, 2 * LANES), f32)
    for cj in range(WIN):
        hits = table_hits(cj, True)
        table += jnp.where(cj_of == cj, nn(high, hits) + nn(low, hits), 0.0)
    table = table.reshape(HEADS, WIN, 2 * LANES).sum(1)
    pack_s[6 * ROWS : 6 * ROWS + HEADS, :] = table[:, 0:LANES]
    pack_s[6 * ROWS + 8 : 6 * ROWS + 8 + HEADS, :] = table[:, LANES:]
    sums_ref[...] = pack_s[...].astype(bf16)

def input_kernel(*refs):
    blocks = [refs[0:4], refs[4:8]]
    gain_ref, parts_ref, out_ref, turn_s = refs[8:]
    f32 = jnp.float32
    channels = parts_ref.shape[1]
    done = []
    for d_qkv_ref, unit_ref, inv_ref, g_ref in blocks:
        d_normed = sum(nt(d_qkv_ref[part], parts_ref[part]) for part in range(3))
        scaled = d_normed * gain_ref[:, 0:channels]
        unit = unit_ref[:, 0:channels]
        mean_one = jnp.sum(scaled, -1, keepdims=True) * (1.0 / channels)
        mean_two = jnp.sum(scaled * unit, -1, keepdims=True) * (1.0 / channels)
        d_input = inv_ref[...] * (scaled - mean_one - unit * mean_two)
        done.append(g_ref[...] + d_input.reshape(g_ref.shape))
    for r in range(turn_s.shape[1]):
        row = jnp.concatenate([block[:, r].reshape(-1, channels) for block in done], 0)
        row = jnp.concatenate([row[-SHIFT:], row[:-SHIFT]], 0)
        turn_s[:, r, :] = row.T
    out_ref[...] = turn_s[...].astype(out_ref.dtype)


def finish_kernel(out_scale, mine_ref, other_ref, core_ref, weight_ref, gain_ref, offset_ref, d_weight_ref, d_bias_ref, d_proj_ref, d_table_ref, d_gain_ref, d_offset_ref):
    channels = weight_ref.shape[0]
    f32 = jnp.float32
    rest = channels - LANES
    mine = mine_ref[...].astype(f32)
    other = other_ref[...].astype(f32)
    here = core_ref[0] == 0
    low = jnp.where(here, mine, other)
    high = jnp.where(here, other, mine)
    both = jnp.concatenate([low, high], 0) * out_scale
    pieces = []
    for at in range(4):
        row = (4 + at // 2) * ROWS
        side = (at % 2) * SPAN
        pieces.append(
            jnp.concatenate(
                [both[at * ROWS : (at + 1) * ROWS, :], both[row : row + ROWS, side : side + rest]], 1
            )
        )
    gain = gain_ref[...].T
    offset = offset_ref[...].T
    d_gain = jnp.zeros((channels, 1), f32)
    d_offset = jnp.zeros((channels, 1), f32)
    for part in range(3):
        across = slice(part * channels, (part + 1) * channels)
        unit = pieces[part][0:channels]
        bias = pieces[part][channels : channels + 1]
        weight = weight_ref[:, across].astype(f32)
        d_weight_ref[:, across] = gain * unit + offset * bias
        d_bias_ref[:, across] = bias
        d_gain += jnp.sum(weight * unit, -1, keepdims=True)
        d_offset += jnp.sum(weight * bias, -1, keepdims=True)
    d_gain_ref[...] = d_gain.T
    d_offset_ref[...] = d_offset.T
    d_proj_ref[...] = pieces[3][0:channels]
    table = jnp.concatenate([both[6 * ROWS : 6 * ROWS + 8], both[6 * ROWS + 8 :]], 1).T
    d_table_ref[...] = table[0 : d_table_ref.shape[0], 0:HEADS]


def whole(memory_space=pltpu.VMEM):
    return pl.BlockSpec(memory_space=memory_space)


def from_behind(shard, axis, by):
    count = lax.axis_size(axis)
    return lax.ppermute(shard, axis, [(i, (i + by) % count) for i in range(count)])


def sum_over_crop(buffer):
    rows, cols = lax.axis_size("row"), lax.axis_size("col")
    half = buffer.shape[0] // cols
    core = lax.axis_index("col")
    other = from_behind(buffer, "col", 1)
    start = core * half
    mine = lax.dynamic_slice_in_dim(buffer, start, half, 0).astype(jnp.float32) + lax.dynamic_slice_in_dim(
        other, start, half, 0
    ).astype(jnp.float32)
    mine = mine.astype(jnp.bfloat16)
    steps = [1 << bit for bit in range((rows - 1).bit_length())]
    for at in range(len(steps)):
        pairs = []
        for r in range(rows):
            for c in range(cols):
                step = steps[(at + c) % len(steps)]
                pairs.append((r * cols + c, (r ^ step) * cols + c))
        came = lax.ppermute(mine, ("row", "col"), pairs)
        mine = (mine.astype(jnp.float32) + came.astype(jnp.float32)).astype(jnp.bfloat16)
    return mine, from_behind(mine, "col", 1)


def on_device(
    tokens, grad_out, regions, ln_gain, ln_offset, qkv_weight, qkv_bias, proj_weight, bias_table
):
    rows, cols, channels = tokens.shape
    f32, bf16 = jnp.float32, jnp.bfloat16
    count = rows * cols
    wins = cols // WIN
    wide = HEADS * SLOT
    params = pltpu.CompilerParams(vmem_limit_bytes=VMEM_LIMIT)

    def call(kernel, name, ins, outs, scratch=()):
        return pl.pallas_call(
            kernel,
            name=name,
            out_shape=tuple(jax.ShapeDtypeStruct(*out) for out in outs),
            in_specs=[whole(pltpu.SMEM) if value.dtype == jnp.int32 and value.ndim == 1 else whole() for value in ins],
            out_specs=(whole(),) * len(outs),
            scratch_shapes=[pltpu.VMEM(*each) for each in scratch],
            compiler_params=params,
        )(*ins)

    x_turned = tokens.transpose(2, 0, 1)
    g_turned = grad_out.transpose(2, 0, 1)
    thin = ((DEEP, SHIFT, cols), bf16)
    first, second, edge = call(
        pack_kernel, "pack", (x_turned, g_turned, regions), (thin, thin, ((DEEP, rows, cols), bf16))
    )
    below = from_behind(first, "row", -1)
    below_two = from_behind(second, "row", -1)
    edge = from_behind(edge, "col", -1)

    table = jnp.pad(bias_table.T, ((0, 8 - HEADS), (0, 2 * LANES - bias_table.shape[0])))
    own_x, own_g, own_id, bias, tok, chan, proj_slots, parts = call(
        prepare_kernel,
        "prepare",
        (x_turned, g_turned, regions, qkv_weight, qkv_bias[None], proj_weight, table),
        (
            ((wins, SHIFT, WIN, channels), f32),
            ((wins, SHIFT, WIN, channels), f32),
            ((wins, SHIFT, WIN, 1), f32),
            ((HEADS, SPAN, LANES), f32),
            ((3, 2 * LANES, wide), bf16),
            ((3, wide, 2 * LANES), bf16),
            ((wide, channels), bf16),
            ((3, channels, channels), bf16),
        ),
        (((channels, rows, cols), f32),),
    )
    gain = jnp.pad(ln_gain, (0, 2 * LANES - channels))[None]
    offset = jnp.pad(ln_offset, (0, 2 * LANES - channels))[None]
    shared = (own_x, own_g, own_id, gain, offset, bias, tok, chan, proj_weight, proj_slots)

    def block(first_win, n, last, ins, name):
        here = n * SPAN
        outs = [
            ((3, here, channels), bf16),
            ((here, 2 * LANES), f32),
            ((here, 1), f32),
            ((n, rows, WIN, channels), f32),
        ]
        score = ((HEADS, SPAN, LANES), f32)
        scratch = [
            ((DEEP, SHIFT, cols), f32),
            ((DEEP, rows, cols), f32),
            ((n, rows, WIN, 2 * LANES), f32),
            ((n, rows, WIN, 1), f32),
            ((here, 2 * LANES), bf16),
            ((here, 2 * LANES), bf16),
            ((here, channels), bf16),
            ((here, channels), bf16),
            ((here, wide), bf16),
            ((here, wide), bf16),
            ((here, channels), bf16),
        ] + [((wide, here), bf16)] * 5
        if last:
            outs += [((BUFFER_ROWS, LANES), bf16)]
            scratch += [((BUFFER_ROWS, LANES), f32), score]
        else:
            outs += [((4, ROWS, channels), f32), score]
        return call(functools.partial(windows_kernel, last, first_win), name, ins + shared, outs, scratch)

    early = (cols // 2 - SHIFT) // (2 * WIN) * 2
    corner = from_behind(below, "col", -1)
    *one, part_sums, score = block(0, early, False, (below,), "windows_left")
    *two, sums = block(
        early, wins - early, True, (below, below_two, edge, corner, part_sums, score), "windows_right"
    )

    mine, other = sum_over_crop(sums)

    (framed,) = call(
        input_kernel,
        "input_backward",
        (*one, *two, gain, parts),
        (((channels, rows, cols), bf16),),
        (((channels, rows, cols), f32),),
    )
    beside = from_behind(framed, "col", 1)
    framed = jnp.where(jnp.arange(cols) < SHIFT, beside, framed)
    above = from_behind(framed[:, rows - SHIFT :], "row", 1)
    d_tokens = jnp.concatenate([above, framed[:, : rows - SHIFT]], 1).transpose(1, 2, 0)

    total_tokens = count * lax.axis_size("row") * lax.axis_size("col")
    core = lax.axis_index("col").astype(jnp.int32).reshape(1)
    d_weight, d_bias, d_proj, d_table, d_gain, d_offset = call(
        functools.partial(finish_kernel, total_tokens ** (-0.5)),
        "finish",
        (mine, other, core, qkv_weight, ln_gain[None], ln_offset[None]),
        (
            (qkv_weight.shape, f32),
            ((1,) + qkv_bias.shape, f32),
            (proj_weight.shape, f32),
            (bias_table.shape, f32),
            ((1,) + ln_gain.shape, f32),
            ((1,) + ln_offset.shape, f32),
        ),
    )
    return (d_tokens, d_weight, d_bias[0], d_proj, d_table, d_gain[0], d_offset[0])


def solution(mesh):
    placed = (
        P(("grp", "row"), "col", None),
        P(("grp", "row"), "col", None),
        P(("grp", "row"), "col"),
        P(),
        P(),
        P(),
        P(),
        P(),
        P(),
    )
    return jax.shard_map(
        on_device,
        mesh=mesh,
        in_specs=placed,
        out_specs=(
            P(("grp", "row"), "col", None),
            P("grp", None),
            P("grp"),
            P("grp", None),
            P("grp", None),
            P("grp"),
            P("grp"),
        ),
        check_vma=False,
    )
```

```python
import functools

import jax
import jax.numpy as jnp
from jax import lax
from jax.experimental import pallas as pl
from jax.experimental.pallas import tpu as pltpu
from jax.sharding import PartitionSpec as P

HEADS = 6
WIN = 8
SHIFT = 4
SPAN = WIN * WIN
MASKED = -10000.0
LANES = 128
SLOT = 32
ROWS = 184
TABLE_ROWS = 16
BUFFER_ROWS = 6 * ROWS + TABLE_ROWS

VMEM_LIMIT = 32 * 1024 * 1024


def nn(left, right):
    return lax.dot_general(left, right, (((1,), (0,)), ((), ())), preferred_element_type=jnp.float32)


def nt(left, right):
    return lax.dot_general(left, right, (((1,), (1,)), ((), ())), preferred_element_type=jnp.float32)


def iota(shape, dim):
    return lax.broadcasted_iota(jnp.int32, shape, dim)


def table_hits(cj, lanes_first):
    shape = (LANES, 2 * LANES) if lanes_first else (2 * LANES, LANES)
    lane = iota(shape, 0 if lanes_first else 1)
    entry = iota(shape, 1 if lanes_first else 0)
    wanted = (lane // WIN) * (2 * WIN - 1) + lane % WIN + (WIN - 1) - cj
    return jnp.where((entry == wanted) & (lane < WIN * (2 * WIN - 1)), 1.0, 0.0).astype(jnp.bfloat16)


def split_three(value):
    high = value.astype(jnp.bfloat16)
    rest = value - high.astype(jnp.float32)
    middle = rest.astype(jnp.bfloat16)
    low = (rest - middle.astype(jnp.float32)).astype(jnp.bfloat16)
    return high, middle, low


def slots(rows):
    size = rows.shape[0] // HEADS
    blank = jnp.zeros((SLOT - size, rows.shape[1]), rows.dtype)
    pieces = []
    for head in range(HEADS):
        pieces += [rows[head * size : (head + 1) * size], blank]
    return jnp.concatenate(pieces, 0)


def unslot(rows, size):
    return jnp.concatenate([rows[head * SLOT : head * SLOT + size] for head in range(HEADS)], 0)


def prepare_kernel(weight_ref, offsets_ref, proj_ref, table_ref, bias_ref, tok_ref, chan_ref, proj_slots_ref, parts_ref):
    channels = weight_ref.shape[0]
    for part in range(3):
        weight = weight_ref[:, part * channels : (part + 1) * channels].astype(jnp.float32)
        parts_ref[part] = weight.astype(jnp.bfloat16)
        high, middle, low = split_three(offsets_ref[:, part * channels : (part + 1) * channels])
        full = jnp.concatenate(
            [
                weight,
                high.astype(jnp.float32),
                middle.astype(jnp.float32),
                low.astype(jnp.float32),
                jnp.zeros((256 - channels - 3, channels), jnp.float32),
            ],
            0,
        )
        turned = slots(full.T)
        chan_ref[part] = turned.astype(jnp.bfloat16)
        if part == 0:
            tok_ref[part, :, 0:channels] = full.astype(jnp.bfloat16)
            tok_ref[part, :, channels:] = jnp.zeros((256, HEADS * SLOT - channels), jnp.bfloat16)
        else:
            tok_ref[part] = turned.T.astype(jnp.bfloat16)
    proj_slots_ref[...] = slots(proj_ref[...].astype(jnp.float32)).astype(jnp.bfloat16)
    pieces = split_three(table_ref[...])
    lane = iota((8, LANES), 1)
    for cj in range(WIN):
        hits = table_hits(cj, False)
        spread = nn(pieces[0], hits) + nn(pieces[1], hits) + nn(pieces[2], hits)
        for rj in range(WIN):
            by = WIN * (WIN - 1 - rj)
            moved = spread if by == 0 else pltpu.roll(spread, LANES - by, 1)
            both = jnp.where(lane < SPAN, moved, pltpu.roll(moved, SPAN, 1))
            for head in range(HEADS):
                bias_ref[head, rj * WIN + cj : rj * WIN + cj + 1, :] = both[head : head + 1, :]


def main_kernel(
    tokens_ref,
    grad_ref,
    region_ref,
    below_ref,
    right_ref,
    corner_ref,
    gain_ref,
    offset_ref,
    bias_ref,
    tok_ref,
    chan_ref,
    proj_ref,
    proj_slots_ref,
    parts_ref,
    core_ref,
    keep_ref,
    send_ref,
    framed_ref,
    turn_s,
    turn_out_s,
    x_s,
    g_s,
    id_s,
    unit_s,
    inv_s,
    unit_low_s,
    normed_s,
    grad_s,
    q_tok_s,
    k_tok_s,
    v_tok_s,
    da_tok_s,
    q_chan_s,
    k_chan_s,
    v_chan_s,
    da_chan_s,
    attended_s,
    d_qkv_s,
    score_s,
    pack_s,
):
    rows, cols, channels = tokens_ref.shape
    head_size = channels // HEADS
    scale = head_size ** (-0.5)
    count = rows * cols
    wins = cols // WIN
    f32 = jnp.float32
    bf16 = jnp.bfloat16

    x_s[:, :, :, LANES:] = jnp.zeros(x_s.shape[:3] + (LANES,), f32)
    turn_s[...] = below_ref[...].astype(f32)
    ids = region_ref[...].astype(f32).T
    at_id = slice(2 * channels, 2 * channels + 1)
    col_part = ids[:, 0:1] - 4.0 * jnp.floor(ids[:, 0:1] * 0.25)
    for r in range(rows):
        if r < rows - SHIFT:
            x_body = tokens_ref[r + SHIFT].astype(f32)
            g_body = grad_ref[r + SHIFT].astype(f32)
            side = right_ref[r].astype(f32)
            id_body = ids[:, r + SHIFT : r + SHIFT + 1]
        else:
            here = r - (rows - SHIFT)
            body = turn_s[:, here, :].T
            x_body = body[:, 0:channels]
            g_body = body[:, channels : 2 * channels]
            side = corner_ref[here].astype(f32)
            id_body = col_part + 4.0 * jnp.floor(side[0:1, at_id] * 0.25)
        x_row = jnp.concatenate([x_body[SHIFT:], side[:, 0:channels]], 0)
        g_row = jnp.concatenate([g_body[SHIFT:], side[:, channels : 2 * channels]], 0)
        id_row = jnp.concatenate([id_body[SHIFT:], side[:, at_id]], 0)
        x_s[:, r, :, 0:channels] = x_row.reshape(wins, WIN, channels)
        g_s[:, r, :, :] = g_row.reshape(wins, WIN, channels)
        id_s[:, r, :, :] = id_row.reshape(wins, WIN, 1)

    x = x_s[...].reshape(count, 2 * LANES)
    lane = iota((1, 2 * LANES), 1)
    inside = lane < channels
    center = jnp.sum(x, -1, keepdims=True) * (1.0 / channels)
    away = jnp.where(inside, x - center, 0.0)
    variance = jnp.sum(away * away, -1, keepdims=True) * (1.0 / channels)
    inv_std = lax.rsqrt(variance + 1e-05)
    unit = away * inv_std
    unit_s[...] = unit
    inv_s[...] = inv_std
    unit_low_s[...] = jnp.where(lane == channels, 1.0, unit).astype(bf16)
    normed_s[...] = jnp.where(
        (lane >= channels) & (lane < channels + 3), 1.0, unit * gain_ref[...] + offset_ref[...]
    ).astype(bf16)
    grad_s[...] = g_s[...].reshape(count, channels).astype(bf16)

    normed = normed_s[...]
    q_tok_s[...] = (nn(normed, tok_ref[0, :, 0:channels]) * scale).astype(bf16)
    k_tok_s[...] = nn(normed, tok_ref[1]).astype(bf16)
    v_tok_s[...] = nn(normed, tok_ref[2]).astype(bf16)
    da_tok_s[...] = nt(grad_s[...], proj_ref[...]).astype(bf16)
    q_chan_s[...] = (nt(chan_ref[0], normed) * scale).astype(bf16)
    k_chan_s[...] = nt(chan_ref[1], normed).astype(bf16)
    v_chan_s[...] = nt(chan_ref[2], normed).astype(bf16)
    da_chan_s[...] = nt(proj_slots_ref[...], grad_s[...]).astype(bf16)

    score_s[...] = jnp.zeros(score_s.shape, f32)
    first = iota((1, LANES), 1) < SPAN
    first_low = jnp.where(first, 1.0, 0.0).astype(bf16)
    second_low = jnp.where(first, 0.0, 1.0).astype(bf16)
    head_of = iota((1, channels), 1) // head_size
    id_lane = iota((1, LANES), 1).astype(f32)

    def pack(square):
        return jnp.where(first, square[0:SPAN], square[SPAN:])

    def spread(packed):
        low = packed.astype(bf16)
        return jnp.concatenate([low * first_low, low * second_low], 0)

    def in_blocks(chan):
        blank = jnp.zeros((SLOT, LANES), bf16)
        lines = []
        for head in range(HEADS):
            line = [blank] * HEADS
            line[head] = chan[head * SLOT : (head + 1) * SLOT]
            lines.append(jnp.concatenate(line, 1))
        return jnp.concatenate(lines, 0)

    def by_head(tok):
        return jnp.concatenate(
            [jnp.where(head_of == head, tok, jnp.zeros_like(tok)) for head in range(HEADS)], 0
        )

    def pair_step(pair, carry):
        at = pl.ds(pl.multiple_of(pair * LANES, LANES), LANES)
        hot = jnp.where(id_s[pl.ds(pair * 2, 2)].reshape(LANES, 1) == id_lane, 1.0, 0.0).astype(bf16)
        match = pack(nt(hot, hot)) > 0.5
        k_chan = k_chan_s[:, at]
        v_chan = v_chan_s[:, at]
        scores = nn(k_tok_s[at, :], in_blocks(q_chan_s[:, at]))
        d_prob = nn(v_tok_s[at, :], in_blocks(da_chan_s[:, at]))
        attended = []
        d_query = []
        probs = []
        d_scores = []
        for head in range(HEADS):
            here = slice(head * LANES, (head + 1) * LANES)
            band = slice(head * SLOT, (head + 1) * SLOT)
            score = jnp.where(match, pack(scores[:, here]) + bias_ref[head], MASKED)
            power = jnp.exp(score - jnp.max(score, 0, keepdims=True))
            prob = power * (1.0 / jnp.sum(power, 0, keepdims=True))
            gradient = pack(d_prob[:, here])
            d_score = prob * (gradient - jnp.sum(prob * gradient, 0, keepdims=True))
            score_s[head] += d_score
            prob_low = spread(prob)
            d_low = spread(d_score)
            attended.append(nn(v_chan[band], prob_low))
            d_query.append(nn(k_chan[band], d_low) * scale)
            probs.append(prob_low)
            d_scores.append(d_low)
        attended_s[:, at] = jnp.concatenate(attended, 0).astype(bf16)
        d_query = jnp.concatenate([piece[0:head_size] for piece in d_query], 0)
        d_qkv_s[0, at, :] = d_query.T.astype(bf16)
        d_qkv_s[1, at, :] = nn(jnp.concatenate(d_scores, 1), by_head(q_tok_s[at, :])).astype(bf16)
        d_qkv_s[2, at, :] = nn(jnp.concatenate(probs, 1), by_head(da_tok_s[at, :])).astype(bf16)
        return carry

    lax.fori_loop(0, count // LANES, pair_step, 0, unroll=True)

    unit_turned = unit_low_s[...].T[0:ROWS]
    rest = channels - LANES
    pieces = [nn(unit_turned, d_qkv_s[part]) for part in range(3)]
    d_proj = nn(attended_s[...], grad_s[...])
    pieces.append(
        jnp.concatenate([unslot(d_proj, head_size), jnp.zeros((ROWS - channels, channels), f32)], 0)
    )
    pack_s[...] = jnp.zeros(pack_s.shape, f32)
    for at, piece in enumerate(pieces):
        pack_s[at * ROWS : (at + 1) * ROWS, :] = piece[:, 0:LANES]
        low = (4 + at // 2) * ROWS
        side = (at % 2) * SPAN
        pack_s[low : low + ROWS, side : side + rest] = piece[:, LANES:]
    lines = []
    for head in range(HEADS):
        both = score_s[head]
        both = jnp.where(first, both + pltpu.roll(both, SPAN, 1), 0.0)
        line = both[(WIN - 1) * WIN :]
        for rj in range(WIN - 1):
            line += pltpu.roll(both[rj * WIN : (rj + 1) * WIN], WIN * (WIN - 1 - rj), 1)
        lines.append(line)
    lines = jnp.concatenate(lines, 0)
    high = lines.astype(bf16)
    low = (lines - high.astype(f32)).astype(bf16)
    cj_of = iota((HEADS * WIN, 1), 0) % WIN
    table = jnp.zeros((HEADS * WIN, 2 * LANES), f32)
    for cj in range(WIN):
        hits = table_hits(cj, True)
        table += jnp.where(cj_of == cj, nn(high, hits) + nn(low, hits), 0.0)
    table = table.reshape(HEADS, WIN, 2 * LANES).sum(1)
    pack_s[6 * ROWS : 6 * ROWS + HEADS, :] = table[:, 0:LANES]
    pack_s[6 * ROWS + 8 : 6 * ROWS + 8 + HEADS, :] = table[:, LANES:]
    half = keep_ref.shape[0]
    low_half = pack_s[0:half, :].astype(bf16)
    high_half = pack_s[half:, :].astype(bf16)
    lower = core_ref[0] == 0
    keep_ref[...] = jnp.where(lower, low_half, high_half)
    send_ref[...] = jnp.where(lower, high_half, low_half)

    d_normed = nt(d_qkv_s[0], parts_ref[0]) + nt(d_qkv_s[1], parts_ref[1]) + nt(d_qkv_s[2], parts_ref[2])
    scaled = d_normed * gain_ref[:, 0:channels]
    unit = unit_s[:, 0:channels]
    mean_one = jnp.sum(scaled, -1, keepdims=True) * (1.0 / channels)
    mean_two = jnp.sum(scaled * unit, -1, keepdims=True) * (1.0 / channels)
    d_input = inv_s[...] * (scaled - mean_one - unit * mean_two)
    g_s[...] = g_s[...] + d_input.reshape(g_s.shape)
    for r in range(rows):
        row = g_s[:, r].reshape(cols, channels)
        row = jnp.concatenate([row[cols - SHIFT :], row[: cols - SHIFT]], 0)
        turn_out_s[:, r, :] = row.T
    framed_ref[...] = turn_out_s[...].astype(bf16)


def finish_kernel(out_scale, mine_ref, other_ref, core_ref, weight_ref, gain_ref, offset_ref, d_weight_ref, d_bias_ref, d_proj_ref, d_table_ref, d_gain_ref, d_offset_ref):
    channels = weight_ref.shape[0]
    f32 = jnp.float32
    rest = channels - LANES
    mine = mine_ref[...].astype(f32)
    other = other_ref[...].astype(f32)
    here = core_ref[0] == 0
    low = jnp.where(here, mine, other)
    high = jnp.where(here, other, mine)
    both = jnp.concatenate([low, high], 0) * out_scale
    pieces = []
    for at in range(4):
        row = (4 + at // 2) * ROWS
        side = (at % 2) * SPAN
        pieces.append(
            jnp.concatenate(
                [both[at * ROWS : (at + 1) * ROWS, :], both[row : row + ROWS, side : side + rest]], 1
            )
        )
    gain = gain_ref[...].T
    offset = offset_ref[...].T
    d_gain = jnp.zeros((channels, 1), f32)
    d_offset = jnp.zeros((channels, 1), f32)
    biases = []
    for part in range(3):
        across = slice(part * channels, (part + 1) * channels)
        unit = pieces[part][0:channels]
        bias = pieces[part][channels : channels + 1]
        weight = weight_ref[:, across].astype(f32)
        d_weight_ref[:, across] = gain * unit + offset * bias
        biases.append(bias)
        d_gain += jnp.sum(weight * unit, -1, keepdims=True)
        d_offset += jnp.sum(weight * bias, -1, keepdims=True)
    d_bias_ref[...] = jnp.concatenate(biases, 1).reshape(d_bias_ref.shape)
    d_gain_ref[...] = d_gain.T.reshape(channels)
    d_offset_ref[...] = d_offset.T.reshape(channels)
    d_proj_ref[...] = pieces[3][0:channels]
    table = jnp.concatenate([both[6 * ROWS : 6 * ROWS + 8], both[6 * ROWS + 8 :]], 1)
    d_table_ref[...] = table[0:HEADS, 0 : d_table_ref.shape[1]]


def whole(memory_space=pltpu.VMEM):
    return pl.BlockSpec(memory_space=memory_space)


def from_behind(shard, axis, by):
    count = lax.axis_size(axis)
    return lax.ppermute(shard, axis, [(i, (i + by) % count) for i in range(count)])


def diagonal(shard, by):
    rows, cols = lax.axis_size("row"), lax.axis_size("col")
    pairs = [
        (r * cols + c, ((r + by) % rows) * cols + (c + by) % cols) for r in range(rows) for c in range(cols)
    ]
    return lax.ppermute(shard, ("row", "col"), pairs)


def exchange_steps():
    rows, cols = lax.axis_size("row"), lax.axis_size("col")
    steps = [1 << bit for bit in range((rows - 1).bit_length())]
    for at in range(len(steps)):
        yield [
            (r * cols + c, (r ^ steps[(at + c) % len(steps)]) * cols + c) for r in range(rows) for c in range(cols)
        ]


def add(left, right):
    return (left.astype(jnp.float32) + right.astype(jnp.float32)).astype(jnp.bfloat16)


def on_device(
    tokens, grad_out, regions, ln_gain, ln_offset, qkv_weight, qkv_bias, proj_weight, bias_table
):
    rows, cols, channels = tokens.shape
    f32, bf16 = jnp.float32, jnp.bfloat16
    count = rows * cols
    params = pltpu.CompilerParams(vmem_limit_bytes=VMEM_LIMIT)

    x_turned = tokens.transpose(2, 0, 1)
    g_turned = grad_out.transpose(2, 0, 1)
    core = lax.axis_index("col").astype(jnp.int32).reshape(1)

    below = jnp.concatenate([x_turned[:, :SHIFT], g_turned[:, :SHIFT]], 0)
    below, near_tokens, near_grad, near_ids = lax.optimization_barrier((below, tokens, grad_out, regions))
    below = from_behind(below, "row", -1)

    def border(row_slice):
        return jnp.concatenate(
            [
                near_tokens[row_slice, :SHIFT],
                near_grad[row_slice, :SHIFT],
                near_ids[row_slice, :SHIFT, None].astype(bf16),
            ],
            -1,
        )

    right = from_behind(border(slice(SHIFT, None)), "col", -1)
    corner = diagonal(border(slice(0, SHIFT)), -1)

    table = jnp.pad(bias_table.T, ((0, 8 - HEADS), (0, 2 * LANES - bias_table.shape[0])))
    wide = HEADS * SLOT
    bias, tok, chan, proj_slots, parts = pl.pallas_call(
        prepare_kernel,
        name="prepare",
        out_shape=(
            jax.ShapeDtypeStruct((HEADS, SPAN, LANES), f32),
            jax.ShapeDtypeStruct((3, 2 * LANES, wide), bf16),
            jax.ShapeDtypeStruct((3, wide, 2 * LANES), bf16),
            jax.ShapeDtypeStruct((wide, channels), bf16),
            jax.ShapeDtypeStruct((3, channels, channels), bf16),
        ),
        in_specs=[whole()] * 4,
        out_specs=(whole(),) * 5,
        compiler_params=params,
    )(qkv_weight, qkv_bias[None], proj_weight, table)

    gain = jnp.pad(ln_gain, (0, 2 * LANES - channels))[None]
    offset = jnp.pad(ln_offset, (0, 2 * LANES - channels))[None]
    wins = cols // WIN
    keep, send, framed = pl.pallas_call(
        main_kernel,
        name="window_attention_backward",
        out_shape=(
            jax.ShapeDtypeStruct((BUFFER_ROWS // 2, LANES), bf16),
            jax.ShapeDtypeStruct((BUFFER_ROWS // 2, LANES), bf16),
            jax.ShapeDtypeStruct((channels, rows, cols), bf16),
        ),
        in_specs=[whole()] * 14 + [whole(pltpu.SMEM)],
        out_specs=(whole(),) * 3,
        scratch_shapes=[
            pltpu.VMEM((2 * channels, SHIFT, cols), f32),
            pltpu.VMEM((channels, rows, cols), f32),
            pltpu.VMEM((wins, rows, WIN, 2 * LANES), f32),
            pltpu.VMEM((wins, rows, WIN, channels), f32),
            pltpu.VMEM((wins, rows, WIN, 1), f32),
            pltpu.VMEM((count, 2 * LANES), f32),
            pltpu.VMEM((count, 1), f32),
            pltpu.VMEM((count, 2 * LANES), bf16),
            pltpu.VMEM((count, 2 * LANES), bf16),
            pltpu.VMEM((count, channels), bf16),
            pltpu.VMEM((count, channels), bf16),
            pltpu.VMEM((count, wide), bf16),
            pltpu.VMEM((count, wide), bf16),
            pltpu.VMEM((count, channels), bf16),
            pltpu.VMEM((wide, count), bf16),
            pltpu.VMEM((wide, count), bf16),
            pltpu.VMEM((wide, count), bf16),
            pltpu.VMEM((wide, count), bf16),
            pltpu.VMEM((wide, count), bf16),
            pltpu.VMEM((3, count, channels), bf16),
            pltpu.VMEM((HEADS, SPAN, LANES), f32),
            pltpu.VMEM((BUFFER_ROWS, LANES), f32),
        ],
        compiler_params=params,
    )(
        near_tokens, near_grad, near_ids, below, right, corner, gain, offset, bias, tok, chan, proj_weight, proj_slots, parts, core
    )

    above = from_behind(framed[:, rows - SHIFT :], "row", 1)
    mine = add(keep, from_behind(send, "col", 1))
    steps = list(exchange_steps())
    for at, pairs in enumerate(steps):
        if at == 1 or len(steps) == 1:
            above, mine = lax.optimization_barrier((above, mine))
            framed = jnp.concatenate([above, framed[:, : rows - SHIFT]], 1)
            beside = from_behind(framed, "col", 1)
        if at == 2:
            beside, mine = lax.optimization_barrier((beside, mine))
        mine = add(mine, lax.ppermute(mine, ("row", "col"), pairs))
    d_tokens = jnp.where(jnp.arange(cols) < SHIFT, beside, framed).transpose(1, 2, 0)
    other = from_behind(mine, "col", 1)

    total_tokens = count * lax.axis_size("row") * lax.axis_size("col")
    d_weight, d_bias, d_proj, d_table, d_gain, d_offset = pl.pallas_call(
        functools.partial(finish_kernel, total_tokens ** (-0.5)),
        name="finish",
        out_shape=(
            jax.ShapeDtypeStruct(qkv_weight.shape, f32),
            jax.ShapeDtypeStruct(qkv_bias.shape, f32),
            jax.ShapeDtypeStruct(proj_weight.shape, f32),
            jax.ShapeDtypeStruct(bias_table.shape[::-1], f32),
            jax.ShapeDtypeStruct(ln_gain.shape, f32),
            jax.ShapeDtypeStruct(ln_offset.shape, f32),
        ),
        in_specs=[whole(), whole(), whole(pltpu.SMEM), whole(), whole(), whole()],
        out_specs=(whole(),) * 6,
        compiler_params=params,
    )(mine, other, core, qkv_weight, ln_gain[None], ln_offset[None])
    return (d_tokens, d_weight, d_bias, d_proj, d_table.T, d_gain, d_offset)


def solution(mesh):
    placed = (
        P(("grp", "row"), "col", None),
        P(("grp", "row"), "col", None),
        P(("grp", "row"), "col"),
        P(),
        P(),
        P(),
        P(),
        P(),
        P(),
    )
    return jax.shard_map(
        on_device,
        mesh=mesh,
        in_specs=placed,
        out_specs=(
            P(("grp", "row"), "col", None),
            P("grp", None),
            P("grp"),
            P("grp", None),
            P("grp", None),
            P("grp"),
            P("grp"),
        ),
        check_vma=False,
    )
```

```python
import functools

import jax
import jax.numpy as jnp
from jax import lax
from jax.experimental import pallas as pl
from jax.experimental.pallas import tpu as pltpu
from jax.sharding import PartitionSpec as P

HEADS = 6
WIN = 8
SHIFT = 4
SPAN = WIN * WIN
MASKED = -10000.0
LANES = 128
SLOT = 32
ROWS = 184
TABLE_ROWS = 16
BUFFER_ROWS = 6 * ROWS + TABLE_ROWS

VMEM_LIMIT = 32 * 1024 * 1024


def nn(left, right):
    return lax.dot_general(left, right, (((1,), (0,)), ((), ())), preferred_element_type=jnp.float32)


def nt(left, right):
    return lax.dot_general(left, right, (((1,), (1,)), ((), ())), preferred_element_type=jnp.float32)


def iota(shape, dim):
    return lax.broadcasted_iota(jnp.int32, shape, dim)


def table_hits(cj, lanes_first):
    shape = (LANES, 2 * LANES) if lanes_first else (2 * LANES, LANES)
    lane = iota(shape, 0 if lanes_first else 1)
    entry = iota(shape, 1 if lanes_first else 0)
    wanted = (lane // WIN) * (2 * WIN - 1) + lane % WIN + (WIN - 1) - cj
    return jnp.where((entry == wanted) & (lane < WIN * (2 * WIN - 1)), 1.0, 0.0).astype(jnp.bfloat16)


def split_three(value):
    high = value.astype(jnp.bfloat16)
    rest = value - high.astype(jnp.float32)
    middle = rest.astype(jnp.bfloat16)
    low = (rest - middle.astype(jnp.float32)).astype(jnp.bfloat16)
    return high, middle, low


def slots(rows):
    size = rows.shape[0] // HEADS
    blank = jnp.zeros((SLOT - size, rows.shape[1]), rows.dtype)
    pieces = []
    for head in range(HEADS):
        pieces += [rows[head * size : (head + 1) * size], blank]
    return jnp.concatenate(pieces, 0)


def unslot(rows, size):
    return jnp.concatenate([rows[head * SLOT : head * SLOT + size] for head in range(HEADS)], 0)


def prepare_kernel(weight_ref, offsets_ref, proj_ref, table_ref, bias_ref, tok_ref, chan_ref, proj_slots_ref, parts_ref):
    channels = weight_ref.shape[0]
    for part in range(3):
        weight = weight_ref[:, part * channels : (part + 1) * channels].astype(jnp.float32)
        parts_ref[part] = weight.astype(jnp.bfloat16)
        high, middle, low = split_three(offsets_ref[:, part * channels : (part + 1) * channels])
        full = jnp.concatenate(
            [
                weight,
                high.astype(jnp.float32),
                middle.astype(jnp.float32),
                low.astype(jnp.float32),
                jnp.zeros((256 - channels - 3, channels), jnp.float32),
            ],
            0,
        )
        turned = slots(full.T)
        chan_ref[part] = turned.astype(jnp.bfloat16)
        if part == 0:
            tok_ref[part, :, 0:channels] = full.astype(jnp.bfloat16)
            tok_ref[part, :, channels:] = jnp.zeros((256, HEADS * SLOT - channels), jnp.bfloat16)
        else:
            tok_ref[part] = turned.T.astype(jnp.bfloat16)
    proj_slots_ref[...] = slots(proj_ref[...].astype(jnp.float32)).astype(jnp.bfloat16)
    pieces = split_three(table_ref[...])
    lane = iota((8, LANES), 1)
    for cj in range(WIN):
        hits = table_hits(cj, False)
        spread = nn(pieces[0], hits) + nn(pieces[1], hits) + nn(pieces[2], hits)
        for rj in range(WIN):
            by = WIN * (WIN - 1 - rj)
            moved = spread if by == 0 else pltpu.roll(spread, LANES - by, 1)
            both = jnp.where(lane < SPAN, moved, pltpu.roll(moved, SPAN, 1))
            for head in range(HEADS):
                bias_ref[head, rj * WIN + cj : rj * WIN + cj + 1, :] = both[head : head + 1, :]


def main_kernel(
    tokens_ref,
    grad_ref,
    region_ref,
    x_below_ref,
    g_below_ref,
    right_ref,
    corner_ref,
    gain_ref,
    offset_ref,
    bias_ref,
    tok_ref,
    chan_ref,
    proj_ref,
    proj_slots_ref,
    core_ref,
    keep_ref,
    send_ref,
    d_qkv_s,
    unit_s,
    inv_s,
    g_s,
    turn_s,
    x_s,
    id_s,
    unit_low_s,
    normed_s,
    grad_s,
    q_tok_s,
    k_tok_s,
    v_tok_s,
    da_tok_s,
    q_chan_s,
    k_chan_s,
    v_chan_s,
    da_chan_s,
    attended_s,
    score_s,
    pack_s,
):
    rows, cols, channels = tokens_ref.shape
    head_size = channels // HEADS
    scale = head_size ** (-0.5)
    count = rows * cols
    wins = cols // WIN
    f32 = jnp.float32
    bf16 = jnp.bfloat16

    x_s[:, :, :, LANES:] = jnp.zeros(x_s.shape[:3] + (LANES,), f32)
    turn_s[0:channels] = x_below_ref[...].astype(f32)
    turn_s[channels:] = g_below_ref[...].astype(f32)
    ids = region_ref[...].astype(f32).T
    at_id = slice(2 * channels, 2 * channels + 1)
    col_part = ids[:, 0:1] - 4.0 * jnp.floor(ids[:, 0:1] * 0.25)
    for r in range(rows):
        if r < rows - SHIFT:
            x_body = tokens_ref[r + SHIFT].astype(f32)
            g_body = grad_ref[r + SHIFT].astype(f32)
            side = right_ref[r].astype(f32)
            id_body = ids[:, r + SHIFT : r + SHIFT + 1]
        else:
            here = r - (rows - SHIFT)
            body = turn_s[:, here, :].T
            x_body = body[:, 0:channels]
            g_body = body[:, channels : 2 * channels]
            side = corner_ref[here].astype(f32)
            id_body = col_part + 4.0 * jnp.floor(side[0:1, at_id] * 0.25)
        x_row = jnp.concatenate([x_body[SHIFT:], side[:, 0:channels]], 0)
        g_row = jnp.concatenate([g_body[SHIFT:], side[:, channels : 2 * channels]], 0)
        id_row = jnp.concatenate([id_body[SHIFT:], side[:, at_id]], 0)
        x_s[:, r, :, 0:channels] = x_row.reshape(wins, WIN, channels)
        g_s[:, r, :, :] = g_row.reshape(wins, WIN, channels)
        id_s[:, r, :, :] = id_row.reshape(wins, WIN, 1)

    x = x_s[...].reshape(count, 2 * LANES)
    lane = iota((1, 2 * LANES), 1)
    inside = lane < channels
    center = jnp.sum(x, -1, keepdims=True) * (1.0 / channels)
    away = jnp.where(inside, x - center, 0.0)
    variance = jnp.sum(away * away, -1, keepdims=True) * (1.0 / channels)
    inv_std = lax.rsqrt(variance + 1e-05)
    unit = away * inv_std
    unit_s[...] = unit
    inv_s[...] = inv_std
    unit_low_s[...] = jnp.where(lane == channels, 1.0, unit).astype(bf16)
    normed_s[...] = jnp.where(
        (lane >= channels) & (lane < channels + 3), 1.0, unit * gain_ref[...] + offset_ref[...]
    ).astype(bf16)
    grad_s[...] = g_s[...].reshape(count, channels).astype(bf16)

    normed = normed_s[...]
    q_tok_s[...] = (nn(normed, tok_ref[0, :, 0:channels]) * scale).astype(bf16)
    k_tok_s[...] = nn(normed, tok_ref[1]).astype(bf16)
    v_tok_s[...] = nn(normed, tok_ref[2]).astype(bf16)
    da_tok_s[...] = nt(grad_s[...], proj_ref[...]).astype(bf16)
    q_chan_s[...] = (nt(chan_ref[0], normed) * scale).astype(bf16)
    k_chan_s[...] = nt(chan_ref[1], normed).astype(bf16)
    v_chan_s[...] = nt(chan_ref[2], normed).astype(bf16)
    da_chan_s[...] = nt(proj_slots_ref[...], grad_s[...]).astype(bf16)

    score_s[...] = jnp.zeros(score_s.shape, f32)
    first = iota((1, LANES), 1) < SPAN
    first_low = jnp.where(first, 1.0, 0.0).astype(bf16)
    second_low = jnp.where(first, 0.0, 1.0).astype(bf16)
    head_of = iota((1, channels), 1) // head_size
    id_lane = iota((1, LANES), 1).astype(f32)

    def pack(square):
        return jnp.where(first, square[0:SPAN], square[SPAN:])

    def spread(packed):
        low = packed.astype(bf16)
        return jnp.concatenate([low * first_low, low * second_low], 0)

    def in_blocks(chan):
        blank = jnp.zeros((SLOT, LANES), bf16)
        lines = []
        for head in range(HEADS):
            line = [blank] * HEADS
            line[head] = chan[head * SLOT : (head + 1) * SLOT]
            lines.append(jnp.concatenate(line, 1))
        return jnp.concatenate(lines, 0)

    def by_head(tok):
        return jnp.concatenate(
            [jnp.where(head_of == head, tok, jnp.zeros_like(tok)) for head in range(HEADS)], 0
        )

    def pair_step(pair, carry):
        at = pl.ds(pl.multiple_of(pair * LANES, LANES), LANES)
        hot = jnp.where(id_s[pl.ds(pair * 2, 2)].reshape(LANES, 1) == id_lane, 1.0, 0.0).astype(bf16)
        match = pack(nt(hot, hot)) > 0.5
        k_chan = k_chan_s[:, at]
        v_chan = v_chan_s[:, at]
        scores = nn(k_tok_s[at, :], in_blocks(q_chan_s[:, at]))
        d_prob = nn(v_tok_s[at, :], in_blocks(da_chan_s[:, at]))
        attended = []
        d_query = []
        probs = []
        d_scores = []
        for head in range(HEADS):
            here = slice(head * LANES, (head + 1) * LANES)
            band = slice(head * SLOT, (head + 1) * SLOT)
            score = jnp.where(match, pack(scores[:, here]) + bias_ref[head], MASKED)
            power = jnp.exp(score - jnp.max(score, 0, keepdims=True))
            prob = power * (1.0 / jnp.sum(power, 0, keepdims=True))
            gradient = pack(d_prob[:, here])
            d_score = prob * (gradient - jnp.sum(prob * gradient, 0, keepdims=True))
            score_s[head] += d_score
            prob_low = spread(prob)
            d_low = spread(d_score)
            attended.append(nn(v_chan[band], prob_low))
            d_query.append(nn(k_chan[band], d_low) * scale)
            probs.append(prob_low)
            d_scores.append(d_low)
        attended_s[:, at] = jnp.concatenate(attended, 0).astype(bf16)
        d_query = jnp.concatenate([piece[0:head_size] for piece in d_query], 0)
        d_qkv_s[0, at, :] = d_query.T.astype(bf16)
        d_qkv_s[1, at, :] = nn(jnp.concatenate(d_scores, 1), by_head(q_tok_s[at, :])).astype(bf16)
        d_qkv_s[2, at, :] = nn(jnp.concatenate(probs, 1), by_head(da_tok_s[at, :])).astype(bf16)
        return carry

    lax.fori_loop(0, count // LANES, pair_step, 0, unroll=True)

    unit_turned = unit_low_s[...].T[0:ROWS]
    rest = channels - LANES
    pieces = [nn(unit_turned, d_qkv_s[part]) for part in range(3)]
    d_proj = nn(attended_s[...], grad_s[...])
    pieces.append(
        jnp.concatenate([unslot(d_proj, head_size), jnp.zeros((ROWS - channels, channels), f32)], 0)
    )
    pack_s[...] = jnp.zeros(pack_s.shape, f32)
    for at, piece in enumerate(pieces):
        pack_s[at * ROWS : (at + 1) * ROWS, :] = piece[:, 0:LANES]
        low = (4 + at // 2) * ROWS
        side = (at % 2) * SPAN
        pack_s[low : low + ROWS, side : side + rest] = piece[:, LANES:]
    lines = []
    for head in range(HEADS):
        both = score_s[head]
        both = jnp.where(first, both + pltpu.roll(both, SPAN, 1), 0.0)
        line = both[(WIN - 1) * WIN :]
        for rj in range(WIN - 1):
            line += pltpu.roll(both[rj * WIN : (rj + 1) * WIN], WIN * (WIN - 1 - rj), 1)
        lines.append(line)
    lines = jnp.concatenate(lines, 0)
    high = lines.astype(bf16)
    low = (lines - high.astype(f32)).astype(bf16)
    cj_of = iota((HEADS * WIN, 1), 0) % WIN
    table = jnp.zeros((HEADS * WIN, 2 * LANES), f32)
    for cj in range(WIN):
        hits = table_hits(cj, True)
        table += jnp.where(cj_of == cj, nn(high, hits) + nn(low, hits), 0.0)
    table = table.reshape(HEADS, WIN, 2 * LANES).sum(1)
    pack_s[6 * ROWS : 6 * ROWS + HEADS, :] = table[:, 0:LANES]
    pack_s[6 * ROWS + 8 : 6 * ROWS + 8 + HEADS, :] = table[:, LANES:]
    half = keep_ref.shape[0]
    low_half = pack_s[0:half, :].astype(bf16)
    high_half = pack_s[half:, :].astype(bf16)
    lower = core_ref[0] == 0
    keep_ref[...] = jnp.where(lower, low_half, high_half)
    send_ref[...] = jnp.where(lower, high_half, low_half)


def input_kernel(d_qkv_ref, unit_ref, inv_ref, g_ref, gain_ref, parts_ref, framed_ref, turn_s):
    wins, rows, _, channels = g_ref.shape
    cols = wins * WIN
    f32 = jnp.float32
    d_normed = sum(nt(d_qkv_ref[part], parts_ref[part]) for part in range(3))
    scaled = d_normed * gain_ref[:, 0:channels]
    unit = unit_ref[:, 0:channels]
    mean_one = jnp.sum(scaled, -1, keepdims=True) * (1.0 / channels)
    mean_two = jnp.sum(scaled * unit, -1, keepdims=True) * (1.0 / channels)
    d_input = inv_ref[...] * (scaled - mean_one - unit * mean_two)
    done = g_ref[...] + d_input.reshape(g_ref.shape)
    for r in range(rows):
        row = done[:, r].reshape(cols, channels)
        row = jnp.concatenate([row[cols - SHIFT :], row[: cols - SHIFT]], 0)
        turn_s[:, r, :] = row.T
    framed_ref[...] = turn_s[...].astype(framed_ref.dtype)


def finish_kernel(out_scale, mine_ref, other_ref, core_ref, weight_ref, gain_ref, offset_ref, d_weight_ref, d_bias_ref, d_proj_ref, d_table_ref, d_gain_ref, d_offset_ref):
    channels = weight_ref.shape[0]
    f32 = jnp.float32
    rest = channels - LANES
    mine = mine_ref[...].astype(f32)
    other = other_ref[...].astype(f32)
    here = core_ref[0] == 0
    low = jnp.where(here, mine, other)
    high = jnp.where(here, other, mine)
    both = jnp.concatenate([low, high], 0) * out_scale
    pieces = []
    for at in range(4):
        row = (4 + at // 2) * ROWS
        side = (at % 2) * SPAN
        pieces.append(
            jnp.concatenate(
                [both[at * ROWS : (at + 1) * ROWS, :], both[row : row + ROWS, side : side + rest]], 1
            )
        )
    gain = gain_ref[...].T
    offset = offset_ref[...].T
    d_gain = jnp.zeros((channels, 1), f32)
    d_offset = jnp.zeros((channels, 1), f32)
    biases = []
    for part in range(3):
        across = slice(part * channels, (part + 1) * channels)
        unit = pieces[part][0:channels]
        bias = pieces[part][channels : channels + 1]
        weight = weight_ref[:, across].astype(f32)
        d_weight_ref[:, across] = gain * unit + offset * bias
        biases.append(bias)
        d_gain += jnp.sum(weight * unit, -1, keepdims=True)
        d_offset += jnp.sum(weight * bias, -1, keepdims=True)
    d_bias_ref[...] = jnp.concatenate(biases, 1).reshape(d_bias_ref.shape)
    d_gain_ref[...] = d_gain.T.reshape(channels)
    d_offset_ref[...] = d_offset.T.reshape(channels)
    d_proj_ref[...] = pieces[3][0:channels]
    table = jnp.concatenate([both[6 * ROWS : 6 * ROWS + 8], both[6 * ROWS + 8 :]], 1)
    d_table_ref[...] = table[0:HEADS, 0 : d_table_ref.shape[1]]


def whole(memory_space=pltpu.VMEM):
    return pl.BlockSpec(memory_space=memory_space)


def from_behind(shard, axis, by):
    count = lax.axis_size(axis)
    return lax.ppermute(shard, axis, [(i, (i + by) % count) for i in range(count)])


def diagonal(shard, by):
    rows, cols = lax.axis_size("row"), lax.axis_size("col")
    pairs = [
        (r * cols + c, ((r + by) % rows) * cols + (c + by) % cols) for r in range(rows) for c in range(cols)
    ]
    return lax.ppermute(shard, ("row", "col"), pairs)


def exchange_steps():
    rows, cols = lax.axis_size("row"), lax.axis_size("col")
    steps = [1 << bit for bit in range((rows - 1).bit_length())]
    for at in range(len(steps)):
        yield [
            (r * cols + c, (r ^ steps[(at + c) % len(steps)]) * cols + c) for r in range(rows) for c in range(cols)
        ]


def add(left, right):
    return (left.astype(jnp.float32) + right.astype(jnp.float32)).astype(jnp.bfloat16)


def on_device(
    tokens, grad_out, regions, ln_gain, ln_offset, qkv_weight, qkv_bias, proj_weight, bias_table
):
    rows, cols, channels = tokens.shape
    f32, bf16 = jnp.float32, jnp.bfloat16
    count = rows * cols
    params = pltpu.CompilerParams(vmem_limit_bytes=VMEM_LIMIT)

    x_turned = tokens.transpose(2, 0, 1)
    g_turned = grad_out.transpose(2, 0, 1)
    core = lax.axis_index("col").astype(jnp.int32).reshape(1)

    x_below = from_behind(x_turned[:, :SHIFT], "row", -1)
    g_below = from_behind(g_turned[:, :SHIFT], "row", -1)
    near_tokens, near_grad, near_ids = tokens, grad_out, regions

    def border(row_slice):
        return jnp.concatenate(
            [
                near_tokens[row_slice, :SHIFT],
                near_grad[row_slice, :SHIFT],
                near_ids[row_slice, :SHIFT, None].astype(bf16),
            ],
            -1,
        )

    right = from_behind(border(slice(SHIFT, None)), "col", -1)
    corner = diagonal(border(slice(0, SHIFT)), -1)

    table = jnp.pad(bias_table.T, ((0, 8 - HEADS), (0, 2 * LANES - bias_table.shape[0])))
    wide = HEADS * SLOT
    bias, tok, chan, proj_slots, parts = pl.pallas_call(
        prepare_kernel,
        name="prepare",
        out_shape=(
            jax.ShapeDtypeStruct((HEADS, SPAN, LANES), f32),
            jax.ShapeDtypeStruct((3, 2 * LANES, wide), bf16),
            jax.ShapeDtypeStruct((3, wide, 2 * LANES), bf16),
            jax.ShapeDtypeStruct((wide, channels), bf16),
            jax.ShapeDtypeStruct((3, channels, channels), bf16),
        ),
        in_specs=[whole()] * 4,
        out_specs=(whole(),) * 5,
        compiler_params=params,
    )(qkv_weight, qkv_bias[None], proj_weight, table)

    gain = jnp.pad(ln_gain, (0, 2 * LANES - channels))[None]
    offset = jnp.pad(ln_offset, (0, 2 * LANES - channels))[None]
    wins = cols // WIN
    keep, send, *saved = pl.pallas_call(
        main_kernel,
        name="window_attention_backward",
        out_shape=(
            jax.ShapeDtypeStruct((BUFFER_ROWS // 2, LANES), bf16),
            jax.ShapeDtypeStruct((BUFFER_ROWS // 2, LANES), bf16),
            jax.ShapeDtypeStruct((3, count, channels), bf16),
            jax.ShapeDtypeStruct((count, 2 * LANES), f32),
            jax.ShapeDtypeStruct((count, 1), f32),
            jax.ShapeDtypeStruct((wins, rows, WIN, channels), f32),
        ),
        in_specs=[whole()] * 14 + [whole(pltpu.SMEM)],
        out_specs=(whole(),) * 6,
        scratch_shapes=[
            pltpu.VMEM((2 * channels, SHIFT, cols), f32),
            pltpu.VMEM((wins, rows, WIN, 2 * LANES), f32),
            pltpu.VMEM((wins, rows, WIN, 1), f32),
            pltpu.VMEM((count, 2 * LANES), bf16),
            pltpu.VMEM((count, 2 * LANES), bf16),
            pltpu.VMEM((count, channels), bf16),
            pltpu.VMEM((count, channels), bf16),
            pltpu.VMEM((count, wide), bf16),
            pltpu.VMEM((count, wide), bf16),
            pltpu.VMEM((count, channels), bf16),
            pltpu.VMEM((wide, count), bf16),
            pltpu.VMEM((wide, count), bf16),
            pltpu.VMEM((wide, count), bf16),
            pltpu.VMEM((wide, count), bf16),
            pltpu.VMEM((wide, count), bf16),
            pltpu.VMEM((HEADS, SPAN, LANES), f32),
            pltpu.VMEM((BUFFER_ROWS, LANES), f32),
        ],
        compiler_params=params,
    )(
        near_tokens, near_grad, near_ids, x_below, g_below, right, corner, gain, offset, bias, tok, chan, proj_weight, proj_slots, core
    )

    mine = add(keep, from_behind(send, "col", 1))
    mine, *saved = lax.optimization_barrier((mine, *saved))
    (framed,) = pl.pallas_call(
        input_kernel,
        name="input_backward",
        out_shape=(jax.ShapeDtypeStruct((channels, rows, cols), bf16),),
        in_specs=[whole()] * 6,
        out_specs=(whole(),),
        scratch_shapes=[pltpu.VMEM((channels, rows, cols), f32)],
        compiler_params=params,
        cost_estimate=pl.CostEstimate(flops=10**9, bytes_accessed=0, transcendentals=0),
    )(*saved, gain, parts)
    steps = list(exchange_steps())
    for at, pairs in enumerate(steps):
        if at == min(1, len(steps) - 1):
            mine, framed = lax.optimization_barrier((mine, framed))
            beside = from_behind(framed, "col", 1)
            framed = jnp.where(jnp.arange(cols) < SHIFT, beside, framed)
        if at == min(2, len(steps) - 1):
            mine, framed = lax.optimization_barrier((mine, framed))
            above = from_behind(framed[:, rows - SHIFT :], "row", 1)
        mine = add(mine, lax.ppermute(mine, ("row", "col"), pairs))
    d_tokens = jnp.concatenate([above, framed[:, : rows - SHIFT]], 1).transpose(1, 2, 0)
    other = from_behind(mine, "col", 1)

    total_tokens = count * lax.axis_size("row") * lax.axis_size("col")
    d_weight, d_bias, d_proj, d_table, d_gain, d_offset = pl.pallas_call(
        functools.partial(finish_kernel, total_tokens ** (-0.5)),
        name="finish",
        out_shape=(
            jax.ShapeDtypeStruct(qkv_weight.shape, f32),
            jax.ShapeDtypeStruct(qkv_bias.shape, f32),
            jax.ShapeDtypeStruct(proj_weight.shape, f32),
            jax.ShapeDtypeStruct(bias_table.shape[::-1], f32),
            jax.ShapeDtypeStruct(ln_gain.shape, f32),
            jax.ShapeDtypeStruct(ln_offset.shape, f32),
        ),
        in_specs=[whole(), whole(), whole(pltpu.SMEM), whole(), whole(), whole()],
        out_specs=(whole(),) * 6,
        compiler_params=params,
    )(mine, other, core, qkv_weight, ln_gain[None], ln_offset[None])
    return (d_tokens, d_weight, d_bias, d_proj, d_table.T, d_gain, d_offset)


def solution(mesh):
    placed = (
        P(("grp", "row"), "col", None),
        P(("grp", "row"), "col", None),
        P(("grp", "row"), "col"),
        P(),
        P(),
        P(),
        P(),
        P(),
        P(),
    )
    return jax.shard_map(
        on_device,
        mesh=mesh,
        in_specs=placed,
        out_specs=(
            P(("grp", "row"), "col", None),
            P("grp", None),
            P("grp"),
            P("grp", None),
            P("grp", None),
            P("grp"),
            P("grp"),
        ),
        check_vma=False,
    )
```

```python
import functools

import jax
import jax.numpy as jnp
from jax import lax
from jax.experimental import pallas as pl
from jax.experimental.pallas import tpu as pltpu
from jax.sharding import PartitionSpec as P

HEADS = 6
WIN = 8
SHIFT = 4
SPAN = WIN * WIN
MASKED = -10000.0
LANES = 128
SLOT = 32
ROWS = 184
TABLE_ROWS = 16
BUFFER_ROWS = 6 * ROWS + TABLE_ROWS

VMEM_LIMIT = 32 * 1024 * 1024


def nn(left, right):
    return lax.dot_general(left, right, (((1,), (0,)), ((), ())), preferred_element_type=jnp.float32)


def nt(left, right):
    return lax.dot_general(left, right, (((1,), (1,)), ((), ())), preferred_element_type=jnp.float32)


def iota(shape, dim):
    return lax.broadcasted_iota(jnp.int32, shape, dim)


def table_hits(cj, lanes_first):
    shape = (LANES, 2 * LANES) if lanes_first else (2 * LANES, LANES)
    lane = iota(shape, 0 if lanes_first else 1)
    entry = iota(shape, 1 if lanes_first else 0)
    wanted = (lane // WIN) * (2 * WIN - 1) + lane % WIN + (WIN - 1) - cj
    return jnp.where((entry == wanted) & (lane < WIN * (2 * WIN - 1)), 1.0, 0.0).astype(jnp.bfloat16)


def split_three(value):
    high = value.astype(jnp.bfloat16)
    rest = value - high.astype(jnp.float32)
    middle = rest.astype(jnp.bfloat16)
    low = (rest - middle.astype(jnp.float32)).astype(jnp.bfloat16)
    return high, middle, low


def slots(rows):
    size = rows.shape[0] // HEADS
    blank = jnp.zeros((SLOT - size, rows.shape[1]), rows.dtype)
    pieces = []
    for head in range(HEADS):
        pieces += [rows[head * size : (head + 1) * size], blank]
    return jnp.concatenate(pieces, 0)


def unslot(rows, size):
    return jnp.concatenate([rows[head * SLOT : head * SLOT + size] for head in range(HEADS)], 0)


def prepare_kernel(weight_ref, offsets_ref, proj_ref, table_ref, bias_ref, tok_ref, chan_ref, proj_slots_ref, parts_ref):
    channels = weight_ref.shape[0]
    for part in range(3):
        weight = weight_ref[:, part * channels : (part + 1) * channels].astype(jnp.float32)
        parts_ref[part] = weight.astype(jnp.bfloat16)
        high, middle, low = split_three(offsets_ref[:, part * channels : (part + 1) * channels])
        full = jnp.concatenate(
            [
                weight,
                high.astype(jnp.float32),
                middle.astype(jnp.float32),
                low.astype(jnp.float32),
                jnp.zeros((256 - channels - 3, channels), jnp.float32),
            ],
            0,
        )
        turned = slots(full.T)
        chan_ref[part] = turned.astype(jnp.bfloat16)
        if part == 0:
            tok_ref[part, :, 0:channels] = full.astype(jnp.bfloat16)
            tok_ref[part, :, channels:] = jnp.zeros((256, HEADS * SLOT - channels), jnp.bfloat16)
        else:
            tok_ref[part] = turned.T.astype(jnp.bfloat16)
    proj_slots_ref[...] = slots(proj_ref[...].astype(jnp.float32)).astype(jnp.bfloat16)
    pieces = split_three(table_ref[...])
    lane = iota((8, LANES), 1)
    for cj in range(WIN):
        hits = table_hits(cj, False)
        spread = nn(pieces[0], hits) + nn(pieces[1], hits) + nn(pieces[2], hits)
        for rj in range(WIN):
            by = WIN * (WIN - 1 - rj)
            moved = spread if by == 0 else pltpu.roll(spread, LANES - by, 1)
            both = jnp.where(lane < SPAN, moved, pltpu.roll(moved, SPAN, 1))
            for head in range(HEADS):
                bias_ref[head, rj * WIN + cj : rj * WIN + cj + 1, :] = both[head : head + 1, :]


def normalize(x, channels, gain_ref, offset_ref):
    f32, bf16 = jnp.float32, jnp.bfloat16
    lane = iota((1, 2 * LANES), 1)
    center = jnp.sum(x, -1, keepdims=True) * (1.0 / channels)
    away = jnp.where(lane < channels, x - center, 0.0)
    variance = jnp.sum(away * away, -1, keepdims=True) * (1.0 / channels)
    inv_std = lax.rsqrt(variance + 1e-05)
    unit = away * inv_std
    unit_low = jnp.where(lane == channels, 1.0, unit).astype(bf16)
    normed = jnp.where(
        (lane >= channels) & (lane < channels + 3), 1.0, unit * gain_ref[...] + offset_ref[...]
    ).astype(bf16)
    return unit, inv_std, unit_low, normed


def project(normed, channels, tok_ref, chan_ref):
    bf16 = jnp.bfloat16
    scale = (channels // HEADS) ** (-0.5)
    return (
        (nn(normed, tok_ref[0, :, 0:channels]) * scale).astype(bf16),
        nn(normed, tok_ref[1]).astype(bf16),
        nn(normed, tok_ref[2]).astype(bf16),
        (nt(chan_ref[0], normed) * scale).astype(bf16),
        nt(chan_ref[1], normed).astype(bf16),
        nt(chan_ref[2], normed).astype(bf16),
    )


def project_kernel(
    tokens_ref,
    x_below_ref,
    right_ref,
    gain_ref,
    offset_ref,
    tok_ref,
    chan_ref,
    unit_ref,
    inv_ref,
    unit_turned_ref,
    q_tok_ref,
    k_tok_ref,
    v_tok_ref,
    q_chan_ref,
    k_chan_ref,
    v_chan_ref,
    x_last_ref,
    turn_s,
    x_s,
):
    rows, cols, channels = tokens_ref.shape
    wins = cols // WIN
    f32 = jnp.float32
    x_s[:, :, :, LANES:] = jnp.zeros(x_s.shape[:3] + (LANES,), f32)
    turn_s[...] = x_below_ref[...].astype(f32)
    for r in range(rows):
        if r < rows - SHIFT:
            body = tokens_ref[r + SHIFT].astype(f32)
            side = right_ref[r].astype(f32)[:, 0:channels]
        else:
            body = turn_s[:, r - (rows - SHIFT), :].T
            side = jnp.zeros((SHIFT, channels), f32)
        row = jnp.concatenate([body[SHIFT:], side], 0)
        x_s[:, r, :, 0:channels] = row.reshape(wins, WIN, channels)
    x_last_ref[...] = x_s[wins - 2 :]
    unit, inv_std, unit_low, normed = normalize(
        x_s[...].reshape(rows * cols, 2 * LANES), channels, gain_ref, offset_ref
    )
    unit_ref[...] = unit
    inv_ref[...] = inv_std
    unit_turned_ref[...] = unit_low.T[0 : unit_turned_ref.shape[0]]
    results = project(normed, channels, tok_ref, chan_ref)
    for target, value in zip(
        (q_tok_ref, k_tok_ref, v_tok_ref, q_chan_ref, k_chan_ref, v_chan_ref), results
    ):
        target[...] = value


def main_kernel(
    grad_ref,
    region_ref,
    g_below_ref,
    right_ref,
    corner_ref,
    gain_ref,
    offset_ref,
    bias_ref,
    tok_ref,
    chan_ref,
    proj_ref,
    proj_slots_ref,
    unit_turned_ref,
    q_tok_ref,
    k_tok_ref,
    v_tok_ref,
    q_chan_ref,
    k_chan_ref,
    v_chan_ref,
    x_last_ref,
    core_ref,
    keep_ref,
    send_ref,
    d_qkv_s,
    g_s,
    unit_last_ref,
    inv_last_ref,
    turn_s,
    x_last_s,
    id_s,
    grad_s,
    da_tok_s,
    da_chan_s,
    attended_s,
    score_s,
    pack_s,
):
    rows, cols, channels = grad_ref.shape
    head_size = channels // HEADS
    scale = head_size ** (-0.5)
    count = rows * cols
    wins = cols // WIN
    f32 = jnp.float32
    bf16 = jnp.bfloat16

    turn_s[...] = g_below_ref[...].astype(f32)
    x_last_s[...] = x_last_ref[...]
    ids = region_ref[...].astype(f32).T
    at_id = slice(2 * channels, 2 * channels + 1)
    col_part = ids[:, 0:1] - 4.0 * jnp.floor(ids[:, 0:1] * 0.25)
    for r in range(rows):
        if r < rows - SHIFT:
            g_body = grad_ref[r + SHIFT].astype(f32)
            side = right_ref[r].astype(f32)
            id_body = ids[:, r + SHIFT : r + SHIFT + 1]
        else:
            here = r - (rows - SHIFT)
            g_body = turn_s[:, here, :].T
            side = corner_ref[here].astype(f32)
            id_body = col_part + 4.0 * jnp.floor(side[0:1, at_id] * 0.25)
            x_last_s[1, r, SHIFT:, 0:channels] = side[:, 0:channels]
        g_row = jnp.concatenate([g_body[SHIFT:], side[:, channels : 2 * channels]], 0)
        id_row = jnp.concatenate([id_body[SHIFT:], side[:, at_id]], 0)
        g_s[:, r, :, :] = g_row.reshape(wins, WIN, channels)
        id_s[:, r, :, :] = id_row.reshape(wins, WIN, 1)
    grad_s[...] = g_s[...].reshape(count, channels).astype(bf16)

    unit_last, inv_last, unit_low, normed = normalize(
        x_last_s[...].reshape(LANES, 2 * LANES), channels, gain_ref, offset_ref
    )
    unit_last_ref[...] = unit_last
    inv_last_ref[...] = inv_last
    last = project(normed, channels, tok_ref, chan_ref)
    da_tok_s[...] = nt(grad_s[...], proj_ref[...]).astype(bf16)
    da_chan_s[...] = nt(proj_slots_ref[...], grad_s[...]).astype(bf16)

    score_s[...] = jnp.zeros(score_s.shape, f32)
    first = iota((1, LANES), 1) < SPAN
    first_low = jnp.where(first, 1.0, 0.0).astype(bf16)
    second_low = jnp.where(first, 0.0, 1.0).astype(bf16)
    head_of = iota((1, channels), 1) // head_size
    id_lane = iota((1, LANES), 1).astype(f32)

    def pack(square):
        return jnp.where(first, square[0:SPAN], square[SPAN:])

    def spread(packed):
        low = packed.astype(bf16)
        return jnp.concatenate([low * first_low, low * second_low], 0)

    def in_blocks(chan):
        blank = jnp.zeros((SLOT, LANES), bf16)
        lines = []
        for head in range(HEADS):
            line = [blank] * HEADS
            line[head] = chan[head * SLOT : (head + 1) * SLOT]
            lines.append(jnp.concatenate(line, 1))
        return jnp.concatenate(lines, 0)

    def by_head(tok):
        return jnp.concatenate(
            [jnp.where(head_of == head, tok, jnp.zeros_like(tok)) for head in range(HEADS)], 0
        )

    for pair in range(count // LANES):
        at = slice(pair * LANES, (pair + 1) * LANES)
        if (pair + 1) * LANES == count:
            q_tok, k_tok, v_tok, q_chan, k_chan, v_chan = last
        else:
            q_tok, k_tok, v_tok = q_tok_ref[at, :], k_tok_ref[at, :], v_tok_ref[at, :]
            q_chan, k_chan, v_chan = q_chan_ref[:, at], k_chan_ref[:, at], v_chan_ref[:, at]
        hot = jnp.where(id_s[pair * 2 : pair * 2 + 2].reshape(LANES, 1) == id_lane, 1.0, 0.0).astype(bf16)
        match = pack(nt(hot, hot)) > 0.5
        scores = nn(k_tok, in_blocks(q_chan))
        d_prob = nn(v_tok, in_blocks(da_chan_s[:, at]))
        attended = []
        d_query = []
        probs = []
        d_scores = []
        for head in range(HEADS):
            here = slice(head * LANES, (head + 1) * LANES)
            band = slice(head * SLOT, (head + 1) * SLOT)
            score = jnp.where(match, pack(scores[:, here]) + bias_ref[head], MASKED)
            power = jnp.exp(score - jnp.max(score, 0, keepdims=True))
            prob = power * (1.0 / jnp.sum(power, 0, keepdims=True))
            gradient = pack(d_prob[:, here])
            d_score = prob * (gradient - jnp.sum(prob * gradient, 0, keepdims=True))
            score_s[head] += d_score
            prob_low = spread(prob)
            d_low = spread(d_score)
            attended.append(nn(v_chan[band], prob_low))
            d_query.append(nn(k_chan[band], d_low) * scale)
            probs.append(prob_low)
            d_scores.append(d_low)
        attended_s[:, at] = jnp.concatenate(attended, 0).astype(bf16)
        d_query = jnp.concatenate([piece[0:head_size] for piece in d_query], 0)
        d_qkv_s[0, at, :] = d_query.T.astype(bf16)
        d_qkv_s[1, at, :] = nn(jnp.concatenate(d_scores, 1), by_head(q_tok)).astype(bf16)
        d_qkv_s[2, at, :] = nn(jnp.concatenate(probs, 1), by_head(da_tok_s[at, :])).astype(bf16)

    unit_turned = jnp.concatenate([unit_turned_ref[:, : count - LANES], unit_low.T[0 : unit_turned_ref.shape[0]]], 1)
    rest = channels - LANES
    pieces = [nn(unit_turned, d_qkv_s[part])[0:ROWS] for part in range(3)]
    d_proj = nn(attended_s[...], grad_s[...])
    pieces.append(
        jnp.concatenate([unslot(d_proj, head_size), jnp.zeros((ROWS - channels, channels), f32)], 0)
    )
    pack_s[...] = jnp.zeros(pack_s.shape, f32)
    for at, piece in enumerate(pieces):
        pack_s[at * ROWS : (at + 1) * ROWS, :] = piece[:, 0:LANES]
        low = (4 + at // 2) * ROWS
        side = (at % 2) * SPAN
        pack_s[low : low + ROWS, side : side + rest] = piece[:, LANES:]
    lines = []
    for head in range(HEADS):
        both = score_s[head]
        both = jnp.where(first, both + pltpu.roll(both, SPAN, 1), 0.0)
        line = both[(WIN - 1) * WIN :]
        for rj in range(WIN - 1):
            line += pltpu.roll(both[rj * WIN : (rj + 1) * WIN], WIN * (WIN - 1 - rj), 1)
        lines.append(line)
    lines = jnp.concatenate(lines, 0)
    high = lines.astype(bf16)
    low = (lines - high.astype(f32)).astype(bf16)
    cj_of = iota((HEADS * WIN, 1), 0) % WIN
    table = jnp.zeros((HEADS * WIN, 2 * LANES), f32)
    for cj in range(WIN):
        hits = table_hits(cj, True)
        table += jnp.where(cj_of == cj, nn(high, hits) + nn(low, hits), 0.0)
    table = table.reshape(HEADS, WIN, 2 * LANES).sum(1)
    pack_s[6 * ROWS : 6 * ROWS + HEADS, :] = table[:, 0:LANES]
    pack_s[6 * ROWS + 8 : 6 * ROWS + 8 + HEADS, :] = table[:, LANES:]
    half = keep_ref.shape[0]
    low_half = pack_s[0:half, :].astype(bf16)
    high_half = pack_s[half:, :].astype(bf16)
    lower = core_ref[0] == 0
    keep_ref[...] = jnp.where(lower, low_half, high_half)
    send_ref[...] = jnp.where(lower, high_half, low_half)


def input_kernel(
    d_qkv_ref, g_ref, unit_last_ref, inv_last_ref, unit_ref, inv_ref, gain_ref, parts_ref, framed_ref, turn_s
):
    wins, rows, _, channels = g_ref.shape
    cols = wins * WIN
    f32 = jnp.float32
    d_normed = sum(nt(d_qkv_ref[part], parts_ref[part]) for part in range(3))
    scaled = d_normed * gain_ref[:, 0:channels]
    unit = jnp.concatenate([unit_ref[:-LANES, 0:channels], unit_last_ref[:, 0:channels]], 0)
    inv_std = jnp.concatenate([inv_ref[:-LANES], inv_last_ref[...]], 0)
    mean_one = jnp.sum(scaled, -1, keepdims=True) * (1.0 / channels)
    mean_two = jnp.sum(scaled * unit, -1, keepdims=True) * (1.0 / channels)
    d_input = inv_std * (scaled - mean_one - unit * mean_two)
    done = g_ref[...] + d_input.reshape(g_ref.shape)
    for r in range(rows):
        row = done[:, r].reshape(cols, channels)
        row = jnp.concatenate([row[cols - SHIFT :], row[: cols - SHIFT]], 0)
        turn_s[:, r, :] = row.T
    framed_ref[...] = turn_s[...].astype(framed_ref.dtype)


def finish_kernel(out_scale, mine_ref, other_ref, core_ref, weight_ref, gain_ref, offset_ref, d_weight_ref, d_bias_ref, d_proj_ref, d_table_ref, d_gain_ref, d_offset_ref):
    channels = weight_ref.shape[0]
    f32 = jnp.float32
    rest = channels - LANES
    mine = mine_ref[...].astype(f32)
    other = other_ref[...].astype(f32)
    here = core_ref[0] == 0
    low = jnp.where(here, mine, other)
    high = jnp.where(here, other, mine)
    both = jnp.concatenate([low, high], 0) * out_scale
    pieces = []
    for at in range(4):
        row = (4 + at // 2) * ROWS
        side = (at % 2) * SPAN
        pieces.append(
            jnp.concatenate(
                [both[at * ROWS : (at + 1) * ROWS, :], both[row : row + ROWS, side : side + rest]], 1
            )
        )
    gain = gain_ref[...].T
    offset = offset_ref[...].T
    d_gain = jnp.zeros((channels, 1), f32)
    d_offset = jnp.zeros((channels, 1), f32)
    biases = []
    for part in range(3):
        across = slice(part * channels, (part + 1) * channels)
        unit = pieces[part][0:channels]
        bias = pieces[part][channels : channels + 1]
        weight = weight_ref[:, across].astype(f32)
        d_weight_ref[:, across] = gain * unit + offset * bias
        biases.append(bias)
        d_gain += jnp.sum(weight * unit, -1, keepdims=True)
        d_offset += jnp.sum(weight * bias, -1, keepdims=True)
    d_bias_ref[...] = jnp.concatenate(biases, 1).reshape(d_bias_ref.shape)
    d_gain_ref[...] = d_gain.T.reshape(channels)
    d_offset_ref[...] = d_offset.T.reshape(channels)
    d_proj_ref[...] = pieces[3][0:channels]
    table = jnp.concatenate([both[6 * ROWS : 6 * ROWS + 8], both[6 * ROWS + 8 :]], 1)
    d_table_ref[...] = table[0:HEADS, 0 : d_table_ref.shape[1]]


def whole(memory_space=pltpu.VMEM):
    return pl.BlockSpec(memory_space=memory_space)


def from_behind(shard, axis, by):
    count = lax.axis_size(axis)
    return lax.ppermute(shard, axis, [(i, (i + by) % count) for i in range(count)])


def diagonal(shard, by):
    rows, cols = lax.axis_size("row"), lax.axis_size("col")
    pairs = [
        (r * cols + c, ((r + by) % rows) * cols + (c + by) % cols) for r in range(rows) for c in range(cols)
    ]
    return lax.ppermute(shard, ("row", "col"), pairs)


def exchange_steps():
    rows, cols = lax.axis_size("row"), lax.axis_size("col")
    steps = [1 << bit for bit in range((rows - 1).bit_length())]
    for at in range(len(steps)):
        yield [
            (r * cols + c, (r ^ steps[(at + c) % len(steps)]) * cols + c) for r in range(rows) for c in range(cols)
        ]


def add(left, right):
    return (left.astype(jnp.float32) + right.astype(jnp.float32)).astype(jnp.bfloat16)


def on_device(
    tokens, grad_out, regions, ln_gain, ln_offset, qkv_weight, qkv_bias, proj_weight, bias_table
):
    rows, cols, channels = tokens.shape
    f32, bf16 = jnp.float32, jnp.bfloat16
    count = rows * cols
    params = pltpu.CompilerParams(vmem_limit_bytes=VMEM_LIMIT)

    x_turned = tokens.transpose(2, 0, 1)
    g_turned = grad_out.transpose(2, 0, 1)
    core = lax.axis_index("col").astype(jnp.int32).reshape(1)

    x_below = from_behind(x_turned[:, :SHIFT], "row", -1)
    g_rows, near_tokens, near_grad, near_ids = lax.optimization_barrier(
        (g_turned[:, :SHIFT], tokens, grad_out, regions)
    )
    g_below = from_behind(g_rows, "row", -1)

    def border(row_slice):
        return jnp.concatenate(
            [
                near_tokens[row_slice, :SHIFT],
                near_grad[row_slice, :SHIFT],
                near_ids[row_slice, :SHIFT, None].astype(bf16),
            ],
            -1,
        )

    right = from_behind(border(slice(SHIFT, None)), "col", -1)
    corner = diagonal(border(slice(0, SHIFT)), -1)

    table = jnp.pad(bias_table.T, ((0, 8 - HEADS), (0, 2 * LANES - bias_table.shape[0])))
    wide = HEADS * SLOT
    bias, tok, chan, proj_slots, parts = pl.pallas_call(
        prepare_kernel,
        name="prepare",
        out_shape=(
            jax.ShapeDtypeStruct((HEADS, SPAN, LANES), f32),
            jax.ShapeDtypeStruct((3, 2 * LANES, wide), bf16),
            jax.ShapeDtypeStruct((3, wide, 2 * LANES), bf16),
            jax.ShapeDtypeStruct((wide, channels), bf16),
            jax.ShapeDtypeStruct((3, channels, channels), bf16),
        ),
        in_specs=[whole()] * 4,
        out_specs=(whole(),) * 5,
        compiler_params=params,
        cost_estimate=pl.CostEstimate(flops=1000, bytes_accessed=1000, transcendentals=0),
    )(qkv_weight, qkv_bias[None], proj_weight, table)

    gain = jnp.pad(ln_gain, (0, 2 * LANES - channels))[None]
    offset = jnp.pad(ln_offset, (0, 2 * LANES - channels))[None]
    wins = cols // WIN
    unit, inv, *projected = pl.pallas_call(
        project_kernel,
        name="project",
        out_shape=(
            jax.ShapeDtypeStruct((count, 2 * LANES), f32),
            jax.ShapeDtypeStruct((count, 1), f32),
            jax.ShapeDtypeStruct((wide, count), bf16),
            jax.ShapeDtypeStruct((count, channels), bf16),
            jax.ShapeDtypeStruct((count, wide), bf16),
            jax.ShapeDtypeStruct((count, wide), bf16),
            jax.ShapeDtypeStruct((wide, count), bf16),
            jax.ShapeDtypeStruct((wide, count), bf16),
            jax.ShapeDtypeStruct((wide, count), bf16),
            jax.ShapeDtypeStruct((2, rows, WIN, 2 * LANES), f32),
        ),
        in_specs=[whole()] * 7,
        out_specs=(whole(),) * 10,
        scratch_shapes=[
            pltpu.VMEM((channels, SHIFT, cols), f32),
            pltpu.VMEM((wins, rows, WIN, 2 * LANES), f32),
        ],
        compiler_params=params,
        cost_estimate=pl.CostEstimate(flops=1000, bytes_accessed=1000, transcendentals=0),
    )(near_tokens, x_below, right, gain, offset, tok, chan)
    keep, send, *saved = pl.pallas_call(
        main_kernel,
        name="window_attention_backward",
        out_shape=(
            jax.ShapeDtypeStruct((BUFFER_ROWS // 2, LANES), bf16),
            jax.ShapeDtypeStruct((BUFFER_ROWS // 2, LANES), bf16),
            jax.ShapeDtypeStruct((3, count, channels), bf16),
            jax.ShapeDtypeStruct((wins, rows, WIN, channels), f32),
            jax.ShapeDtypeStruct((LANES, 2 * LANES), f32),
            jax.ShapeDtypeStruct((LANES, 1), f32),
        ),
        in_specs=[whole()] * 20 + [whole(pltpu.SMEM)],
        out_specs=(whole(),) * 6,
        scratch_shapes=[
            pltpu.VMEM((channels, SHIFT, cols), f32),
            pltpu.VMEM((2, rows, WIN, 2 * LANES), f32),
            pltpu.VMEM((wins, rows, WIN, 1), f32),
            pltpu.VMEM((count, channels), bf16),
            pltpu.VMEM((count, channels), bf16),
            pltpu.VMEM((wide, count), bf16),
            pltpu.VMEM((wide, count), bf16),
            pltpu.VMEM((HEADS, SPAN, LANES), f32),
            pltpu.VMEM((BUFFER_ROWS, LANES), f32),
        ],
        compiler_params=params,
    )(
        near_grad, near_ids, g_below, right, corner, gain, offset, bias, tok, chan, proj_weight, proj_slots,
        *projected, core,
    )
    saved = [*saved, unit, inv]

    mine = add(keep, from_behind(send, "col", 1))
    mine, *saved = lax.optimization_barrier((mine, *saved))
    (framed,) = pl.pallas_call(
        input_kernel,
        name="input_backward",
        out_shape=(jax.ShapeDtypeStruct((channels, rows, cols), bf16),),
        in_specs=[whole()] * 8,
        out_specs=(whole(),),
        scratch_shapes=[pltpu.VMEM((channels, rows, cols), f32)],
        compiler_params=params,
        cost_estimate=pl.CostEstimate(flops=10**9, bytes_accessed=0, transcendentals=0),
    )(*saved, gain, parts)
    steps = list(exchange_steps())
    for at, pairs in enumerate(steps):
        if at == min(1, len(steps) - 1):
            mine, framed = lax.optimization_barrier((mine, framed))
            beside = from_behind(framed, "col", 1)
            framed = jnp.where(jnp.arange(cols) < SHIFT, beside, framed)
        if at == min(2, len(steps) - 1):
            mine, framed = lax.optimization_barrier((mine, framed))
            above = from_behind(framed[:, rows - SHIFT :], "row", 1)
        mine = add(mine, lax.ppermute(mine, ("row", "col"), pairs))
    d_tokens = jnp.concatenate([above, framed[:, : rows - SHIFT]], 1).transpose(1, 2, 0)
    other = from_behind(mine, "col", 1)

    total_tokens = count * lax.axis_size("row") * lax.axis_size("col")
    d_weight, d_bias, d_proj, d_table, d_gain, d_offset = pl.pallas_call(
        functools.partial(finish_kernel, total_tokens ** (-0.5)),
        name="finish",
        out_shape=(
            jax.ShapeDtypeStruct(qkv_weight.shape, f32),
            jax.ShapeDtypeStruct(qkv_bias.shape, f32),
            jax.ShapeDtypeStruct(proj_weight.shape, f32),
            jax.ShapeDtypeStruct(bias_table.shape[::-1], f32),
            jax.ShapeDtypeStruct(ln_gain.shape, f32),
            jax.ShapeDtypeStruct(ln_offset.shape, f32),
        ),
        in_specs=[whole(), whole(), whole(pltpu.SMEM), whole(), whole(), whole()],
        out_specs=(whole(),) * 6,
        compiler_params=params,
    )(mine, other, core, qkv_weight, ln_gain[None], ln_offset[None])
    return (d_tokens, d_weight, d_bias, d_proj, d_table.T, d_gain, d_offset)


def solution(mesh):
    placed = (
        P(("grp", "row"), "col", None),
        P(("grp", "row"), "col", None),
        P(("grp", "row"), "col"),
        P(),
        P(),
        P(),
        P(),
        P(),
        P(),
    )
    return jax.shard_map(
        on_device,
        mesh=mesh,
        in_specs=placed,
        out_specs=(
            P(("grp", "row"), "col", None),
            P("grp", None),
            P("grp"),
            P("grp", None),
            P("grp", None),
            P("grp"),
            P("grp"),
        ),
        check_vma=False,
    )
```

```python
import functools

import jax
import jax.numpy as jnp
from jax import lax
from jax.experimental import pallas as pl
from jax.experimental.pallas import tpu as pltpu
from jax.sharding import PartitionSpec as P

HEADS = 6
WIN = 8
SHIFT = 4
SPAN = WIN * WIN
MASKED = -10000.0
LANES = 128
SLOT = 32
ROWS = 184
TABLE_ROWS = 16
BUFFER_ROWS = 6 * ROWS + TABLE_ROWS

VMEM_LIMIT = 32 * 1024 * 1024


def nn(left, right):
    return lax.dot_general(left, right, (((1,), (0,)), ((), ())), preferred_element_type=jnp.float32)


def nt(left, right):
    return lax.dot_general(left, right, (((1,), (1,)), ((), ())), preferred_element_type=jnp.float32)


def iota(shape, dim):
    return lax.broadcasted_iota(jnp.int32, shape, dim)


def table_hits(cj, lanes_first):
    shape = (LANES, 2 * LANES) if lanes_first else (2 * LANES, LANES)
    lane = iota(shape, 0 if lanes_first else 1)
    entry = iota(shape, 1 if lanes_first else 0)
    wanted = (lane // WIN) * (2 * WIN - 1) + lane % WIN + (WIN - 1) - cj
    return jnp.where((entry == wanted) & (lane < WIN * (2 * WIN - 1)), 1.0, 0.0).astype(jnp.bfloat16)


def split_three(value):
    high = value.astype(jnp.bfloat16)
    rest = value - high.astype(jnp.float32)
    middle = rest.astype(jnp.bfloat16)
    low = (rest - middle.astype(jnp.float32)).astype(jnp.bfloat16)
    return high, middle, low


def slots(rows):
    size = rows.shape[0] // HEADS
    blank = jnp.zeros((SLOT - size, rows.shape[1]), rows.dtype)
    pieces = []
    for head in range(HEADS):
        pieces += [rows[head * size : (head + 1) * size], blank]
    return jnp.concatenate(pieces, 0)


def unslot(rows, size):
    return jnp.concatenate([rows[head * SLOT : head * SLOT + size] for head in range(HEADS)], 0)


def prepare_kernel(weight_ref, offsets_ref, proj_ref, table_ref, bias_ref, tok_ref, chan_ref, proj_slots_ref, parts_ref):
    channels = weight_ref.shape[0]
    for part in range(3):
        weight = weight_ref[:, part * channels : (part + 1) * channels].astype(jnp.float32)
        parts_ref[part] = weight.astype(jnp.bfloat16)
        high, middle, low = split_three(offsets_ref[:, part * channels : (part + 1) * channels])
        full = jnp.concatenate(
            [
                weight,
                high.astype(jnp.float32),
                middle.astype(jnp.float32),
                low.astype(jnp.float32),
                jnp.zeros((256 - channels - 3, channels), jnp.float32),
            ],
            0,
        )
        turned = slots(full.T)
        chan_ref[part] = turned.astype(jnp.bfloat16)
        if part == 0:
            tok_ref[part, :, 0:channels] = full.astype(jnp.bfloat16)
            tok_ref[part, :, channels:] = jnp.zeros((256, HEADS * SLOT - channels), jnp.bfloat16)
        else:
            tok_ref[part] = turned.T.astype(jnp.bfloat16)
    proj_slots_ref[...] = slots(proj_ref[...].astype(jnp.float32)).astype(jnp.bfloat16)
    pieces = split_three(table_ref[...])
    lane = iota((8, LANES), 1)
    for cj in range(WIN):
        hits = table_hits(cj, False)
        spread = nn(pieces[0], hits) + nn(pieces[1], hits) + nn(pieces[2], hits)
        for rj in range(WIN):
            by = WIN * (WIN - 1 - rj)
            moved = spread if by == 0 else pltpu.roll(spread, LANES - by, 1)
            both = jnp.where(lane < SPAN, moved, pltpu.roll(moved, SPAN, 1))
            for head in range(HEADS):
                bias_ref[head, rj * WIN + cj : rj * WIN + cj + 1, :] = both[head : head + 1, :]


def normalize(x, channels, gain_ref, offset_ref):
    f32, bf16 = jnp.float32, jnp.bfloat16
    lane = iota((1, 2 * LANES), 1)
    center = jnp.sum(x, -1, keepdims=True) * (1.0 / channels)
    away = jnp.where(lane < channels, x - center, 0.0)
    variance = jnp.sum(away * away, -1, keepdims=True) * (1.0 / channels)
    inv_std = lax.rsqrt(variance + 1e-05)
    unit = away * inv_std
    unit_low = jnp.where(lane == channels, 1.0, unit).astype(bf16)
    normed = jnp.where(
        (lane >= channels) & (lane < channels + 3), 1.0, unit * gain_ref[...] + offset_ref[...]
    ).astype(bf16)
    return unit, inv_std, unit_low, normed


def project(normed, channels, tok_ref, chan_ref):
    bf16 = jnp.bfloat16
    scale = (channels // HEADS) ** (-0.5)
    return (
        (nn(normed, tok_ref[0, :, 0:channels]) * scale).astype(bf16),
        nn(normed, tok_ref[1]).astype(bf16),
        nn(normed, tok_ref[2]).astype(bf16),
        (nt(chan_ref[0], normed) * scale).astype(bf16),
        nt(chan_ref[1], normed).astype(bf16),
        nt(chan_ref[2], normed).astype(bf16),
    )


def project_kernel(
    tokens_ref,
    x_above_ref,
    right_ref,
    gain_ref,
    offset_ref,
    tok_ref,
    chan_ref,
    unit_ref,
    inv_ref,
    unit_turned_ref,
    q_tok_ref,
    k_tok_ref,
    v_tok_ref,
    q_chan_ref,
    k_chan_ref,
    v_chan_ref,
    x_last_ref,
    turn_s,
    x_s,
):
    rows, cols, channels = tokens_ref.shape
    wins = cols // WIN
    f32 = jnp.float32
    x_s[:, :, :, LANES:] = jnp.zeros(x_s.shape[:3] + (LANES,), f32)
    turn_s[...] = x_above_ref[...].astype(f32)
    for r in range(rows):
        if r < SHIFT:
            body = turn_s[:, r, :].T
            side = jnp.zeros((SHIFT, channels), f32)
        else:
            body = tokens_ref[r - SHIFT].astype(f32)
            side = right_ref[r - SHIFT].astype(f32)[:, 0:channels]
        row = jnp.concatenate([body[SHIFT:], side], 0)
        x_s[:, r, :, 0:channels] = row.reshape(wins, WIN, channels)
    x_last_ref[...] = x_s[wins - 2 :]
    unit, inv_std, unit_low, normed = normalize(
        x_s[...].reshape(rows * cols, 2 * LANES), channels, gain_ref, offset_ref
    )
    unit_ref[...] = unit
    inv_ref[...] = inv_std
    unit_turned_ref[...] = unit_low.T[0 : unit_turned_ref.shape[0]]
    results = project(normed, channels, tok_ref, chan_ref)
    for target, value in zip(
        (q_tok_ref, k_tok_ref, v_tok_ref, q_chan_ref, k_chan_ref, v_chan_ref), results
    ):
        target[...] = value


def main_kernel(
    grad_ref,
    region_ref,
    g_above_ref,
    right_ref,
    corner_ref,
    gain_ref,
    offset_ref,
    bias_ref,
    tok_ref,
    chan_ref,
    proj_ref,
    proj_slots_ref,
    unit_turned_ref,
    q_tok_ref,
    k_tok_ref,
    v_tok_ref,
    q_chan_ref,
    k_chan_ref,
    v_chan_ref,
    x_last_ref,
    core_ref,
    keep_ref,
    send_ref,
    d_qkv_s,
    g_s,
    unit_last_ref,
    inv_last_ref,
    turn_s,
    x_last_s,
    id_s,
    grad_s,
    da_tok_s,
    da_chan_s,
    attended_s,
    score_s,
    pack_s,
):
    rows, cols, channels = grad_ref.shape
    head_size = channels // HEADS
    scale = head_size ** (-0.5)
    count = rows * cols
    wins = cols // WIN
    f32 = jnp.float32
    bf16 = jnp.bfloat16

    turn_s[...] = g_above_ref[...].astype(f32)
    x_last_s[...] = x_last_ref[...]
    ids = region_ref[...].astype(f32).T
    at_id = slice(2 * channels, 2 * channels + 1)
    col_part = ids[:, 0:1] - 4.0 * jnp.floor(ids[:, 0:1] * 0.25)
    for r in range(rows):
        if r >= SHIFT:
            g_body = grad_ref[r - SHIFT].astype(f32)
            side = right_ref[r - SHIFT].astype(f32)
            id_body = ids[:, r - SHIFT : r - SHIFT + 1]
        else:
            g_body = turn_s[:, r, :].T
            side = corner_ref[r].astype(f32)
            id_body = col_part + 4.0 * jnp.floor(side[0:1, at_id] * 0.25)
            x_last_s[1, r, SHIFT:, 0:channels] = side[:, 0:channels]
        g_row = jnp.concatenate([g_body[SHIFT:], side[:, channels : 2 * channels]], 0)
        id_row = jnp.concatenate([id_body[SHIFT:], side[:, at_id]], 0)
        g_s[:, r, :, :] = g_row.reshape(wins, WIN, channels)
        id_s[:, r, :, :] = id_row.reshape(wins, WIN, 1)
    grad_s[...] = g_s[...].reshape(count, channels).astype(bf16)

    unit_last, inv_last, unit_low, normed = normalize(
        x_last_s[...].reshape(LANES, 2 * LANES), channels, gain_ref, offset_ref
    )
    unit_last_ref[...] = unit_last
    inv_last_ref[...] = inv_last
    last = project(normed, channels, tok_ref, chan_ref)
    da_tok_s[...] = nt(grad_s[...], proj_ref[...]).astype(bf16)
    da_chan_s[...] = nt(proj_slots_ref[...], grad_s[...]).astype(bf16)

    score_s[...] = jnp.zeros(score_s.shape, f32)
    first = iota((1, LANES), 1) < SPAN
    first_low = jnp.where(first, 1.0, 0.0).astype(bf16)
    second_low = jnp.where(first, 0.0, 1.0).astype(bf16)
    head_of = iota((1, channels), 1) // head_size
    id_lane = iota((1, LANES), 1).astype(f32)

    def pack(square):
        return jnp.where(first, square[0:SPAN], square[SPAN:])

    def spread(packed):
        low = packed.astype(bf16)
        return jnp.concatenate([low * first_low, low * second_low], 0)

    def in_blocks(chan):
        blank = jnp.zeros((SLOT, LANES), bf16)
        lines = []
        for head in range(HEADS):
            line = [blank] * HEADS
            line[head] = chan[head * SLOT : (head + 1) * SLOT]
            lines.append(jnp.concatenate(line, 1))
        return jnp.concatenate(lines, 0)

    def by_head(tok):
        return jnp.concatenate(
            [jnp.where(head_of == head, tok, jnp.zeros_like(tok)) for head in range(HEADS)], 0
        )

    for pair in range(count // LANES):
        at = slice(pair * LANES, (pair + 1) * LANES)
        if (pair + 1) * LANES == count:
            q_tok, k_tok, v_tok, q_chan, k_chan, v_chan = last
        else:
            q_tok, k_tok, v_tok = q_tok_ref[at, :], k_tok_ref[at, :], v_tok_ref[at, :]
            q_chan, k_chan, v_chan = q_chan_ref[:, at], k_chan_ref[:, at], v_chan_ref[:, at]
        hot = jnp.where(id_s[pair * 2 : pair * 2 + 2].reshape(LANES, 1) == id_lane, 1.0, 0.0).astype(bf16)
        match = pack(nt(hot, hot)) > 0.5
        scores = nn(k_tok, in_blocks(q_chan))
        d_prob = nn(v_tok, in_blocks(da_chan_s[:, at]))
        attended = []
        d_query = []
        probs = []
        d_scores = []
        for head in range(HEADS):
            here = slice(head * LANES, (head + 1) * LANES)
            band = slice(head * SLOT, (head + 1) * SLOT)
            score = jnp.where(match, pack(scores[:, here]) + bias_ref[head], MASKED)
            power = jnp.exp(score - jnp.max(score, 0, keepdims=True))
            prob = power * (1.0 / jnp.sum(power, 0, keepdims=True))
            gradient = pack(d_prob[:, here])
            d_score = prob * (gradient - jnp.sum(prob * gradient, 0, keepdims=True))
            score_s[head] += d_score
            prob_low = spread(prob)
            d_low = spread(d_score)
            attended.append(nn(v_chan[band], prob_low))
            d_query.append(nn(k_chan[band], d_low) * scale)
            probs.append(prob_low)
            d_scores.append(d_low)
        attended_s[:, at] = jnp.concatenate(attended, 0).astype(bf16)
        d_query = jnp.concatenate([piece[0:head_size] for piece in d_query], 0)
        d_qkv_s[0, at, :] = d_query.T.astype(bf16)
        d_qkv_s[1, at, :] = nn(jnp.concatenate(d_scores, 1), by_head(q_tok)).astype(bf16)
        d_qkv_s[2, at, :] = nn(jnp.concatenate(probs, 1), by_head(da_tok_s[at, :])).astype(bf16)

    unit_turned = jnp.concatenate([unit_turned_ref[:, : count - LANES], unit_low.T[0 : unit_turned_ref.shape[0]]], 1)
    rest = channels - LANES
    pieces = [nn(unit_turned, d_qkv_s[part])[0:ROWS] for part in range(3)]
    d_proj = nn(attended_s[...], grad_s[...])
    pieces.append(
        jnp.concatenate([unslot(d_proj, head_size), jnp.zeros((ROWS - channels, channels), f32)], 0)
    )
    pack_s[...] = jnp.zeros(pack_s.shape, f32)
    for at, piece in enumerate(pieces):
        pack_s[at * ROWS : (at + 1) * ROWS, :] = piece[:, 0:LANES]
        low = (4 + at // 2) * ROWS
        side = (at % 2) * SPAN
        pack_s[low : low + ROWS, side : side + rest] = piece[:, LANES:]
    lines = []
    for head in range(HEADS):
        both = score_s[head]
        both = jnp.where(first, both + pltpu.roll(both, SPAN, 1), 0.0)
        line = both[(WIN - 1) * WIN :]
        for rj in range(WIN - 1):
            line += pltpu.roll(both[rj * WIN : (rj + 1) * WIN], WIN * (WIN - 1 - rj), 1)
        lines.append(line)
    lines = jnp.concatenate(lines, 0)
    high = lines.astype(bf16)
    low = (lines - high.astype(f32)).astype(bf16)
    cj_of = iota((HEADS * WIN, 1), 0) % WIN
    table = jnp.zeros((HEADS * WIN, 2 * LANES), f32)
    for cj in range(WIN):
        hits = table_hits(cj, True)
        table += jnp.where(cj_of == cj, nn(high, hits) + nn(low, hits), 0.0)
    table = table.reshape(HEADS, WIN, 2 * LANES).sum(1)
    pack_s[6 * ROWS : 6 * ROWS + HEADS, :] = table[:, 0:LANES]
    pack_s[6 * ROWS + 8 : 6 * ROWS + 8 + HEADS, :] = table[:, LANES:]
    half = keep_ref.shape[0]
    low_half = pack_s[0:half, :].astype(bf16)
    high_half = pack_s[half:, :].astype(bf16)
    lower = core_ref[0] == 0
    keep_ref[...] = jnp.where(lower, low_half, high_half)
    send_ref[...] = jnp.where(lower, high_half, low_half)


def input_kernel(
    d_qkv_ref, g_ref, unit_last_ref, inv_last_ref, unit_ref, inv_ref, gain_ref, parts_ref, framed_ref, turn_s
):
    wins, rows, _, channels = g_ref.shape
    cols = wins * WIN
    f32 = jnp.float32
    d_normed = sum(nt(d_qkv_ref[part], parts_ref[part]) for part in range(3))
    scaled = d_normed * gain_ref[:, 0:channels]
    unit = jnp.concatenate([unit_ref[:-LANES, 0:channels], unit_last_ref[:, 0:channels]], 0)
    inv_std = jnp.concatenate([inv_ref[:-LANES], inv_last_ref[...]], 0)
    mean_one = jnp.sum(scaled, -1, keepdims=True) * (1.0 / channels)
    mean_two = jnp.sum(scaled * unit, -1, keepdims=True) * (1.0 / channels)
    d_input = inv_std * (scaled - mean_one - unit * mean_two)
    done = g_ref[...] + d_input.reshape(g_ref.shape)
    for r in range(rows):
        row = done[:, r].reshape(cols, channels)
        row = jnp.concatenate([row[cols - SHIFT :], row[: cols - SHIFT]], 0)
        turn_s[:, r, :] = row.T
    framed_ref[...] = turn_s[...].astype(framed_ref.dtype)


def finish_kernel(out_scale, mine_ref, other_ref, core_ref, weight_ref, gain_ref, offset_ref, d_weight_ref, d_bias_ref, d_proj_ref, d_table_ref, d_gain_ref, d_offset_ref):
    channels = weight_ref.shape[0]
    f32 = jnp.float32
    rest = channels - LANES
    mine = mine_ref[...].astype(f32)
    other = other_ref[...].astype(f32)
    here = core_ref[0] == 0
    low = jnp.where(here, mine, other)
    high = jnp.where(here, other, mine)
    both = jnp.concatenate([low, high], 0) * out_scale
    pieces = []
    for at in range(4):
        row = (4 + at // 2) * ROWS
        side = (at % 2) * SPAN
        pieces.append(
            jnp.concatenate(
                [both[at * ROWS : (at + 1) * ROWS, :], both[row : row + ROWS, side : side + rest]], 1
            )
        )
    gain = gain_ref[...].T
    offset = offset_ref[...].T
    d_gain = jnp.zeros((channels, 1), f32)
    d_offset = jnp.zeros((channels, 1), f32)
    biases = []
    for part in range(3):
        across = slice(part * channels, (part + 1) * channels)
        unit = pieces[part][0:channels]
        bias = pieces[part][channels : channels + 1]
        weight = weight_ref[:, across].astype(f32)
        d_weight_ref[:, across] = gain * unit + offset * bias
        biases.append(bias)
        d_gain += jnp.sum(weight * unit, -1, keepdims=True)
        d_offset += jnp.sum(weight * bias, -1, keepdims=True)
    d_bias_ref[...] = jnp.concatenate(biases, 1).reshape(d_bias_ref.shape)
    d_gain_ref[...] = d_gain.T.reshape(channels)
    d_offset_ref[...] = d_offset.T.reshape(channels)
    d_proj_ref[...] = pieces[3][0:channels]
    table = jnp.concatenate([both[6 * ROWS : 6 * ROWS + 8], both[6 * ROWS + 8 :]], 1)
    d_table_ref[...] = table[0:HEADS, 0 : d_table_ref.shape[1]]


def whole(memory_space=pltpu.VMEM):
    return pl.BlockSpec(memory_space=memory_space)


def from_behind(shard, axis, by):
    count = lax.axis_size(axis)
    return lax.ppermute(shard, axis, [(i, (i + by) % count) for i in range(count)])


def diagonal(shard):
    rows, cols = lax.axis_size("row"), lax.axis_size("col")
    pairs = [
        (r * cols + c, ((r + 1) % rows) * cols + (c - 1) % cols) for r in range(rows) for c in range(cols)
    ]
    return lax.ppermute(shard, ("row", "col"), pairs)


def exchange_steps():
    rows, cols = lax.axis_size("row"), lax.axis_size("col")
    steps = [1 << bit for bit in range((rows - 1).bit_length())]
    for at in range(len(steps)):
        yield [
            (r * cols + c, (r ^ steps[(at + c) % len(steps)]) * cols + c) for r in range(rows) for c in range(cols)
        ]


def add(left, right):
    return (left.astype(jnp.float32) + right.astype(jnp.float32)).astype(jnp.bfloat16)


def on_device(
    tokens, grad_out, regions, ln_gain, ln_offset, qkv_weight, qkv_bias, proj_weight, bias_table
):
    rows, cols, channels = tokens.shape
    f32, bf16 = jnp.float32, jnp.bfloat16
    count = rows * cols
    params = pltpu.CompilerParams(vmem_limit_bytes=VMEM_LIMIT)

    x_turned = tokens.transpose(2, 0, 1)
    g_turned = grad_out.transpose(2, 0, 1)
    core = lax.axis_index("col").astype(jnp.int32).reshape(1)

    x_above = from_behind(x_turned[:, rows - SHIFT :], "row", 1)
    g_rows, near_tokens, near_grad, near_ids = lax.optimization_barrier(
        (g_turned[:, rows - SHIFT :], tokens, grad_out, regions)
    )
    g_above = from_behind(g_rows, "row", 1)

    def border(row_slice):
        return jnp.concatenate(
            [
                near_tokens[row_slice, :SHIFT],
                near_grad[row_slice, :SHIFT],
                near_ids[row_slice, :SHIFT, None].astype(bf16),
            ],
            -1,
        )

    right = from_behind(border(slice(0, rows - SHIFT)), "col", -1)
    corner = diagonal(border(slice(rows - SHIFT, None)))

    table = jnp.pad(bias_table.T, ((0, 8 - HEADS), (0, 2 * LANES - bias_table.shape[0])))
    wide = HEADS * SLOT
    bias, tok, chan, proj_slots, parts = pl.pallas_call(
        prepare_kernel,
        name="prepare",
        out_shape=(
            jax.ShapeDtypeStruct((HEADS, SPAN, LANES), f32),
            jax.ShapeDtypeStruct((3, 2 * LANES, wide), bf16),
            jax.ShapeDtypeStruct((3, wide, 2 * LANES), bf16),
            jax.ShapeDtypeStruct((wide, channels), bf16),
            jax.ShapeDtypeStruct((3, channels, channels), bf16),
        ),
        in_specs=[whole()] * 4,
        out_specs=(whole(),) * 5,
        compiler_params=params,
        cost_estimate=pl.CostEstimate(flops=1000, bytes_accessed=1000, transcendentals=0),
    )(qkv_weight, qkv_bias[None], proj_weight, table)

    gain = jnp.pad(ln_gain, (0, 2 * LANES - channels))[None]
    offset = jnp.pad(ln_offset, (0, 2 * LANES - channels))[None]
    wins = cols // WIN
    unit, inv, *projected = pl.pallas_call(
        project_kernel,
        name="project",
        out_shape=(
            jax.ShapeDtypeStruct((count, 2 * LANES), f32),
            jax.ShapeDtypeStruct((count, 1), f32),
            jax.ShapeDtypeStruct((wide, count), bf16),
            jax.ShapeDtypeStruct((count, channels), bf16),
            jax.ShapeDtypeStruct((count, wide), bf16),
            jax.ShapeDtypeStruct((count, wide), bf16),
            jax.ShapeDtypeStruct((wide, count), bf16),
            jax.ShapeDtypeStruct((wide, count), bf16),
            jax.ShapeDtypeStruct((wide, count), bf16),
            jax.ShapeDtypeStruct((2, rows, WIN, 2 * LANES), f32),
        ),
        in_specs=[whole()] * 7,
        out_specs=(whole(),) * 10,
        scratch_shapes=[
            pltpu.VMEM((channels, SHIFT, cols), f32),
            pltpu.VMEM((wins, rows, WIN, 2 * LANES), f32),
        ],
        compiler_params=params,
        cost_estimate=pl.CostEstimate(flops=1000, bytes_accessed=1000, transcendentals=0),
    )(near_tokens, x_above, right, gain, offset, tok, chan)
    keep, send, *saved = pl.pallas_call(
        main_kernel,
        name="window_attention_backward",
        out_shape=(
            jax.ShapeDtypeStruct((BUFFER_ROWS // 2, LANES), bf16),
            jax.ShapeDtypeStruct((BUFFER_ROWS // 2, LANES), bf16),
            jax.ShapeDtypeStruct((3, count, channels), bf16),
            jax.ShapeDtypeStruct((wins, rows, WIN, channels), f32),
            jax.ShapeDtypeStruct((LANES, 2 * LANES), f32),
            jax.ShapeDtypeStruct((LANES, 1), f32),
        ),
        in_specs=[whole()] * 20 + [whole(pltpu.SMEM)],
        out_specs=(whole(),) * 6,
        scratch_shapes=[
            pltpu.VMEM((channels, SHIFT, cols), f32),
            pltpu.VMEM((2, rows, WIN, 2 * LANES), f32),
            pltpu.VMEM((wins, rows, WIN, 1), f32),
            pltpu.VMEM((count, channels), bf16),
            pltpu.VMEM((count, channels), bf16),
            pltpu.VMEM((wide, count), bf16),
            pltpu.VMEM((wide, count), bf16),
            pltpu.VMEM((HEADS, SPAN, LANES), f32),
            pltpu.VMEM((BUFFER_ROWS, LANES), f32),
        ],
        compiler_params=params,
    )(
        near_grad, near_ids, g_above, right, corner, gain, offset, bias, tok, chan, proj_weight, proj_slots,
        *projected, core,
    )
    saved = [*saved, unit, inv]

    mine = add(keep, from_behind(send, "col", 1))
    mine, *saved = lax.optimization_barrier((mine, *saved))
    (framed,) = pl.pallas_call(
        input_kernel,
        name="input_backward",
        out_shape=(jax.ShapeDtypeStruct((channels, rows, cols), bf16),),
        in_specs=[whole()] * 8,
        out_specs=(whole(),),
        scratch_shapes=[pltpu.VMEM((channels, rows, cols), f32)],
        compiler_params=params,
        cost_estimate=pl.CostEstimate(flops=10**9, bytes_accessed=0, transcendentals=0),
    )(*saved, gain, parts)
    steps = list(exchange_steps())
    for at, pairs in enumerate(steps):
        if at == min(1, len(steps) - 1):
            mine, framed = lax.optimization_barrier((mine, framed))
            beside = from_behind(framed, "col", 1)
            framed = jnp.where(jnp.arange(cols) < SHIFT, beside, framed)
        if at == min(2, len(steps) - 1):
            mine, framed = lax.optimization_barrier((mine, framed))
            below = from_behind(framed[:, :SHIFT], "row", -1)
        mine = add(mine, lax.ppermute(mine, ("row", "col"), pairs))
    d_tokens = jnp.concatenate([framed[:, SHIFT:], below], 1).transpose(1, 2, 0)
    other = from_behind(mine, "col", 1)

    total_tokens = count * lax.axis_size("row") * lax.axis_size("col")
    d_weight, d_bias, d_proj, d_table, d_gain, d_offset = pl.pallas_call(
        functools.partial(finish_kernel, total_tokens ** (-0.5)),
        name="finish",
        out_shape=(
            jax.ShapeDtypeStruct(qkv_weight.shape, f32),
            jax.ShapeDtypeStruct(qkv_bias.shape, f32),
            jax.ShapeDtypeStruct(proj_weight.shape, f32),
            jax.ShapeDtypeStruct(bias_table.shape[::-1], f32),
            jax.ShapeDtypeStruct(ln_gain.shape, f32),
            jax.ShapeDtypeStruct(ln_offset.shape, f32),
        ),
        in_specs=[whole(), whole(), whole(pltpu.SMEM), whole(), whole(), whole()],
        out_specs=(whole(),) * 6,
        compiler_params=params,
    )(mine, other, core, qkv_weight, ln_gain[None], ln_offset[None])
    return (d_tokens, d_weight, d_bias, d_proj, d_table.T, d_gain, d_offset)


def solution(mesh):
    placed = (
        P(("grp", "row"), "col", None),
        P(("grp", "row"), "col", None),
        P(("grp", "row"), "col"),
        P(),
        P(),
        P(),
        P(),
        P(),
        P(),
    )
    return jax.shard_map(
        on_device,
        mesh=mesh,
        in_specs=placed,
        out_specs=(
            P(("grp", "row"), "col", None),
            P("grp", None),
            P("grp"),
            P("grp", None),
            P("grp", None),
            P("grp"),
            P("grp"),
        ),
        check_vma=False,
    )
```

```python
import functools

import jax
import jax.numpy as jnp
from jax import lax
from jax.experimental import pallas as pl
from jax.experimental.pallas import tpu as pltpu
from jax.sharding import PartitionSpec as P

HEADS = 6
WIN = 8
SHIFT = 4
SPAN = WIN * WIN
MASKED = -10000.0
LANES = 128
SLOT = 32
ROWS = 184
TABLE_ROWS = 16
BUFFER_ROWS = 6 * ROWS + TABLE_ROWS

VMEM_LIMIT = 32 * 1024 * 1024


def nn(left, right):
    return lax.dot_general(left, right, (((1,), (0,)), ((), ())), preferred_element_type=jnp.float32)


def nt(left, right):
    return lax.dot_general(left, right, (((1,), (1,)), ((), ())), preferred_element_type=jnp.float32)


def iota(shape, dim):
    return lax.broadcasted_iota(jnp.int32, shape, dim)


def table_hits(cj, lanes_first):
    shape = (LANES, 2 * LANES) if lanes_first else (2 * LANES, LANES)
    lane = iota(shape, 0 if lanes_first else 1)
    entry = iota(shape, 1 if lanes_first else 0)
    wanted = (lane // WIN) * (2 * WIN - 1) + lane % WIN + (WIN - 1) - cj
    return jnp.where((entry == wanted) & (lane < WIN * (2 * WIN - 1)), 1.0, 0.0).astype(jnp.bfloat16)


def split_three(value):
    high = value.astype(jnp.bfloat16)
    rest = value - high.astype(jnp.float32)
    middle = rest.astype(jnp.bfloat16)
    low = (rest - middle.astype(jnp.float32)).astype(jnp.bfloat16)
    return high, middle, low


def slots(rows):
    size = rows.shape[0] // HEADS
    blank = jnp.zeros((SLOT - size, rows.shape[1]), rows.dtype)
    pieces = []
    for head in range(HEADS):
        pieces += [rows[head * size : (head + 1) * size], blank]
    return jnp.concatenate(pieces, 0)


def unslot(rows, size):
    return jnp.concatenate([rows[head * SLOT : head * SLOT + size] for head in range(HEADS)], 0)


def prepare_kernel(weight_ref, offsets_ref, proj_ref, table_ref, bias_ref, tok_ref, chan_ref, proj_slots_ref, parts_ref):
    channels = weight_ref.shape[0]
    for part in range(3):
        weight = weight_ref[:, part * channels : (part + 1) * channels].astype(jnp.float32)
        parts_ref[part] = weight.astype(jnp.bfloat16)
        high, middle, low = split_three(offsets_ref[:, part * channels : (part + 1) * channels])
        full = jnp.concatenate(
            [
                weight,
                high.astype(jnp.float32),
                middle.astype(jnp.float32),
                low.astype(jnp.float32),
                jnp.zeros((256 - channels - 3, channels), jnp.float32),
            ],
            0,
        )
        turned = slots(full.T)
        chan_ref[part] = turned.astype(jnp.bfloat16)
        if part == 0:
            tok_ref[part, :, 0:channels] = full.astype(jnp.bfloat16)
            tok_ref[part, :, channels:] = jnp.zeros((256, HEADS * SLOT - channels), jnp.bfloat16)
        else:
            tok_ref[part] = turned.T.astype(jnp.bfloat16)
    proj_slots_ref[...] = slots(proj_ref[...].astype(jnp.float32)).astype(jnp.bfloat16)
    pieces = split_three(table_ref[...])
    lane = iota((8, LANES), 1)
    for cj in range(WIN):
        hits = table_hits(cj, False)
        spread = nn(pieces[0], hits) + nn(pieces[1], hits) + nn(pieces[2], hits)
        for rj in range(WIN):
            by = WIN * (WIN - 1 - rj)
            moved = spread if by == 0 else pltpu.roll(spread, LANES - by, 1)
            both = jnp.where(lane < SPAN, moved, pltpu.roll(moved, SPAN, 1))
            for head in range(HEADS):
                bias_ref[head, rj * WIN + cj : rj * WIN + cj + 1, :] = both[head : head + 1, :]


def normalize(x, channels, gain_ref, offset_ref):
    f32, bf16 = jnp.float32, jnp.bfloat16
    lane = iota((1, 2 * LANES), 1)
    center = jnp.sum(x, -1, keepdims=True) * (1.0 / channels)
    away = jnp.where(lane < channels, x - center, 0.0)
    variance = jnp.sum(away * away, -1, keepdims=True) * (1.0 / channels)
    inv_std = lax.rsqrt(variance + 1e-05)
    unit = away * inv_std
    unit_low = jnp.where(lane == channels, 1.0, unit).astype(bf16)
    normed = jnp.where(
        (lane >= channels) & (lane < channels + 3), 1.0, unit * gain_ref[...] + offset_ref[...]
    ).astype(bf16)
    return unit, inv_std, unit_low, normed


def project(normed, channels, tok_ref, chan_ref):
    bf16 = jnp.bfloat16
    scale = (channels // HEADS) ** (-0.5)
    return (
        (nn(normed, tok_ref[0, :, 0:channels]) * scale).astype(bf16),
        nn(normed, tok_ref[1]).astype(bf16),
        nn(normed, tok_ref[2]).astype(bf16),
        (nt(chan_ref[0], normed) * scale).astype(bf16),
        nt(chan_ref[1], normed).astype(bf16),
        nt(chan_ref[2], normed).astype(bf16),
    )


def project_kernel(
    tokens_ref,
    x_above_ref,
    right_ref,
    gain_ref,
    offset_ref,
    tok_ref,
    chan_ref,
    unit_ref,
    inv_ref,
    unit_turned_ref,
    q_tok_ref,
    k_tok_ref,
    v_tok_ref,
    q_chan_ref,
    k_chan_ref,
    v_chan_ref,
    x_last_ref,
    turn_s,
    x_s,
):
    rows, cols, channels = tokens_ref.shape
    wins = cols // WIN
    f32 = jnp.float32
    x_s[:, :, :, LANES:] = jnp.zeros(x_s.shape[:3] + (LANES,), f32)
    turn_s[...] = x_above_ref[...].astype(f32)
    for r in range(rows):
        if r < SHIFT:
            body = turn_s[:, r, :].T
            side = jnp.zeros((SHIFT, channels), f32)
        else:
            body = tokens_ref[r - SHIFT].astype(f32)
            side = right_ref[r - SHIFT].astype(f32)[:, 0:channels]
        row = jnp.concatenate([body[SHIFT:], side], 0)
        x_s[:, r, :, 0:channels] = row.reshape(wins, WIN, channels)
    x_last_ref[...] = x_s[wins - 2 :]
    unit, inv_std, unit_low, normed = normalize(
        x_s[...].reshape(rows * cols, 2 * LANES), channels, gain_ref, offset_ref
    )
    unit_ref[...] = unit
    inv_ref[...] = inv_std
    unit_turned_ref[...] = unit_low.T[0 : unit_turned_ref.shape[0]]
    results = project(normed, channels, tok_ref, chan_ref)
    for target, value in zip(
        (q_tok_ref, k_tok_ref, v_tok_ref, q_chan_ref, k_chan_ref, v_chan_ref), results
    ):
        target[...] = value


def main_kernel(
    grad_ref,
    region_ref,
    g_above_ref,
    right_ref,
    corner_ref,
    gain_ref,
    offset_ref,
    bias_ref,
    tok_ref,
    chan_ref,
    proj_ref,
    proj_slots_ref,
    unit_turned_ref,
    q_tok_ref,
    k_tok_ref,
    v_tok_ref,
    q_chan_ref,
    k_chan_ref,
    v_chan_ref,
    x_last_ref,
    core_ref,
    keep_ref,
    send_ref,
    d_qkv_s,
    g_s,
    unit_last_ref,
    inv_last_ref,
    turn_s,
    x_last_s,
    id_s,
    grad_s,
    da_tok_s,
    da_chan_s,
    attended_s,
    score_s,
    pack_s,
):
    rows, cols, channels = grad_ref.shape
    head_size = channels // HEADS
    scale = head_size ** (-0.5)
    count = rows * cols
    wins = cols // WIN
    f32 = jnp.float32
    bf16 = jnp.bfloat16

    turn_s[...] = g_above_ref[...].astype(f32)
    x_last_s[...] = x_last_ref[...]
    ids = region_ref[...].astype(f32).T
    at_id = slice(2 * channels, 2 * channels + 1)
    col_part = ids[:, 0:1] - 4.0 * jnp.floor(ids[:, 0:1] * 0.25)
    for r in range(rows):
        if r >= SHIFT:
            g_body = grad_ref[r - SHIFT].astype(f32)
            side = right_ref[r - SHIFT].astype(f32)
            id_body = ids[:, r - SHIFT : r - SHIFT + 1]
        else:
            g_body = turn_s[:, r, :].T
            side = corner_ref[r].astype(f32)
            id_body = col_part + 4.0 * jnp.floor(side[0:1, at_id] * 0.25)
            x_last_s[1, r, SHIFT:, 0:channels] = side[:, 0:channels]
        g_row = jnp.concatenate([g_body[SHIFT:], side[:, channels : 2 * channels]], 0)
        id_row = jnp.concatenate([id_body[SHIFT:], side[:, at_id]], 0)
        g_s[:, r, :, :] = g_row.reshape(wins, WIN, channels)
        id_s[:, r, :, :] = id_row.reshape(wins, WIN, 1)
    grad_s[...] = g_s[...].reshape(count, channels).astype(bf16)

    unit_last, inv_last, unit_low, normed = normalize(
        x_last_s[...].reshape(LANES, 2 * LANES), channels, gain_ref, offset_ref
    )
    unit_last_ref[...] = unit_last
    inv_last_ref[...] = inv_last
    last = project(normed, channels, tok_ref, chan_ref)
    da_tok_s[...] = nt(grad_s[...], proj_ref[...]).astype(bf16)
    da_chan_s[...] = nt(proj_slots_ref[...], grad_s[...]).astype(bf16)

    score_s[...] = jnp.zeros(score_s.shape, f32)
    first = iota((1, LANES), 1) < SPAN
    first_low = jnp.where(first, 1.0, 0.0).astype(bf16)
    second_low = jnp.where(first, 0.0, 1.0).astype(bf16)
    head_of = iota((1, channels), 1) // head_size
    id_lane = iota((1, LANES), 1).astype(f32)

    def pack(square):
        return jnp.where(first, square[0:SPAN], square[SPAN:])

    def spread(packed):
        low = packed.astype(bf16)
        return jnp.concatenate([low * first_low, low * second_low], 0)

    def in_blocks(chan):
        blank = jnp.zeros((SLOT, LANES), bf16)
        lines = []
        for head in range(HEADS):
            line = [blank] * HEADS
            line[head] = chan[head * SLOT : (head + 1) * SLOT]
            lines.append(jnp.concatenate(line, 1))
        return jnp.concatenate(lines, 0)

    def by_head(tok):
        return jnp.concatenate(
            [jnp.where(head_of == head, tok, jnp.zeros_like(tok)) for head in range(HEADS)], 0
        )

    for pair in range(count // LANES):
        at = slice(pair * LANES, (pair + 1) * LANES)
        if (pair + 1) * LANES == count:
            q_tok, k_tok, v_tok, q_chan, k_chan, v_chan = last
        else:
            q_tok, k_tok, v_tok = q_tok_ref[at, :], k_tok_ref[at, :], v_tok_ref[at, :]
            q_chan, k_chan, v_chan = q_chan_ref[:, at], k_chan_ref[:, at], v_chan_ref[:, at]
        hot = jnp.where(id_s[pair * 2 : pair * 2 + 2].reshape(LANES, 1) == id_lane, 1.0, 0.0).astype(bf16)
        match = pack(nt(hot, hot)) > 0.5
        scores = nn(k_tok, in_blocks(q_chan))
        d_prob = nn(v_tok, in_blocks(da_chan_s[:, at]))
        attended = []
        d_query = []
        probs = []
        d_scores = []
        for head in range(HEADS):
            here = slice(head * LANES, (head + 1) * LANES)
            band = slice(head * SLOT, (head + 1) * SLOT)
            score = jnp.where(match, pack(scores[:, here]) + bias_ref[head], MASKED)
            power = jnp.exp(score - jnp.max(score, 0, keepdims=True))
            prob = power * (1.0 / jnp.sum(power, 0, keepdims=True))
            gradient = pack(d_prob[:, here])
            d_score = prob * (gradient - jnp.sum(prob * gradient, 0, keepdims=True))
            score_s[head] += d_score
            prob_low = spread(prob)
            d_low = spread(d_score)
            attended.append(nn(v_chan[band], prob_low))
            d_query.append(nn(k_chan[band], d_low) * scale)
            probs.append(prob_low)
            d_scores.append(d_low)
        attended_s[:, at] = jnp.concatenate(attended, 0).astype(bf16)
        d_query = jnp.concatenate([piece[0:head_size] for piece in d_query], 0)
        d_qkv_s[0, at, :] = d_query.T.astype(bf16)
        d_qkv_s[1, at, :] = nn(jnp.concatenate(d_scores, 1), by_head(q_tok)).astype(bf16)
        d_qkv_s[2, at, :] = nn(jnp.concatenate(probs, 1), by_head(da_tok_s[at, :])).astype(bf16)

    unit_turned = jnp.concatenate([unit_turned_ref[:, : count - LANES], unit_low.T[0 : unit_turned_ref.shape[0]]], 1)
    rest = channels - LANES
    pieces = [nn(unit_turned, d_qkv_s[part])[0:ROWS] for part in range(3)]
    d_proj = nn(attended_s[...], grad_s[...])
    pieces.append(
        jnp.concatenate([unslot(d_proj, head_size), jnp.zeros((ROWS - channels, channels), f32)], 0)
    )
    pack_s[...] = jnp.zeros(pack_s.shape, f32)
    for at, piece in enumerate(pieces):
        pack_s[at * ROWS : (at + 1) * ROWS, :] = piece[:, 0:LANES]
        low = (4 + at // 2) * ROWS
        side = (at % 2) * SPAN
        pack_s[low : low + ROWS, side : side + rest] = piece[:, LANES:]
    lines = []
    for head in range(HEADS):
        both = score_s[head]
        both = jnp.where(first, both + pltpu.roll(both, SPAN, 1), 0.0)
        line = both[(WIN - 1) * WIN :]
        for rj in range(WIN - 1):
            line += pltpu.roll(both[rj * WIN : (rj + 1) * WIN], WIN * (WIN - 1 - rj), 1)
        lines.append(line)
    lines = jnp.concatenate(lines, 0)
    high = lines.astype(bf16)
    low = (lines - high.astype(f32)).astype(bf16)
    cj_of = iota((HEADS * WIN, 1), 0) % WIN
    table = jnp.zeros((HEADS * WIN, 2 * LANES), f32)
    for cj in range(WIN):
        hits = table_hits(cj, True)
        table += jnp.where(cj_of == cj, nn(high, hits) + nn(low, hits), 0.0)
    table = table.reshape(HEADS, WIN, 2 * LANES).sum(1)
    pack_s[6 * ROWS : 6 * ROWS + HEADS, :] = table[:, 0:LANES]
    pack_s[6 * ROWS + 8 : 6 * ROWS + 8 + HEADS, :] = table[:, LANES:]
    half = keep_ref.shape[0]
    low_half = pack_s[0:half, :].astype(bf16)
    high_half = pack_s[half:, :].astype(bf16)
    lower = core_ref[0] == 0
    keep_ref[...] = jnp.where(lower, low_half, high_half)
    send_ref[...] = jnp.where(lower, high_half, low_half)


def input_kernel(
    d_qkv_ref, g_ref, unit_last_ref, inv_last_ref, unit_ref, inv_ref, gain_ref, parts_ref, framed_ref, turn_s
):
    wins, rows, _, channels = g_ref.shape
    cols = wins * WIN
    f32 = jnp.float32
    d_normed = sum(nt(d_qkv_ref[part], parts_ref[part]) for part in range(3))
    scaled = d_normed * gain_ref[:, 0:channels]
    unit = jnp.concatenate([unit_ref[:-LANES, 0:channels], unit_last_ref[:, 0:channels]], 0)
    inv_std = jnp.concatenate([inv_ref[:-LANES], inv_last_ref[...]], 0)
    mean_one = jnp.sum(scaled, -1, keepdims=True) * (1.0 / channels)
    mean_two = jnp.sum(scaled * unit, -1, keepdims=True) * (1.0 / channels)
    d_input = inv_std * (scaled - mean_one - unit * mean_two)
    done = g_ref[...] + d_input.reshape(g_ref.shape)
    for r in range(rows):
        row = done[:, r].reshape(cols, channels)
        row = jnp.concatenate([row[cols - SHIFT :], row[: cols - SHIFT]], 0)
        turn_s[:, r, :] = row.T
    framed_ref[...] = turn_s[...].astype(framed_ref.dtype)


def finish_kernel(
    out_scale,
    mine_ref,
    other_ref,
    core_ref,
    weight_ref,
    gain_ref,
    offset_ref,
    d_weight_ref,
    d_bias_ref,
    d_proj_ref,
    d_table_ref,
    d_gain_ref,
    d_offset_ref,
):
    channels = weight_ref.shape[0]
    f32 = jnp.float32
    rest = channels - LANES
    mine = mine_ref[...].astype(f32)
    other = other_ref[...].astype(f32)
    here = core_ref[0] == 0
    low = jnp.where(here, mine, other)
    high = jnp.where(here, other, mine)
    both = jnp.concatenate([low, high], 0) * out_scale
    pieces = []
    for at in range(4):
        row = (4 + at // 2) * ROWS
        side = (at % 2) * SPAN
        pieces.append(
            jnp.concatenate(
                [both[at * ROWS : (at + 1) * ROWS, :], both[row : row + ROWS, side : side + rest]], 1
            )
        )
    gain = gain_ref[...].T
    offset = offset_ref[...].T
    ones = jnp.ones((8, channels), jnp.bfloat16)
    products = jnp.zeros((channels, channels), f32)
    d_offset = jnp.zeros((8, channels), f32)
    biases = []
    for part in range(3):
        across = slice(part * channels, (part + 1) * channels)
        unit = pieces[part][0:channels]
        bias = pieces[part][channels : channels + 1]
        weight = weight_ref[:, across]
        d_weight_ref[:, across] = gain * unit + offset * bias
        biases.append(bias)
        products += weight.astype(f32) * unit
        for term in split_three(bias):
            d_offset += nt(jnp.broadcast_to(term, (8, channels)), weight)
    d_bias_ref[...] = jnp.concatenate(biases, 1).reshape(d_bias_ref.shape)
    d_gain = sum(nt(ones, term) for term in split_three(products))
    d_gain_ref[...] = d_gain[0:1].reshape(channels)
    d_offset_ref[...] = d_offset[0:1].reshape(channels)
    d_proj_ref[...] = pieces[3][0:channels]
    table = jnp.concatenate([both[6 * ROWS : 6 * ROWS + 8], both[6 * ROWS + 8 :]], 1)
    d_table_ref[...] = table[0:HEADS, 0 : d_table_ref.shape[1]]


def whole(memory_space=pltpu.VMEM):
    return pl.BlockSpec(memory_space=memory_space)


def from_behind(shard, axis, by):
    count = lax.axis_size(axis)
    return lax.ppermute(shard, axis, [(i, (i + by) % count) for i in range(count)])


def diagonal(shard):
    rows, cols = lax.axis_size("row"), lax.axis_size("col")
    pairs = [
        (r * cols + c, ((r + 1) % rows) * cols + (c - 1) % cols) for r in range(rows) for c in range(cols)
    ]
    return lax.ppermute(shard, ("row", "col"), pairs)


def exchange_steps():
    rows, cols = lax.axis_size("row"), lax.axis_size("col")
    steps = [1 << bit for bit in range((rows - 1).bit_length())]
    for at in range(len(steps)):
        yield [
            (r * cols + c, (r ^ steps[(at - c) % len(steps)]) * cols + c) for r in range(rows) for c in range(cols)
        ]


def add(left, right):
    return (left.astype(jnp.float32) + right.astype(jnp.float32)).astype(jnp.bfloat16)


def on_device(
    tokens, grad_out, regions, ln_gain, ln_offset, qkv_weight, qkv_bias, proj_weight, bias_table
):
    rows, cols, channels = tokens.shape
    f32, bf16 = jnp.float32, jnp.bfloat16
    count = rows * cols
    params = pltpu.CompilerParams(vmem_limit_bytes=VMEM_LIMIT)

    x_turned = tokens.transpose(2, 0, 1)
    g_turned = grad_out.transpose(2, 0, 1)
    core = lax.axis_index("col").astype(jnp.int32).reshape(1)

    x_above = from_behind(x_turned[:, rows - SHIFT :], "row", 1)
    g_rows, near_tokens, near_grad, near_ids = lax.optimization_barrier(
        (g_turned[:, rows - SHIFT :], tokens, grad_out, regions)
    )
    g_above = from_behind(g_rows, "row", 1)

    def border(row_slice):
        return jnp.concatenate(
            [
                near_tokens[row_slice, :SHIFT],
                near_grad[row_slice, :SHIFT],
                near_ids[row_slice, :SHIFT, None].astype(bf16),
            ],
            -1,
        )

    right = from_behind(border(slice(0, rows - SHIFT)), "col", -1)
    corner = diagonal(border(slice(rows - SHIFT, None)))

    table = jnp.pad(bias_table.T, ((0, 8 - HEADS), (0, 2 * LANES - bias_table.shape[0])))
    wide = HEADS * SLOT
    bias, tok, chan, proj_slots, parts = pl.pallas_call(
        prepare_kernel,
        name="prepare",
        out_shape=(
            jax.ShapeDtypeStruct((HEADS, SPAN, LANES), f32),
            jax.ShapeDtypeStruct((3, 2 * LANES, wide), bf16),
            jax.ShapeDtypeStruct((3, wide, 2 * LANES), bf16),
            jax.ShapeDtypeStruct((wide, channels), bf16),
            jax.ShapeDtypeStruct((3, channels, channels), bf16),
        ),
        in_specs=[whole()] * 4,
        out_specs=(whole(),) * 5,
        compiler_params=params,
        cost_estimate=pl.CostEstimate(flops=1000, bytes_accessed=1000, transcendentals=0),
    )(qkv_weight, qkv_bias[None], proj_weight, table)

    gain = jnp.pad(ln_gain, (0, 2 * LANES - channels))[None]
    offset = jnp.pad(ln_offset, (0, 2 * LANES - channels))[None]
    wins = cols // WIN
    unit, inv, *projected = pl.pallas_call(
        project_kernel,
        name="project",
        out_shape=(
            jax.ShapeDtypeStruct((count, 2 * LANES), f32),
            jax.ShapeDtypeStruct((count, 1), f32),
            jax.ShapeDtypeStruct((wide, count), bf16),
            jax.ShapeDtypeStruct((count, channels), bf16),
            jax.ShapeDtypeStruct((count, wide), bf16),
            jax.ShapeDtypeStruct((count, wide), bf16),
            jax.ShapeDtypeStruct((wide, count), bf16),
            jax.ShapeDtypeStruct((wide, count), bf16),
            jax.ShapeDtypeStruct((wide, count), bf16),
            jax.ShapeDtypeStruct((2, rows, WIN, 2 * LANES), f32),
        ),
        in_specs=[whole()] * 7,
        out_specs=(whole(),) * 10,
        scratch_shapes=[
            pltpu.VMEM((channels, SHIFT, cols), f32),
            pltpu.VMEM((wins, rows, WIN, 2 * LANES), f32),
        ],
        compiler_params=params,
        cost_estimate=pl.CostEstimate(flops=1000, bytes_accessed=1000, transcendentals=0),
    )(near_tokens, x_above, right, gain, offset, tok, chan)
    keep, send, *saved = pl.pallas_call(
        main_kernel,
        name="window_attention_backward",
        out_shape=(
            jax.ShapeDtypeStruct((BUFFER_ROWS // 2, LANES), bf16),
            jax.ShapeDtypeStruct((BUFFER_ROWS // 2, LANES), bf16),
            jax.ShapeDtypeStruct((3, count, channels), bf16),
            jax.ShapeDtypeStruct((wins, rows, WIN, channels), f32),
            jax.ShapeDtypeStruct((LANES, 2 * LANES), f32),
            jax.ShapeDtypeStruct((LANES, 1), f32),
        ),
        in_specs=[whole()] * 20 + [whole(pltpu.SMEM)],
        out_specs=(whole(),) * 6,
        scratch_shapes=[
            pltpu.VMEM((channels, SHIFT, cols), f32),
            pltpu.VMEM((2, rows, WIN, 2 * LANES), f32),
            pltpu.VMEM((wins, rows, WIN, 1), f32),
            pltpu.VMEM((count, channels), bf16),
            pltpu.VMEM((count, channels), bf16),
            pltpu.VMEM((wide, count), bf16),
            pltpu.VMEM((wide, count), bf16),
            pltpu.VMEM((HEADS, SPAN, LANES), f32),
            pltpu.VMEM((BUFFER_ROWS, LANES), f32),
        ],
        compiler_params=params,
    )(
        near_grad, near_ids, g_above, right, corner, gain, offset, bias, tok, chan, proj_weight, proj_slots,
        *projected, core,
    )
    saved = [*saved, unit, inv]

    mine = add(keep, from_behind(send, "col", 1))
    mine, *saved = lax.optimization_barrier((mine, *saved))
    (framed,) = pl.pallas_call(
        input_kernel,
        name="input_backward",
        out_shape=(jax.ShapeDtypeStruct((channels, rows, cols), bf16),),
        in_specs=[whole()] * 8,
        out_specs=(whole(),),
        scratch_shapes=[pltpu.VMEM((channels, rows, cols), f32)],
        compiler_params=params,
        cost_estimate=pl.CostEstimate(flops=10**9, bytes_accessed=0, transcendentals=0),
    )(*saved, gain, parts)
    below = from_behind(framed[:, :SHIFT], "row", -1)
    for pairs in exchange_steps():
        mine = add(mine, lax.ppermute(mine, ("row", "col"), pairs))
    framed = jnp.concatenate([framed[:, SHIFT:], below], 1)
    beside = from_behind(framed, "col", 1)
    d_tokens = jnp.where(jnp.arange(cols) < SHIFT, beside, framed).transpose(1, 2, 0)
    other = from_behind(mine, "col", 1)

    total_tokens = count * lax.axis_size("row") * lax.axis_size("col")
    d_weight, d_bias, d_proj, d_table, d_gain, d_offset = pl.pallas_call(
        functools.partial(finish_kernel, total_tokens ** (-0.5)),
        name="finish",
        out_shape=(
            jax.ShapeDtypeStruct(qkv_weight.shape, f32),
            jax.ShapeDtypeStruct(qkv_bias.shape, f32),
            jax.ShapeDtypeStruct(proj_weight.shape, f32),
            jax.ShapeDtypeStruct(bias_table.shape[::-1], f32),
            jax.ShapeDtypeStruct(ln_gain.shape, f32),
            jax.ShapeDtypeStruct(ln_offset.shape, f32),
        ),
        in_specs=[whole(), whole(), whole(pltpu.SMEM), whole(), whole(), whole()],
        out_specs=(whole(),) * 6,
        compiler_params=params,
    )(mine, other, core, qkv_weight, ln_gain[None], ln_offset[None])
    return (d_tokens, d_weight, d_bias, d_proj, d_table.T, d_gain, d_offset)


def solution(mesh):
    placed = (
        P(("grp", "row"), "col", None),
        P(("grp", "row"), "col", None),
        P(("grp", "row"), "col"),
        P(),
        P(),
        P(),
        P(),
        P(),
        P(),
    )
    return jax.shard_map(
        on_device,
        mesh=mesh,
        in_specs=placed,
        out_specs=(
            P(("grp", "row"), "col", None),
            P("grp", None),
            P("grp"),
            P("grp", None),
            P("grp", None),
            P("grp"),
            P("grp"),
        ),
        check_vma=False,
    )
```

```python
import functools

import jax
import jax.numpy as jnp
from jax import lax
from jax.experimental import pallas as pl
from jax.experimental.pallas import tpu as pltpu
from jax.sharding import PartitionSpec as P

HEADS = 6
WIN = 8
SHIFT = 4
SPAN = WIN * WIN
MASKED = -10000.0
LANES = 128
SLOT = 32
ROWS = 184
TABLE_ROWS = 16
BUFFER_ROWS = 6 * ROWS + TABLE_ROWS

VMEM_LIMIT = 32 * 1024 * 1024


def nn(left, right):
    return lax.dot_general(left, right, (((1,), (0,)), ((), ())), preferred_element_type=jnp.float32)


def nt(left, right):
    return lax.dot_general(left, right, (((1,), (1,)), ((), ())), preferred_element_type=jnp.float32)


def iota(shape, dim):
    return lax.broadcasted_iota(jnp.int32, shape, dim)


def table_hits(cj, lanes_first):
    shape = (LANES, 2 * LANES) if lanes_first else (2 * LANES, LANES)
    lane = iota(shape, 0 if lanes_first else 1)
    entry = iota(shape, 1 if lanes_first else 0)
    wanted = (lane // WIN) * (2 * WIN - 1) + lane % WIN + (WIN - 1) - cj
    return jnp.where((entry == wanted) & (lane < WIN * (2 * WIN - 1)), 1.0, 0.0).astype(jnp.bfloat16)


def split_three(value):
    high = value.astype(jnp.bfloat16)
    rest = value - high.astype(jnp.float32)
    middle = rest.astype(jnp.bfloat16)
    low = (rest - middle.astype(jnp.float32)).astype(jnp.bfloat16)
    return high, middle, low


def slots(rows):
    size = rows.shape[0] // HEADS
    blank = jnp.zeros((SLOT - size, rows.shape[1]), rows.dtype)
    pieces = []
    for head in range(HEADS):
        pieces += [rows[head * size : (head + 1) * size], blank]
    return jnp.concatenate(pieces, 0)


def unslot(rows, size):
    return jnp.concatenate([rows[head * SLOT : head * SLOT + size] for head in range(HEADS)], 0)


def prepare_kernel(weight_ref, offsets_ref, proj_ref, table_ref, bias_ref, tok_ref, chan_ref, proj_slots_ref, parts_ref):
    channels = weight_ref.shape[0]
    for part in range(3):
        weight = weight_ref[:, part * channels : (part + 1) * channels].astype(jnp.float32)
        parts_ref[part] = weight.astype(jnp.bfloat16)
        high, middle, low = split_three(offsets_ref[:, part * channels : (part + 1) * channels])
        full = jnp.concatenate(
            [
                weight,
                high.astype(jnp.float32),
                middle.astype(jnp.float32),
                low.astype(jnp.float32),
                jnp.zeros((256 - channels - 3, channels), jnp.float32),
            ],
            0,
        )
        turned = slots(full.T)
        chan_ref[part] = turned.astype(jnp.bfloat16)
        if part == 0:
            tok_ref[part, :, 0:channels] = full.astype(jnp.bfloat16)
            tok_ref[part, :, channels:] = jnp.zeros((256, HEADS * SLOT - channels), jnp.bfloat16)
        else:
            tok_ref[part] = turned.T.astype(jnp.bfloat16)
    proj_slots_ref[...] = slots(proj_ref[...].astype(jnp.float32)).astype(jnp.bfloat16)
    pieces = split_three(table_ref[...])
    lane = iota((8, LANES), 1)
    for cj in range(WIN):
        hits = table_hits(cj, False)
        spread = nn(pieces[0], hits) + nn(pieces[1], hits) + nn(pieces[2], hits)
        for rj in range(WIN):
            by = WIN * (WIN - 1 - rj)
            moved = spread if by == 0 else pltpu.roll(spread, LANES - by, 1)
            both = jnp.where(lane < SPAN, moved, pltpu.roll(moved, SPAN, 1))
            for head in range(HEADS):
                bias_ref[head, rj * WIN + cj : rj * WIN + cj + 1, :] = both[head : head + 1, :]


def normalize(x, channels, gain_ref, offset_ref):
    f32, bf16 = jnp.float32, jnp.bfloat16
    lane = iota((1, 2 * LANES), 1)
    center = jnp.sum(x, -1, keepdims=True) * (1.0 / channels)
    away = jnp.where(lane < channels, x - center, 0.0)
    variance = jnp.sum(away * away, -1, keepdims=True) * (1.0 / channels)
    inv_std = lax.rsqrt(variance + 1e-05)
    unit = away * inv_std
    unit_low = jnp.where(lane == channels, 1.0, unit).astype(bf16)
    normed = jnp.where(
        (lane >= channels) & (lane < channels + 3), 1.0, unit * gain_ref[...] + offset_ref[...]
    ).astype(bf16)
    return unit, inv_std, unit_low, normed


def project(normed, channels, tok_ref, chan_ref):
    bf16 = jnp.bfloat16
    scale = (channels // HEADS) ** (-0.5)
    return (
        (nn(normed, tok_ref[0, :, 0:channels]) * scale).astype(bf16),
        nn(normed, tok_ref[1]).astype(bf16),
        nn(normed, tok_ref[2]).astype(bf16),
        (nt(chan_ref[0], normed) * scale).astype(bf16),
        nt(chan_ref[1], normed).astype(bf16),
        nt(chan_ref[2], normed).astype(bf16),
    )


def project_kernel(
    tokens_ref,
    x_above_ref,
    right_ref,
    gain_ref,
    offset_ref,
    tok_ref,
    chan_ref,
    unit_ref,
    inv_ref,
    unit_turned_ref,
    q_tok_ref,
    k_tok_ref,
    v_tok_ref,
    q_chan_ref,
    k_chan_ref,
    v_chan_ref,
    x_last_ref,
    turn_s,
    x_s,
):
    rows, cols, channels = tokens_ref.shape
    wins = cols // WIN
    f32 = jnp.float32
    x_s[:, :, :, LANES:] = jnp.zeros(x_s.shape[:3] + (LANES,), f32)
    turn_s[...] = x_above_ref[...].astype(f32)
    for r in range(rows):
        if r < SHIFT:
            body = turn_s[:, r, :].T
            side = jnp.zeros((SHIFT, channels), f32)
        else:
            body = tokens_ref[r - SHIFT].astype(f32)
            side = right_ref[r - SHIFT].astype(f32)[:, 0:channels]
        row = jnp.concatenate([body[SHIFT:], side], 0)
        x_s[:, r, :, 0:channels] = row.reshape(wins, WIN, channels)
    x_last_ref[...] = x_s[wins - 2 :]
    unit, inv_std, unit_low, normed = normalize(
        x_s[...].reshape(rows * cols, 2 * LANES), channels, gain_ref, offset_ref
    )
    unit_ref[...] = unit
    inv_ref[...] = inv_std
    unit_turned_ref[...] = unit_low.T[0 : unit_turned_ref.shape[0]]
    results = project(normed, channels, tok_ref, chan_ref)
    for target, value in zip(
        (q_tok_ref, k_tok_ref, v_tok_ref, q_chan_ref, k_chan_ref, v_chan_ref), results
    ):
        target[...] = value


def main_kernel(
    grad_ref,
    region_ref,
    g_above_ref,
    right_ref,
    corner_ref,
    gain_ref,
    offset_ref,
    bias_ref,
    tok_ref,
    chan_ref,
    proj_ref,
    proj_slots_ref,
    unit_turned_ref,
    q_tok_ref,
    k_tok_ref,
    v_tok_ref,
    q_chan_ref,
    k_chan_ref,
    v_chan_ref,
    x_last_ref,
    core_ref,
    keep_ref,
    send_ref,
    d_qkv_s,
    g_s,
    unit_last_ref,
    inv_last_ref,
    turn_s,
    x_last_s,
    id_s,
    grad_s,
    da_tok_s,
    da_chan_s,
    attended_s,
    score_s,
    pack_s,
):
    rows, cols, channels = grad_ref.shape
    head_size = channels // HEADS
    scale = head_size ** (-0.5)
    count = rows * cols
    wins = cols // WIN
    f32 = jnp.float32
    bf16 = jnp.bfloat16

    turn_s[...] = g_above_ref[...].astype(f32)
    x_last_s[...] = x_last_ref[...]
    ids = region_ref[...].astype(f32).T
    at_id = slice(2 * channels, 2 * channels + 1)
    col_part = ids[:, 0:1] - 4.0 * jnp.floor(ids[:, 0:1] * 0.25)
    for r in range(rows):
        if r >= SHIFT:
            g_body = grad_ref[r - SHIFT].astype(f32)
            side = right_ref[r - SHIFT].astype(f32)
            id_body = ids[:, r - SHIFT : r - SHIFT + 1]
        else:
            g_body = turn_s[:, r, :].T
            side = corner_ref[r].astype(f32)
            id_body = col_part + 4.0 * jnp.floor(side[0:1, at_id] * 0.25)
            x_last_s[1, r, SHIFT:, 0:channels] = side[:, 0:channels]
        g_row = jnp.concatenate([g_body[SHIFT:], side[:, channels : 2 * channels]], 0)
        id_row = jnp.concatenate([id_body[SHIFT:], side[:, at_id]], 0)
        g_s[:, r, :, :] = g_row.reshape(wins, WIN, channels)
        id_s[:, r, :, :] = id_row.reshape(wins, WIN, 1)
    grad_s[...] = g_s[...].reshape(count, channels).astype(bf16)

    unit_last, inv_last, unit_low, normed = normalize(
        x_last_s[...].reshape(LANES, 2 * LANES), channels, gain_ref, offset_ref
    )
    unit_last_ref[...] = unit_last
    inv_last_ref[...] = inv_last
    last = project(normed, channels, tok_ref, chan_ref)
    da_tok_s[...] = nt(grad_s[...], proj_ref[...]).astype(bf16)
    da_chan_s[...] = nt(proj_slots_ref[...], grad_s[...]).astype(bf16)

    score_s[...] = jnp.zeros(score_s.shape, f32)
    first = iota((1, LANES), 1) < SPAN
    first_low = jnp.where(first, 1.0, 0.0).astype(bf16)
    second_low = jnp.where(first, 0.0, 1.0).astype(bf16)
    head_of = iota((1, channels), 1) // head_size
    id_lane = iota((1, LANES), 1).astype(f32)

    def pack(square):
        return jnp.where(first, square[0:SPAN], square[SPAN:])

    def spread(packed):
        low = packed.astype(bf16)
        return jnp.concatenate([low * first_low, low * second_low], 0)

    def in_blocks(chan):
        blank = jnp.zeros((SLOT, LANES), bf16)
        lines = []
        for head in range(HEADS):
            line = [blank] * HEADS
            line[head] = chan[head * SLOT : (head + 1) * SLOT]
            lines.append(jnp.concatenate(line, 1))
        return jnp.concatenate(lines, 0)

    def by_head(tok):
        return jnp.concatenate(
            [jnp.where(head_of == head, tok, jnp.zeros_like(tok)) for head in range(HEADS)], 0
        )

    for pair in range(count // LANES):
        at = slice(pair * LANES, (pair + 1) * LANES)
        if (pair + 1) * LANES == count:
            q_tok, k_tok, v_tok, q_chan, k_chan, v_chan = last
        else:
            q_tok, k_tok, v_tok = q_tok_ref[at, :], k_tok_ref[at, :], v_tok_ref[at, :]
            q_chan, k_chan, v_chan = q_chan_ref[:, at], k_chan_ref[:, at], v_chan_ref[:, at]
        hot = jnp.where(id_s[pair * 2 : pair * 2 + 2].reshape(LANES, 1) == id_lane, 1.0, 0.0).astype(bf16)
        match = pack(nt(hot, hot)) > 0.5
        scores = nn(k_tok, in_blocks(q_chan))
        d_prob = nn(v_tok, in_blocks(da_chan_s[:, at]))
        attended = []
        d_query = []
        probs = []
        d_scores = []
        for head in range(HEADS):
            here = slice(head * LANES, (head + 1) * LANES)
            band = slice(head * SLOT, (head + 1) * SLOT)
            score = jnp.where(match, pack(scores[:, here]) + bias_ref[head], MASKED)
            power = jnp.exp(score - jnp.max(score, 0, keepdims=True))
            prob = power * (1.0 / jnp.sum(power, 0, keepdims=True))
            gradient = pack(d_prob[:, here])
            d_score = prob * (gradient - jnp.sum(prob * gradient, 0, keepdims=True))
            score_s[head] += d_score
            prob_low = spread(prob)
            d_low = spread(d_score)
            attended.append(nn(v_chan[band], prob_low))
            d_query.append(nn(k_chan[band], d_low) * scale)
            probs.append(prob_low)
            d_scores.append(d_low)
        attended_s[:, at] = jnp.concatenate(attended, 0).astype(bf16)
        d_query = jnp.concatenate([piece[0:head_size] for piece in d_query], 0)
        d_qkv_s[0, at, :] = d_query.T.astype(bf16)
        d_qkv_s[1, at, :] = nn(jnp.concatenate(d_scores, 1), by_head(q_tok)).astype(bf16)
        d_qkv_s[2, at, :] = nn(jnp.concatenate(probs, 1), by_head(da_tok_s[at, :])).astype(bf16)

    unit_turned = jnp.concatenate([unit_turned_ref[:, : count - LANES], unit_low.T[0 : unit_turned_ref.shape[0]]], 1)
    rest = channels - LANES
    pieces = [nn(unit_turned, d_qkv_s[part])[0:ROWS] for part in range(3)]
    d_proj = nn(attended_s[...], grad_s[...])
    pieces.append(
        jnp.concatenate([unslot(d_proj, head_size), jnp.zeros((ROWS - channels, channels), f32)], 0)
    )
    pack_s[...] = jnp.zeros(pack_s.shape, f32)
    for at, piece in enumerate(pieces):
        pack_s[at * ROWS : (at + 1) * ROWS, :] = piece[:, 0:LANES]
        low = (4 + at // 2) * ROWS
        side = (at % 2) * SPAN
        pack_s[low : low + ROWS, side : side + rest] = piece[:, LANES:]
    lines = []
    for head in range(HEADS):
        both = score_s[head]
        both = jnp.where(first, both + pltpu.roll(both, SPAN, 1), 0.0)
        line = both[(WIN - 1) * WIN :]
        for rj in range(WIN - 1):
            line += pltpu.roll(both[rj * WIN : (rj + 1) * WIN], WIN * (WIN - 1 - rj), 1)
        lines.append(line)
    lines = jnp.concatenate(lines, 0)
    high = lines.astype(bf16)
    low = (lines - high.astype(f32)).astype(bf16)
    cj_of = iota((HEADS * WIN, 1), 0) % WIN
    table = jnp.zeros((HEADS * WIN, 2 * LANES), f32)
    for cj in range(WIN):
        hits = table_hits(cj, True)
        table += jnp.where(cj_of == cj, nn(high, hits) + nn(low, hits), 0.0)
    table = table.reshape(HEADS, WIN, 2 * LANES).sum(1)
    pack_s[6 * ROWS : 6 * ROWS + HEADS, :] = table[:, 0:LANES]
    pack_s[6 * ROWS + 8 : 6 * ROWS + 8 + HEADS, :] = table[:, LANES:]
    half = keep_ref.shape[0]
    low_half = pack_s[0:half, :].astype(bf16)
    high_half = pack_s[half:, :].astype(bf16)
    lower = core_ref[0] == 0
    keep_ref[...] = jnp.where(lower, low_half, high_half)
    send_ref[...] = jnp.where(lower, high_half, low_half)


def input_kernel(
    d_qkv_ref, g_ref, unit_last_ref, inv_last_ref, unit_ref, inv_ref, gain_ref, parts_ref, framed_ref, turn_s
):
    wins, rows, _, channels = g_ref.shape
    cols = wins * WIN
    f32 = jnp.float32
    d_normed = sum(nt(d_qkv_ref[part], parts_ref[part]) for part in range(3))
    scaled = d_normed * gain_ref[:, 0:channels]
    unit = jnp.concatenate([unit_ref[:-LANES, 0:channels], unit_last_ref[:, 0:channels]], 0)
    inv_std = jnp.concatenate([inv_ref[:-LANES], inv_last_ref[...]], 0)
    mean_one = jnp.sum(scaled, -1, keepdims=True) * (1.0 / channels)
    mean_two = jnp.sum(scaled * unit, -1, keepdims=True) * (1.0 / channels)
    d_input = inv_std * (scaled - mean_one - unit * mean_two)
    done = g_ref[...] + d_input.reshape(g_ref.shape)
    for r in range(rows):
        row = done[:, r].reshape(cols, channels)
        row = jnp.concatenate([row[cols - SHIFT :], row[: cols - SHIFT]], 0)
        turn_s[:, r, :] = row.T
    framed_ref[...] = turn_s[...].astype(framed_ref.dtype)


def finish_kernel(
    out_scale,
    mine_ref,
    other_ref,
    core_ref,
    weight_ref,
    gain_ref,
    offset_ref,
    d_weight_ref,
    d_bias_ref,
    d_proj_ref,
    d_table_ref,
    d_gain_ref,
    d_offset_ref,
):
    channels = weight_ref.shape[0]
    f32 = jnp.float32
    rest = channels - LANES
    mine = mine_ref[...].astype(f32)
    other = other_ref[...].astype(f32)
    here = core_ref[0] == 0
    low = jnp.where(here, mine, other)
    high = jnp.where(here, other, mine)
    both = jnp.concatenate([low, high], 0) * out_scale
    pieces = []
    for at in range(4):
        row = (4 + at // 2) * ROWS
        side = (at % 2) * SPAN
        pieces.append(
            jnp.concatenate(
                [both[at * ROWS : (at + 1) * ROWS, :], both[row : row + ROWS, side : side + rest]], 1
            )
        )
    gain = gain_ref[...]
    offset = offset_ref[...]
    ones = jnp.ones((8, channels), jnp.bfloat16)
    products = jnp.zeros((channels, channels), f32)
    d_offset = jnp.zeros((8, channels), f32)
    biases = []
    for part in range(3):
        across = slice(part * channels, (part + 1) * channels)
        unit = pieces[part][0:channels]
        bias = pieces[part][channels : channels + 1]
        weight = weight_ref[:, across]
        d_weight_ref[:, across] = gain * unit + offset * bias
        biases.append(bias)
        products += weight.astype(f32) * unit
        for term in split_three(bias):
            d_offset += nt(jnp.broadcast_to(term, (8, channels)), weight)
    d_bias_ref[...] = jnp.concatenate(biases, 1).reshape(d_bias_ref.shape)
    d_gain = sum(nt(ones, term) for term in split_three(products))
    d_gain_ref[...] = d_gain[0:1].reshape(channels)
    d_offset_ref[...] = d_offset[0:1].reshape(channels)
    d_proj_ref[...] = pieces[3][0:channels]
    table = jnp.concatenate([both[6 * ROWS : 6 * ROWS + 8], both[6 * ROWS + 8 :]], 1)
    d_table_ref[...] = table[0:HEADS, 0 : d_table_ref.shape[1]]


def whole(memory_space=pltpu.VMEM):
    return pl.BlockSpec(memory_space=memory_space)


def from_behind(shard, axis, by):
    count = lax.axis_size(axis)
    return lax.ppermute(shard, axis, [(i, (i + by) % count) for i in range(count)])


def diagonal(shard):
    rows, cols = lax.axis_size("row"), lax.axis_size("col")
    pairs = [
        (r * cols + c, ((r + 1) % rows) * cols + (c - 1) % cols) for r in range(rows) for c in range(cols)
    ]
    return lax.ppermute(shard, ("row", "col"), pairs)


def exchange_steps():
    rows, cols = lax.axis_size("row"), lax.axis_size("col")
    steps = [1 << bit for bit in range((rows - 1).bit_length())]
    for at in range(len(steps)):
        yield [
            (r * cols + c, (r ^ steps[(at - 1 - c) % len(steps)]) * cols + c) for r in range(rows) for c in range(cols)
        ]


def add(left, right):
    return (left.astype(jnp.float32) + right.astype(jnp.float32)).astype(jnp.bfloat16)


def on_device(
    tokens, grad_out, regions, ln_gain, ln_offset, qkv_weight, qkv_bias, proj_weight, bias_table
):
    rows, cols, channels = tokens.shape
    f32, bf16 = jnp.float32, jnp.bfloat16
    count = rows * cols
    params = pltpu.CompilerParams(vmem_limit_bytes=VMEM_LIMIT)

    x_turned = tokens.transpose(2, 0, 1)
    g_turned = grad_out.transpose(2, 0, 1)
    core = lax.axis_index("col").astype(jnp.int32).reshape(1)

    x_above = from_behind(x_turned[:, rows - SHIFT :], "row", 1)
    g_rows, near_tokens, near_grad, near_ids = lax.optimization_barrier(
        (g_turned[:, rows - SHIFT :], tokens, grad_out, regions)
    )
    g_above = from_behind(g_rows, "row", 1)

    def border(row_slice):
        return jnp.concatenate(
            [
                near_tokens[row_slice, :SHIFT],
                near_grad[row_slice, :SHIFT],
                near_ids[row_slice, :SHIFT, None].astype(bf16),
            ],
            -1,
        )

    right = from_behind(border(slice(0, rows - SHIFT)), "col", -1)
    corner = diagonal(border(slice(rows - SHIFT, None)))

    table = jnp.pad(bias_table.T, ((0, 8 - HEADS), (0, 2 * LANES - bias_table.shape[0])))
    wide = HEADS * SLOT
    bias, tok, chan, proj_slots, parts = pl.pallas_call(
        prepare_kernel,
        name="prepare",
        out_shape=(
            jax.ShapeDtypeStruct((HEADS, SPAN, LANES), f32),
            jax.ShapeDtypeStruct((3, 2 * LANES, wide), bf16),
            jax.ShapeDtypeStruct((3, wide, 2 * LANES), bf16),
            jax.ShapeDtypeStruct((wide, channels), bf16),
            jax.ShapeDtypeStruct((3, channels, channels), bf16),
        ),
        in_specs=[whole()] * 4,
        out_specs=(whole(),) * 5,
        compiler_params=params,
        cost_estimate=pl.CostEstimate(flops=1000, bytes_accessed=1000, transcendentals=0),
    )(qkv_weight, qkv_bias[None], proj_weight, table)

    gain = jnp.pad(ln_gain, (0, 2 * LANES - channels))[None]
    offset = jnp.pad(ln_offset, (0, 2 * LANES - channels))[None]
    wins = cols // WIN
    unit, inv, *projected = pl.pallas_call(
        project_kernel,
        name="project",
        out_shape=(
            jax.ShapeDtypeStruct((count, 2 * LANES), f32),
            jax.ShapeDtypeStruct((count, 1), f32),
            jax.ShapeDtypeStruct((wide, count), bf16),
            jax.ShapeDtypeStruct((count, channels), bf16),
            jax.ShapeDtypeStruct((count, wide), bf16),
            jax.ShapeDtypeStruct((count, wide), bf16),
            jax.ShapeDtypeStruct((wide, count), bf16),
            jax.ShapeDtypeStruct((wide, count), bf16),
            jax.ShapeDtypeStruct((wide, count), bf16),
            jax.ShapeDtypeStruct((2, rows, WIN, 2 * LANES), f32),
        ),
        in_specs=[whole()] * 7,
        out_specs=(whole(),) * 10,
        scratch_shapes=[
            pltpu.VMEM((channels, SHIFT, cols), f32),
            pltpu.VMEM((wins, rows, WIN, 2 * LANES), f32),
        ],
        compiler_params=params,
        cost_estimate=pl.CostEstimate(flops=1000, bytes_accessed=1000, transcendentals=0),
    )(near_tokens, x_above, right, gain, offset, tok, chan)
    keep, send, *saved = pl.pallas_call(
        main_kernel,
        name="window_attention_backward",
        out_shape=(
            jax.ShapeDtypeStruct((BUFFER_ROWS // 2, LANES), bf16),
            jax.ShapeDtypeStruct((BUFFER_ROWS // 2, LANES), bf16),
            jax.ShapeDtypeStruct((3, count, channels), bf16),
            jax.ShapeDtypeStruct((wins, rows, WIN, channels), f32),
            jax.ShapeDtypeStruct((LANES, 2 * LANES), f32),
            jax.ShapeDtypeStruct((LANES, 1), f32),
        ),
        in_specs=[whole()] * 20 + [whole(pltpu.SMEM)],
        out_specs=(whole(),) * 6,
        scratch_shapes=[
            pltpu.VMEM((channels, SHIFT, cols), f32),
            pltpu.VMEM((2, rows, WIN, 2 * LANES), f32),
            pltpu.VMEM((wins, rows, WIN, 1), f32),
            pltpu.VMEM((count, channels), bf16),
            pltpu.VMEM((count, channels), bf16),
            pltpu.VMEM((wide, count), bf16),
            pltpu.VMEM((wide, count), bf16),
            pltpu.VMEM((HEADS, SPAN, LANES), f32),
            pltpu.VMEM((BUFFER_ROWS, LANES), f32),
        ],
        compiler_params=params,
    )(
        near_grad, near_ids, g_above, right, corner, gain, offset, bias, tok, chan, proj_weight, proj_slots,
        *projected, core,
    )
    saved = [*saved, unit, inv]

    mine = add(keep, from_behind(send, "col", 1))
    mine, *saved = lax.optimization_barrier((mine, *saved))
    (framed,) = pl.pallas_call(
        input_kernel,
        name="input_backward",
        out_shape=(jax.ShapeDtypeStruct((channels, rows, cols), bf16),),
        in_specs=[whole()] * 8,
        out_specs=(whole(),),
        scratch_shapes=[pltpu.VMEM((channels, rows, cols), f32)],
        compiler_params=params,
        cost_estimate=pl.CostEstimate(flops=10**9, bytes_accessed=0, transcendentals=0),
    )(*saved, gain, parts)
    below = from_behind(framed[:, :SHIFT], "row", -1)
    for pairs in exchange_steps():
        mine = add(mine, lax.ppermute(mine, ("row", "col"), pairs))
    framed = jnp.concatenate([framed[:, SHIFT:], below], 1)
    beside = from_behind(framed, "col", 1)
    d_tokens = jnp.where(jnp.arange(cols) < SHIFT, beside, framed).transpose(1, 2, 0)
    other = from_behind(mine, "col", 1)

    total_tokens = count * lax.axis_size("row") * lax.axis_size("col")
    d_weight, d_bias, d_proj, d_table, d_gain, d_offset = pl.pallas_call(
        functools.partial(finish_kernel, total_tokens ** (-0.5)),
        name="finish",
        out_shape=(
            jax.ShapeDtypeStruct(qkv_weight.shape, f32),
            jax.ShapeDtypeStruct(qkv_bias.shape, f32),
            jax.ShapeDtypeStruct(proj_weight.shape, f32),
            jax.ShapeDtypeStruct(bias_table.shape[::-1], f32),
            jax.ShapeDtypeStruct(ln_gain.shape, f32),
            jax.ShapeDtypeStruct(ln_offset.shape, f32),
        ),
        in_specs=[whole(), whole(), whole(pltpu.SMEM), whole(), whole(), whole()],
        out_specs=(whole(),) * 6,
        compiler_params=params,
    )(mine, other, core, qkv_weight, ln_gain[:, None], ln_offset[:, None])
    return (d_tokens, d_weight, d_bias, d_proj, d_table.T, d_gain, d_offset)


def solution(mesh):
    placed = (
        P(("grp", "row"), "col", None),
        P(("grp", "row"), "col", None),
        P(("grp", "row"), "col"),
        P(),
        P(),
        P(),
        P(),
        P(),
        P(),
    )
    return jax.shard_map(
        on_device,
        mesh=mesh,
        in_specs=placed,
        out_specs=(
            P(("grp", "row"), "col", None),
            P("grp", None),
            P("grp"),
            P("grp", None),
            P("grp", None),
            P("grp"),
            P("grp"),
        ),
        check_vma=False,
    )
```

```python
import functools

import jax
import jax.numpy as jnp
from jax import lax
from jax.experimental import pallas as pl
from jax.experimental.pallas import tpu as pltpu
from jax.sharding import PartitionSpec as P

HEADS = 6
WIN = 8
SHIFT = 4
SPAN = WIN * WIN
MASKED = -10000.0
LANES = 128
SLOT = 32
ROWS = 184
TABLE_ROWS = 16
BUFFER_ROWS = 6 * ROWS + TABLE_ROWS

VMEM_LIMIT = 32 * 1024 * 1024


def nn(left, right):
    return lax.dot_general(left, right, (((1,), (0,)), ((), ())), preferred_element_type=jnp.float32)


def nt(left, right):
    return lax.dot_general(left, right, (((1,), (1,)), ((), ())), preferred_element_type=jnp.float32)


def iota(shape, dim):
    return lax.broadcasted_iota(jnp.int32, shape, dim)


def table_hits(cj, lanes_first):
    shape = (LANES, 2 * LANES) if lanes_first else (2 * LANES, LANES)
    lane = iota(shape, 0 if lanes_first else 1)
    entry = iota(shape, 1 if lanes_first else 0)
    wanted = (lane // WIN) * (2 * WIN - 1) + lane % WIN + (WIN - 1) - cj
    return jnp.where((entry == wanted) & (lane < WIN * (2 * WIN - 1)), 1.0, 0.0).astype(jnp.bfloat16)


def split_three(value):
    high = value.astype(jnp.bfloat16)
    rest = value - high.astype(jnp.float32)
    middle = rest.astype(jnp.bfloat16)
    low = (rest - middle.astype(jnp.float32)).astype(jnp.bfloat16)
    return high, middle, low


def slots(rows):
    size = rows.shape[0] // HEADS
    blank = jnp.zeros((SLOT - size, rows.shape[1]), rows.dtype)
    pieces = []
    for head in range(HEADS):
        pieces += [rows[head * size : (head + 1) * size], blank]
    return jnp.concatenate(pieces, 0)


def unslot(rows, size):
    return jnp.concatenate([rows[head * SLOT : head * SLOT + size] for head in range(HEADS)], 0)


def prepare_kernel(weight_ref, offsets_ref, proj_ref, table_ref, bias_ref, tok_ref, chan_ref, proj_slots_ref, parts_ref):
    channels = weight_ref.shape[0]
    for part in range(3):
        weight = weight_ref[:, part * channels : (part + 1) * channels].astype(jnp.float32)
        parts_ref[part] = weight.astype(jnp.bfloat16)
        high, middle, low = split_three(offsets_ref[:, part * channels : (part + 1) * channels])
        full = jnp.concatenate(
            [
                weight,
                high.astype(jnp.float32),
                middle.astype(jnp.float32),
                low.astype(jnp.float32),
                jnp.zeros((256 - channels - 3, channels), jnp.float32),
            ],
            0,
        )
        turned = slots(full.T)
        chan_ref[part] = turned.astype(jnp.bfloat16)
        if part == 0:
            tok_ref[part, :, 0:channels] = full.astype(jnp.bfloat16)
            tok_ref[part, :, channels:] = jnp.zeros((256, HEADS * SLOT - channels), jnp.bfloat16)
        else:
            tok_ref[part] = turned.T.astype(jnp.bfloat16)
    proj_slots_ref[...] = slots(proj_ref[...].astype(jnp.float32)).astype(jnp.bfloat16)
    pieces = split_three(table_ref[...])
    lane = iota((8, LANES), 1)
    for cj in range(WIN):
        hits = table_hits(cj, False)
        spread = nn(pieces[0], hits) + nn(pieces[1], hits) + nn(pieces[2], hits)
        for rj in range(WIN):
            by = WIN * (WIN - 1 - rj)
            moved = spread if by == 0 else pltpu.roll(spread, LANES - by, 1)
            both = jnp.where(lane < SPAN, moved, pltpu.roll(moved, SPAN, 1))
            for head in range(HEADS):
                bias_ref[head, rj * WIN + cj : rj * WIN + cj + 1, :] = both[head : head + 1, :]


def normalize(x, channels, gain_ref, offset_ref):
    f32, bf16 = jnp.float32, jnp.bfloat16
    lane = iota((1, 2 * LANES), 1)
    center = jnp.sum(x, -1, keepdims=True) * (1.0 / channels)
    away = jnp.where(lane < channels, x - center, 0.0)
    variance = jnp.sum(away * away, -1, keepdims=True) * (1.0 / channels)
    inv_std = lax.rsqrt(variance + 1e-05)
    unit = away * inv_std
    unit_low = jnp.where(lane == channels, 1.0, unit).astype(bf16)
    normed = jnp.where(
        (lane >= channels) & (lane < channels + 3), 1.0, unit * gain_ref[...] + offset_ref[...]
    ).astype(bf16)
    return unit, inv_std, unit_low, normed


def project(normed, channels, tok_ref, chan_ref):
    bf16 = jnp.bfloat16
    scale = (channels // HEADS) ** (-0.5)
    return (
        (nn(normed, tok_ref[0, :, 0:channels]) * scale).astype(bf16),
        nn(normed, tok_ref[1]).astype(bf16),
        nn(normed, tok_ref[2]).astype(bf16),
        (nt(chan_ref[0], normed) * scale).astype(bf16),
        nt(chan_ref[1], normed).astype(bf16),
        nt(chan_ref[2], normed).astype(bf16),
    )


def project_kernel(
    tokens_ref,
    x_above_ref,
    right_ref,
    gain_ref,
    offset_ref,
    tok_ref,
    chan_ref,
    unit_ref,
    inv_ref,
    unit_turned_ref,
    q_tok_ref,
    k_tok_ref,
    v_tok_ref,
    q_chan_ref,
    k_chan_ref,
    v_chan_ref,
    x_last_ref,
    turn_s,
    x_s,
):
    rows, cols, channels = tokens_ref.shape
    wins = cols // WIN
    f32 = jnp.float32
    x_s[:, :, :, LANES:] = jnp.zeros(x_s.shape[:3] + (LANES,), f32)
    turn_s[...] = x_above_ref[...].astype(f32)
    for r in range(rows):
        if r < SHIFT:
            body = turn_s[:, r, :].T
            side = jnp.zeros((SHIFT, channels), f32)
        else:
            body = tokens_ref[r - SHIFT].astype(f32)
            side = right_ref[r - SHIFT].astype(f32)[:, 0:channels]
        row = jnp.concatenate([body[SHIFT:], side], 0)
        x_s[:, r, :, 0:channels] = row.reshape(wins, WIN, channels)
    x_last_ref[...] = x_s[wins - 2 :]
    unit, inv_std, unit_low, normed = normalize(
        x_s[...].reshape(rows * cols, 2 * LANES), channels, gain_ref, offset_ref
    )
    unit_ref[...] = unit
    inv_ref[...] = inv_std
    unit_turned_ref[...] = unit_low.T[0 : unit_turned_ref.shape[0]]
    results = project(normed, channels, tok_ref, chan_ref)
    for target, value in zip(
        (q_tok_ref, k_tok_ref, v_tok_ref, q_chan_ref, k_chan_ref, v_chan_ref), results
    ):
        target[...] = value


def main_kernel(
    grad_ref,
    region_ref,
    g_above_ref,
    right_ref,
    corner_ref,
    gain_ref,
    offset_ref,
    bias_ref,
    tok_ref,
    chan_ref,
    proj_ref,
    proj_slots_ref,
    unit_turned_ref,
    q_tok_ref,
    k_tok_ref,
    v_tok_ref,
    q_chan_ref,
    k_chan_ref,
    v_chan_ref,
    x_last_ref,
    core_ref,
    keep_ref,
    send_ref,
    d_qkv_s,
    g_s,
    unit_last_ref,
    inv_last_ref,
    turn_s,
    x_last_s,
    id_s,
    grad_s,
    da_tok_s,
    da_chan_s,
    attended_s,
    score_s,
    pack_s,
):
    rows, cols, channels = grad_ref.shape
    head_size = channels // HEADS
    scale = head_size ** (-0.5)
    count = rows * cols
    wins = cols // WIN
    f32 = jnp.float32
    bf16 = jnp.bfloat16

    turn_s[...] = g_above_ref[...].astype(f32)
    x_last_s[...] = x_last_ref[...]
    ids = region_ref[...].astype(f32).T
    at_id = slice(2 * channels, 2 * channels + 1)
    col_part = ids[:, 0:1] - 4.0 * jnp.floor(ids[:, 0:1] * 0.25)
    for r in range(rows):
        if r >= SHIFT:
            g_body = grad_ref[r - SHIFT].astype(f32)
            side = right_ref[r - SHIFT].astype(f32)
            id_body = ids[:, r - SHIFT : r - SHIFT + 1]
        else:
            g_body = turn_s[:, r, :].T
            side = corner_ref[r].astype(f32)
            id_body = col_part + 4.0 * jnp.floor(side[0:1, at_id] * 0.25)
            x_last_s[1, r, SHIFT:, 0:channels] = side[:, 0:channels]
        g_row = jnp.concatenate([g_body[SHIFT:], side[:, channels : 2 * channels]], 0)
        id_row = jnp.concatenate([id_body[SHIFT:], side[:, at_id]], 0)
        g_s[:, r, :, :] = g_row.reshape(wins, WIN, channels)
        id_s[:, r, :, :] = id_row.reshape(wins, WIN, 1)
    grad_s[...] = g_s[...].reshape(count, channels).astype(bf16)

    unit_last, inv_last, unit_low, normed = normalize(
        x_last_s[...].reshape(LANES, 2 * LANES), channels, gain_ref, offset_ref
    )
    unit_last_ref[...] = unit_last
    inv_last_ref[...] = inv_last
    last = project(normed, channels, tok_ref, chan_ref)
    da_tok_s[...] = nt(grad_s[...], proj_ref[...]).astype(bf16)
    da_chan_s[...] = nt(proj_slots_ref[...], grad_s[...]).astype(bf16)

    score_s[...] = jnp.zeros(score_s.shape, f32)
    first = iota((1, LANES), 1) < SPAN
    first_low = jnp.where(first, 1.0, 0.0).astype(bf16)
    second_low = jnp.where(first, 0.0, 1.0).astype(bf16)
    head_of = iota((1, channels), 1) // head_size
    id_lane = iota((1, LANES), 1).astype(f32)

    def pack(square):
        return jnp.where(first, square[0:SPAN], square[SPAN:])

    def spread(packed):
        low = packed.astype(bf16)
        return jnp.concatenate([low * first_low, low * second_low], 0)

    def in_blocks(chan):
        blank = jnp.zeros((SLOT, LANES), bf16)
        lines = []
        for head in range(HEADS):
            line = [blank] * HEADS
            line[head] = chan[head * SLOT : (head + 1) * SLOT]
            lines.append(jnp.concatenate(line, 1))
        return jnp.concatenate(lines, 0)

    def by_head(tok):
        return jnp.concatenate(
            [jnp.where(head_of == head, tok, jnp.zeros_like(tok)) for head in range(HEADS)], 0
        )

    for pair in range(count // LANES):
        at = slice(pair * LANES, (pair + 1) * LANES)
        if (pair + 1) * LANES == count:
            q_tok, k_tok, v_tok, q_chan, k_chan, v_chan = last
        else:
            q_tok, k_tok, v_tok = q_tok_ref[at, :], k_tok_ref[at, :], v_tok_ref[at, :]
            q_chan, k_chan, v_chan = q_chan_ref[:, at], k_chan_ref[:, at], v_chan_ref[:, at]
        hot = jnp.where(id_s[pair * 2 : pair * 2 + 2].reshape(LANES, 1) == id_lane, 1.0, 0.0).astype(bf16)
        match = pack(nt(hot, hot)) > 0.5
        scores = nn(k_tok, in_blocks(q_chan))
        d_prob = nn(v_tok, in_blocks(da_chan_s[:, at]))
        attended = []
        d_query = []
        probs = []
        d_scores = []
        for head in range(HEADS):
            here = slice(head * LANES, (head + 1) * LANES)
            band = slice(head * SLOT, (head + 1) * SLOT)
            score = jnp.where(match, pack(scores[:, here]) + bias_ref[head], MASKED)
            power = jnp.exp(score - jnp.max(score, 0, keepdims=True))
            prob = power * (1.0 / jnp.sum(power, 0, keepdims=True))
            gradient = pack(d_prob[:, here])
            d_score = prob * (gradient - jnp.sum(prob * gradient, 0, keepdims=True))
            score_s[head] += d_score
            prob_low = spread(prob)
            d_low = spread(d_score)
            attended.append(nn(v_chan[band], prob_low))
            d_query.append(nn(k_chan[band], d_low) * scale)
            probs.append(prob_low)
            d_scores.append(d_low)
        attended_s[:, at] = jnp.concatenate(attended, 0).astype(bf16)
        d_query = jnp.concatenate([piece[0:head_size] for piece in d_query], 0)
        d_qkv_s[0, at, :] = d_query.T.astype(bf16)
        d_qkv_s[1, at, :] = nn(jnp.concatenate(d_scores, 1), by_head(q_tok)).astype(bf16)
        d_qkv_s[2, at, :] = nn(jnp.concatenate(probs, 1), by_head(da_tok_s[at, :])).astype(bf16)

    unit_turned = jnp.concatenate([unit_turned_ref[:, : count - LANES], unit_low.T[0 : unit_turned_ref.shape[0]]], 1)
    rest = channels - LANES
    pieces = [nn(unit_turned, d_qkv_s[part])[0:ROWS] for part in range(3)]
    d_proj = nn(attended_s[...], grad_s[...])
    pieces.append(
        jnp.concatenate([unslot(d_proj, head_size), jnp.zeros((ROWS - channels, channels), f32)], 0)
    )
    pack_s[...] = jnp.zeros(pack_s.shape, f32)
    for at, piece in enumerate(pieces):
        pack_s[at * ROWS : (at + 1) * ROWS, :] = piece[:, 0:LANES]
        low = (4 + at // 2) * ROWS
        side = (at % 2) * SPAN
        pack_s[low : low + ROWS, side : side + rest] = piece[:, LANES:]
    lines = []
    for head in range(HEADS):
        both = score_s[head]
        both = jnp.where(first, both + pltpu.roll(both, SPAN, 1), 0.0)
        line = both[(WIN - 1) * WIN :]
        for rj in range(WIN - 1):
            line += pltpu.roll(both[rj * WIN : (rj + 1) * WIN], WIN * (WIN - 1 - rj), 1)
        lines.append(line)
    lines = jnp.concatenate(lines, 0)
    high = lines.astype(bf16)
    low = (lines - high.astype(f32)).astype(bf16)
    cj_of = iota((HEADS * WIN, 1), 0) % WIN
    table = jnp.zeros((HEADS * WIN, 2 * LANES), f32)
    for cj in range(WIN):
        hits = table_hits(cj, True)
        table += jnp.where(cj_of == cj, nn(high, hits) + nn(low, hits), 0.0)
    table = table.reshape(HEADS, WIN, 2 * LANES).sum(1)
    pack_s[6 * ROWS : 6 * ROWS + HEADS, :] = table[:, 0:LANES]
    pack_s[6 * ROWS + 8 : 6 * ROWS + 8 + HEADS, :] = table[:, LANES:]
    half = keep_ref.shape[0]
    low_half = pack_s[0:half, :].astype(bf16)
    high_half = pack_s[half:, :].astype(bf16)
    lower = core_ref[0] == 0
    keep_ref[...] = jnp.where(lower, low_half, high_half)
    send_ref[...] = jnp.where(lower, high_half, low_half)


def input_kernel(
    d_qkv_ref, g_ref, unit_last_ref, inv_last_ref, unit_ref, inv_ref, gain_ref, parts_ref, framed_ref, turn_s
):
    wins, rows, _, channels = g_ref.shape
    cols = wins * WIN
    f32 = jnp.float32
    d_normed = sum(nt(d_qkv_ref[part], parts_ref[part]) for part in range(3))
    scaled = d_normed * gain_ref[:, 0:channels]
    unit = jnp.concatenate([unit_ref[:-LANES, 0:channels], unit_last_ref[:, 0:channels]], 0)
    inv_std = jnp.concatenate([inv_ref[:-LANES], inv_last_ref[...]], 0)
    mean_one = jnp.sum(scaled, -1, keepdims=True) * (1.0 / channels)
    mean_two = jnp.sum(scaled * unit, -1, keepdims=True) * (1.0 / channels)
    d_input = inv_std * (scaled - mean_one - unit * mean_two)
    done = g_ref[...] + d_input.reshape(g_ref.shape)
    for r in range(rows):
        row = done[:, r].reshape(cols, channels)
        row = jnp.concatenate([row[cols - SHIFT :], row[: cols - SHIFT]], 0)
        turn_s[:, r, :] = row.T
    framed_ref[...] = turn_s[...].astype(framed_ref.dtype)


def finish_kernel(
    out_scale,
    mine_ref,
    other_ref,
    core_ref,
    weight_ref,
    gain_ref,
    offset_ref,
    d_weight_ref,
    d_bias_ref,
    d_proj_ref,
    d_table_ref,
    d_gain_ref,
    d_offset_ref,
):
    channels = weight_ref.shape[1]
    f32 = jnp.float32
    rest = channels - LANES
    mine = mine_ref[...].astype(f32)
    other = other_ref[...].astype(f32)
    here = core_ref[0] == 0
    low = jnp.where(here, mine, other)
    high = jnp.where(here, other, mine)
    both = jnp.concatenate([low, high], 0) * out_scale
    pieces = []
    for at in range(4):
        row = (4 + at // 2) * ROWS
        side = (at % 2) * SPAN
        pieces.append(
            jnp.concatenate(
                [both[at * ROWS : (at + 1) * ROWS, :], both[row : row + ROWS, side : side + rest]], 1
            )
        )
    gain = gain_ref[...]
    offset = offset_ref[...]
    ones = jnp.ones((8, channels), jnp.bfloat16)
    products = jnp.zeros((channels, channels), f32)
    d_offset = jnp.zeros((8, channels), f32)
    biases = []
    for part in range(3):
        across = slice(part * channels, (part + 1) * channels)
        unit = pieces[part][0:channels]
        bias = pieces[part][channels : channels + 1]
        weight = weight_ref[part]
        d_weight_ref[:, across] = gain * unit + offset * bias
        biases.append(bias)
        products += weight.astype(f32) * unit
        for term in split_three(bias):
            d_offset += nt(jnp.broadcast_to(term, (8, channels)), weight)
    d_bias_ref[...] = jnp.concatenate(biases, 1).reshape(d_bias_ref.shape)
    d_gain = sum(nt(ones, term) for term in split_three(products))
    d_gain_ref[...] = d_gain[0:1].reshape(channels)
    d_offset_ref[...] = d_offset[0:1].reshape(channels)
    d_proj_ref[...] = pieces[3][0:channels]
    table = jnp.concatenate([both[6 * ROWS : 6 * ROWS + 8], both[6 * ROWS + 8 :]], 1)
    d_table_ref[...] = table[0:HEADS, 0 : d_table_ref.shape[1]]


def whole(memory_space=pltpu.VMEM):
    return pl.BlockSpec(memory_space=memory_space)


def from_behind(shard, axis, by):
    count = lax.axis_size(axis)
    return lax.ppermute(shard, axis, [(i, (i + by) % count) for i in range(count)])


def diagonal(shard):
    rows, cols = lax.axis_size("row"), lax.axis_size("col")
    pairs = [
        (r * cols + c, ((r + 1) % rows) * cols + (c - 1) % cols) for r in range(rows) for c in range(cols)
    ]
    return lax.ppermute(shard, ("row", "col"), pairs)


def exchange_steps():
    rows, cols = lax.axis_size("row"), lax.axis_size("col")
    steps = [1 << bit for bit in range((rows - 1).bit_length())]
    for at in range(len(steps)):
        yield [
            (r * cols + c, (r ^ steps[(at - 1 - c) % len(steps)]) * cols + c) for r in range(rows) for c in range(cols)
        ]


def add(left, right):
    return (left.astype(jnp.float32) + right.astype(jnp.float32)).astype(jnp.bfloat16)


def on_device(
    tokens, grad_out, regions, ln_gain, ln_offset, qkv_weight, qkv_bias, proj_weight, bias_table
):
    rows, cols, channels = tokens.shape
    f32, bf16 = jnp.float32, jnp.bfloat16
    count = rows * cols
    params = pltpu.CompilerParams(vmem_limit_bytes=VMEM_LIMIT)

    x_turned = tokens.transpose(2, 0, 1)
    g_turned = grad_out.transpose(2, 0, 1)
    core = lax.axis_index("col").astype(jnp.int32).reshape(1)

    x_above = from_behind(x_turned[:, rows - SHIFT :], "row", 1)
    g_rows, near_tokens, near_grad, near_ids = lax.optimization_barrier(
        (g_turned[:, rows - SHIFT :], tokens, grad_out, regions)
    )
    g_above = from_behind(g_rows, "row", 1)

    def border(row_slice):
        return jnp.concatenate(
            [
                near_tokens[row_slice, :SHIFT],
                near_grad[row_slice, :SHIFT],
                near_ids[row_slice, :SHIFT, None].astype(bf16),
            ],
            -1,
        )

    right = from_behind(border(slice(0, rows - SHIFT)), "col", -1)
    corner = diagonal(border(slice(rows - SHIFT, None)))

    table = jnp.pad(bias_table.T, ((0, 8 - HEADS), (0, 2 * LANES - bias_table.shape[0])))
    wide = HEADS * SLOT
    bias, tok, chan, proj_slots, parts = pl.pallas_call(
        prepare_kernel,
        name="prepare",
        out_shape=(
            jax.ShapeDtypeStruct((HEADS, SPAN, LANES), f32),
            jax.ShapeDtypeStruct((3, 2 * LANES, wide), bf16),
            jax.ShapeDtypeStruct((3, wide, 2 * LANES), bf16),
            jax.ShapeDtypeStruct((wide, channels), bf16),
            jax.ShapeDtypeStruct((3, channels, channels), bf16),
        ),
        in_specs=[whole()] * 4,
        out_specs=(whole(),) * 5,
        compiler_params=params,
        cost_estimate=pl.CostEstimate(flops=1000, bytes_accessed=1000, transcendentals=0),
    )(qkv_weight, qkv_bias[None], proj_weight, table)

    gain = jnp.pad(ln_gain, (0, 2 * LANES - channels))[None]
    offset = jnp.pad(ln_offset, (0, 2 * LANES - channels))[None]
    wins = cols // WIN
    unit, inv, *projected = pl.pallas_call(
        project_kernel,
        name="project",
        out_shape=(
            jax.ShapeDtypeStruct((count, 2 * LANES), f32),
            jax.ShapeDtypeStruct((count, 1), f32),
            jax.ShapeDtypeStruct((wide, count), bf16),
            jax.ShapeDtypeStruct((count, channels), bf16),
            jax.ShapeDtypeStruct((count, wide), bf16),
            jax.ShapeDtypeStruct((count, wide), bf16),
            jax.ShapeDtypeStruct((wide, count), bf16),
            jax.ShapeDtypeStruct((wide, count), bf16),
            jax.ShapeDtypeStruct((wide, count), bf16),
            jax.ShapeDtypeStruct((2, rows, WIN, 2 * LANES), f32),
        ),
        in_specs=[whole()] * 7,
        out_specs=(whole(),) * 10,
        scratch_shapes=[
            pltpu.VMEM((channels, SHIFT, cols), f32),
            pltpu.VMEM((wins, rows, WIN, 2 * LANES), f32),
        ],
        compiler_params=params,
        cost_estimate=pl.CostEstimate(flops=1000, bytes_accessed=1000, transcendentals=0),
    )(near_tokens, x_above, right, gain, offset, tok, chan)
    keep, send, *saved = pl.pallas_call(
        main_kernel,
        name="window_attention_backward",
        out_shape=(
            jax.ShapeDtypeStruct((BUFFER_ROWS // 2, LANES), bf16),
            jax.ShapeDtypeStruct((BUFFER_ROWS // 2, LANES), bf16),
            jax.ShapeDtypeStruct((3, count, channels), bf16),
            jax.ShapeDtypeStruct((wins, rows, WIN, channels), f32),
            jax.ShapeDtypeStruct((LANES, 2 * LANES), f32),
            jax.ShapeDtypeStruct((LANES, 1), f32),
        ),
        in_specs=[whole()] * 20 + [whole(pltpu.SMEM)],
        out_specs=(whole(),) * 6,
        scratch_shapes=[
            pltpu.VMEM((channels, SHIFT, cols), f32),
            pltpu.VMEM((2, rows, WIN, 2 * LANES), f32),
            pltpu.VMEM((wins, rows, WIN, 1), f32),
            pltpu.VMEM((count, channels), bf16),
            pltpu.VMEM((count, channels), bf16),
            pltpu.VMEM((wide, count), bf16),
            pltpu.VMEM((wide, count), bf16),
            pltpu.VMEM((HEADS, SPAN, LANES), f32),
            pltpu.VMEM((BUFFER_ROWS, LANES), f32),
        ],
        compiler_params=params,
    )(
        near_grad, near_ids, g_above, right, corner, gain, offset, bias, tok, chan, proj_weight, proj_slots,
        *projected, core,
    )
    saved = [*saved, unit, inv]

    mine = add(keep, from_behind(send, "col", 1))
    mine, *saved = lax.optimization_barrier((mine, *saved))
    (framed,) = pl.pallas_call(
        input_kernel,
        name="input_backward",
        out_shape=(jax.ShapeDtypeStruct((channels, rows, cols), bf16),),
        in_specs=[whole()] * 8,
        out_specs=(whole(),),
        scratch_shapes=[pltpu.VMEM((channels, rows, cols), f32)],
        compiler_params=params,
        cost_estimate=pl.CostEstimate(flops=10**9, bytes_accessed=0, transcendentals=0),
    )(*saved, gain, parts)
    below = from_behind(framed[:, :SHIFT], "row", -1)
    for pairs in exchange_steps():
        mine = add(mine, lax.ppermute(mine, ("row", "col"), pairs))
    framed = jnp.concatenate([framed[:, SHIFT:], below], 1)
    beside = from_behind(framed, "col", 1)
    d_tokens = jnp.where(jnp.arange(cols) < SHIFT, beside, framed).transpose(1, 2, 0)
    other = from_behind(mine, "col", 1)

    total_tokens = count * lax.axis_size("row") * lax.axis_size("col")
    d_weight, d_bias, d_proj, d_table, d_gain, d_offset = pl.pallas_call(
        functools.partial(finish_kernel, total_tokens ** (-0.5)),
        name="finish",
        out_shape=(
            jax.ShapeDtypeStruct(qkv_weight.shape, f32),
            jax.ShapeDtypeStruct(qkv_bias.shape, f32),
            jax.ShapeDtypeStruct(proj_weight.shape, f32),
            jax.ShapeDtypeStruct(bias_table.shape[::-1], f32),
            jax.ShapeDtypeStruct(ln_gain.shape, f32),
            jax.ShapeDtypeStruct(ln_offset.shape, f32),
        ),
        in_specs=[whole(), whole(), whole(pltpu.SMEM), whole(), whole(), whole()],
        out_specs=(whole(),) * 6,
        compiler_params=params,
    )(mine, other, core, parts, ln_gain[:, None], ln_offset[:, None])
    return (d_tokens, d_weight, d_bias, d_proj, d_table.T, d_gain, d_offset)


def solution(mesh):
    placed = (
        P(("grp", "row"), "col", None),
        P(("grp", "row"), "col", None),
        P(("grp", "row"), "col"),
        P(),
        P(),
        P(),
        P(),
        P(),
        P(),
    )
    return jax.shard_map(
        on_device,
        mesh=mesh,
        in_specs=placed,
        out_specs=(
            P(("grp", "row"), "col", None),
            P("grp", None),
            P("grp"),
            P("grp", None),
            P("grp", None),
            P("grp"),
            P("grp"),
        ),
        check_vma=False,
    )
```
